32 devices in a mesh: dp: 4 (over z), seq: 8 (over y, x, core).
Axes of the slice: x: 2, y: 2, z: 4, core: 2. Of those that a mesh axis runs over, the one named last changes fastest.
Arguments:
- token_ids: int32 [4, 2048], P('dp', 'seq'), may hold values from 0 to 31999
- response_mask: int32 [4, 2048], P('dp', 'seq'), may hold values from 0 to 1, as said below
- deal_order: int32 [8], replicated, may hold values from 0 to 7, each once
- owners: int32 [7], replicated, may hold values from 0 to 3
- embed_table: float32 [32000, 576], P('seq'), may hold values from -0.48 to 0.48
- w_query: float32 [576, 576], P('seq'), may hold values from -0.25 to 0.25
- w_kv: float32 [576, 384], P('seq'), may hold values from -0.25 to 0.25
- w_out: float32 [576, 576], P('seq'), may hold values from -1 to 1
- w_gate_up: float32 [576, 3072], P('seq'), may hold values from -0.25 to 0.25
- w_down: float32 [1536, 576], P('seq'), may hold values from -0.15625 to 0.15625
- gains: float32 [3, 576], P(None, 'seq'), may hold values from 0.5 to 1.5
- first_embed: float32 [32000, 576], P('seq'), may hold values from -1.4305115e-06 to 1.4305115e-06
- first_query: float32 [576, 576], P('seq'), may hold values from -1.4305115e-06 to 1.4305115e-06
- first_kv: float32 [576, 384], P('seq'), may hold values from -1.4305115e-06 to 1.4305115e-06
- first_out: float32 [576, 576], P('seq'), may hold values from -1.4305115e-06 to 1.4305115e-06
- first_gate_up: float32 [576, 3072], P('seq'), may hold values from -1.4305115e-06 to 1.4305115e-06
- first_down: float32 [1536, 576], P('seq'), may hold values from -1.4305115e-06 to 1.4305115e-06
- first_gains: float32 [3, 576], P(None, 'seq'), may hold values from -1.5258789e-05 to 1.5258789e-05
- second_embed: float32 [32000, 576], P('seq'), may hold values from 2.3938826e-13 to 9.557327e-13
- second_query: float32 [576, 576], P('seq'), may hold values from 2.3938826e-13 to 9.557327e-13
- second_kv: float32 [576, 384], P('seq'), may hold values from 2.3938826e-13 to 9.557327e-13
- second_out: float32 [576, 576], P('seq'), may hold values from 2.3938826e-13 to 9.557327e-13
- second_gate_up: float32 [576, 3072], P('seq'), may hold values from 2.3938826e-13 to 9.557327e-13
- second_down: float32 [1536, 576], P('seq'), may hold values from 2.3938826e-13 to 9.557327e-13
- second_gains: float32 [3, 576], P(None, 'seq'), may hold values from 2.3938827e-11 to 9.5573265e-11
Outputs:
- new_embed: float32 [32000, 576], P('seq')
- new_query: float32 [576, 576], P('seq')
- new_kv: float32 [576, 384], P('seq')
- new_out: float32 [576, 576], P('seq')
- new_gate_up: float32 [576, 3072], P('seq')
- new_down: float32 [1536, 576], P('seq')
- new_gains: float32 [3, 576], P(None, 'seq')
- next_first_embed: float32 [32000, 576], P('seq')
- next_first_query: float32 [576, 576], P('seq')
- next_first_kv: float32 [576, 384], P('seq')
- next_first_out: float32 [576, 576], P('seq')
- next_first_gate_up: float32 [576, 3072], P('seq')
- next_first_down: float32 [1536, 576], P('seq')
- next_first_gains: float32 [3, 576], P(None, 'seq')
- next_second_embed: float32 [32000, 576], P('seq')
- next_second_query: float32 [576, 576], P('seq')
- next_second_kv: float32 [576, 384], P('seq')
- next_second_out: float32 [576, 576], P('seq')
- next_second_gate_up: float32 [576, 3072], P('seq')
- next_second_down: float32 [1536, 576], P('seq')
- next_second_gains: float32 [3, 576], P(None, 'seq')
- loss: float32 [], replicated
- grad_norm: float32 [], replicated
The draws below stay inside these ranges and needn't reach their ends.
Inputs may be any that keep to these rules, and one draw needn't show every extreme that they name: `response_mask`: each sequence has zeros on its first positions (a prompt of 256 to 1535 of them) and ones after them. `deal_order`: A permutation of the indices of seq. `owners`: in the order embed_table, w_query, w_kv, w_out, w_gate_up, w_down, gains.
All inputs are finite; a program needn't handle non-finite values.
Results may differ from the reference program's by a relative error of at most 0.0034.
The reference program's roundings to bfloat16 on the way count: a program that leaves them out, or rounds other values in their place, can miss the bound.
Values may be sent and summed in bfloat16 or wider, within the bound.
No kernel may reach another device: no remote copies, remote signals or barrier semaphores. Data moves between devices by JAX's collectives and lax.ppermute only.
A program may use at most 448 MiB of HBM per device.

```python
import math
import jax
import jax.numpy as jnp
import numpy as np
from jax import lax

D = 576
H = 9
KVH = 3
HD = 64
FF = 1536
VOCAB = 32000
LEN = 2048
LAYERS = 2
STEP_NO = 10
SEQS = 4
PARAMS = 21972672
N_DP = 4
N_SEQ = 8


def draw_response_mask(key, part):
    prompt = jax.random.randint(key, (SEQS, 1), LEN // 8, 3 * LEN // 4)
    return (jnp.arange(LEN)[None, :] >= prompt).astype(jnp.int32)


def set_ends(array, stream_key, least, high):
    longest = array.shape.index(max(array.shape))
    spots = []
    for shift in (0, 1):
        where = [jax.random.randint(jax.random.fold_in(stream_key, axis), (), 0, length) for axis, length in enumerate(array.shape)]
        where[longest] = (where[longest] + shift) % array.shape[longest]
        spots.append(tuple(where))
    return array.at[spots[0]].set(least).at[spots[1]].set(high)


def steps_of(own_key, dims, split, low, high):
    gain, own = 1.0, jax.random.fold_in(own_key, 6)
    for dim, blocks in split:
        draws = jnp.exp(jax.random.uniform(jax.random.fold_in(own, dim), (blocks,), jnp.float32, low / len(split), high / len(split)))
        gain = gain * jnp.repeat(draws, dims[dim] // blocks).reshape([-1 if axis == dim else 1 for axis in range(len(dims))])
    return gain


def rank_bounds(number_of, skew):
    weights = [(1 << 20) // math.isqrt(standing ** skew) + 1 for standing in range(1, number_of + 1)]
    scale = 1 + sum(weights) // (1 << 30)
    return np.cumsum(np.array([max(1, weight // scale) for weight in weights]))


def ranked_ids(own_key, shape, number_of, slope):
    grid = rank_bounds(number_of, slope)
    lot = jax.random.randint(jax.random.fold_in(own_key, 1), shape, 0, int(grid[number_of - 1]))
    grade = jnp.searchsorted(jnp.asarray(grid, jnp.int32), lot, side="right")
    return jax.random.permutation(jax.random.fold_in(own_key, 2), number_of)[grade].astype(jnp.int32)


def noise(stream_key, extent, width, most, pieces=(), kind=jnp.bfloat16):
    result = jax.random.normal(stream_key, extent, jnp.float32) * width
    if len(pieces) > 0:
        result = steps_of(stream_key, extent, pieces, -0.22, 0.18) * result
    return jnp.clip(result, min=-most, max=most).astype(kind)


def setup_inputs(seed: int = 0) -> dict:
    keys = jax.random.split(jax.random.key(seed), 26)
    return {
        "token_ids": set_ends(ranked_ids(keys[0], (SEQS, LEN), VOCAB, 2), jax.random.fold_in(keys[0], 3), 0, VOCAB - 1).astype(jnp.int32),
        "response_mask": draw_response_mask(jax.random.fold_in(keys[25], 71), 0),
        "deal_order": jax.random.permutation(keys[2], N_SEQ).astype(jnp.int32),
        "owners": set_ends(jax.random.randint(keys[3], (7,), 0, N_DP), jax.random.fold_in(keys[3], 1), 0, N_DP - 1).astype(jnp.int32),
        "embed_table": noise(keys[4], (VOCAB, D), 0.08, 0.48, ((0, 8),), jnp.float32),
        "w_query": noise(keys[5], (D, H * HD), D ** -0.5, 0.25, ((0, 8),), jnp.float32),
        "w_kv": noise(keys[6], (D, 2 * KVH * HD), D ** -0.5, 0.25, ((0, 8),), jnp.float32),
        "w_out": noise(keys[7], (H * HD, D), (max(H * HD // 16, 1)) ** -0.5, 1.0, ((0, 8),), jnp.float32),
        "w_gate_up": noise(keys[8], (D, 2 * FF), D ** -0.5, 0.25, ((0, 8),), jnp.float32),
        "w_down": noise(keys[9], (FF, D), FF ** -0.5, 0.15625, ((0, 8),), jnp.float32),
        "gains": jnp.clip(1.0 + 0.1 * jax.random.normal(keys[10], (3, D), jnp.float32), 0.5, 1.5),
        "first_embed": noise(keys[11], (VOCAB, D), (0.00111 / PARAMS ** 0.5), 1.430511474609375e-06, ((0, 8),), jnp.float32),
        "first_query": noise(keys[12], (D, H * HD), (0.00111 / PARAMS ** 0.5), 1.430511474609375e-06, ((0, 8),), jnp.float32),
        "first_kv": noise(keys[13], (D, 2 * KVH * HD), (0.00111 / PARAMS ** 0.5), 1.430511474609375e-06, ((0, 8),), jnp.float32),
        "first_out": noise(keys[14], (H * HD, D), (0.00111 / PARAMS ** 0.5), 1.430511474609375e-06, ((0, 8),), jnp.float32),
        "first_gate_up": noise(keys[15], (D, 2 * FF), (0.00111 / PARAMS ** 0.5), 1.430511474609375e-06, ((0, 8),), jnp.float32),
        "first_down": noise(keys[16], (FF, D), (0.00111 / PARAMS ** 0.5), 1.430511474609375e-06, ((0, 8),), jnp.float32),
        "first_gains": noise(keys[17], (3, D), (0.0111 / PARAMS ** 0.5), 1.52587890625e-05, ((1, 8),), jnp.float32),
        "second_embed": jnp.clip(jnp.exp(math.log(9.557326718229175e-13) - 1.38439148 * jax.random.uniform(keys[18], (VOCAB, D), jnp.float32) ** steps_of(keys[18], (VOCAB, D), ((0, 8),), -0.2, 0.2)), 2.393882618176302e-13, 9.557326718229175e-13),
        "second_query": jnp.clip(jnp.exp(math.log(9.557326718229175e-13) - 1.38439148 * jax.random.uniform(keys[19], (D, H * HD), jnp.float32) ** steps_of(keys[19], (D, H * HD), ((0, 8),), -0.2, 0.2)), 2.393882618176302e-13, 9.557326718229175e-13),
        "second_kv": jnp.clip(jnp.exp(math.log(9.557326718229175e-13) - 1.38439148 * jax.random.uniform(keys[20], (D, 2 * KVH * HD), jnp.float32) ** steps_of(keys[20], (D, 2 * KVH * HD), ((0, 8),), -0.2, 0.2)), 2.393882618176302e-13, 9.557326718229175e-13),
        "second_out": jnp.clip(jnp.exp(math.log(9.557326718229175e-13) - 1.38439148 * jax.random.uniform(keys[21], (H * HD, D), jnp.float32) ** steps_of(keys[21], (H * HD, D), ((0, 8),), -0.2, 0.2)), 2.393882618176302e-13, 9.557326718229175e-13),
        "second_gate_up": jnp.clip(jnp.exp(math.log(9.557326718229175e-13) - 1.38439148 * jax.random.uniform(keys[22], (D, 2 * FF), jnp.float32) ** steps_of(keys[22], (D, 2 * FF), ((0, 8),), -0.2, 0.2)), 2.393882618176302e-13, 9.557326718229175e-13),
        "second_down": jnp.clip(jnp.exp(math.log(9.557326718229175e-13) - 1.38439148 * jax.random.uniform(keys[23], (FF, D), jnp.float32) ** steps_of(keys[23], (FF, D), ((0, 8),), -0.2, 0.2)), 2.393882618176302e-13, 9.557326718229175e-13),
        "second_gains": jnp.clip(jnp.exp(math.log(9.557326458020654e-11) - 1.3843914 * jax.random.uniform(keys[24], (3, D), jnp.float32) ** steps_of(keys[24], (3, D), ((1, 8),), -0.2, 0.2)), 2.3938826615443887e-11, 9.557326458020654e-11),
    }


EPSILON = 1e-05
CLIP = 0.01
RATE = 0.1
BETA_ONE = 0.9
BETA_TWO = 0.95
ADAM_EPSILON = 1e-08
DECAY = 0.1
MASKED = -1000000000.0

@jax.custom_vjp
def low(v):
    return lax.optimization_barrier(v.astype(jnp.bfloat16)).astype(jnp.float32)

@jax.custom_vjp
def low_back(v):
    return v

def low_keep(v):
    return (low(v), None)

def low_pass(kept, grad):
    return (grad,)

def back_keep(v):
    return (v, None)

def back_low(kept, grad):
    return (low(grad),)
low.defvjp(low_keep, low_pass)
low_back.defvjp(back_keep, back_low)

def product(left, right):
    return jnp.dot(left, right, precision=lax.Precision.HIGHEST, preferred_element_type=jnp.float32)

def rms_norm(values, gain_row):
    return values * lax.rsqrt(lax.optimization_barrier(jnp.mean(values * values, -1, keepdims=True)) + EPSILON) * gain_row

def rotate(values, cosine, sine_wave):
    half_size = values.shape[-1] // 2
    cos_full = cosine[:, None, :]
    sin_full = sine_wave[:, None, :]
    first_half = values[..., :half_size]
    second_half = values[..., half_size:]
    return jnp.concatenate([first_half * cos_full - second_half * sin_full, first_half * sin_full + second_half * cos_full], -1)

def block_forward(x_in, block, cosine, sine_wave):
    query_weight, kv_weight, out_weight, gate_weight, down_weight, gain_rows = block
    row_count = x_in.shape[0]
    normed = low(rms_norm(x_in, gain_rows[0]))
    q_raw = low_back(product(normed, query_weight))
    kv_raw = low_back(product(normed, kv_weight))
    queries = rotate(q_raw.reshape(row_count, H, HD), cosine, sine_wave)
    key_rot = rotate(kv_raw[:, :KVH * HD].reshape(row_count, KVH, HD), cosine, sine_wave)
    value_rows = kv_raw[:, KVH * HD:].reshape(row_count, KVH, HD)
    queries = low(low_back(queries))
    key_rot = low(low_back(key_rot))
    value_rows = low(low_back(value_rows))
    grouped = queries.reshape(row_count, KVH, H // KVH, HD)
    scores = jnp.einsum('ckgd,lkd->kgcl', grouped, key_rot, precision=lax.Precision.HIGHEST) * HD ** (-0.5)
    positions = jnp.arange(row_count)
    scores = jnp.where(positions[:, None] >= positions[None, :], scores, MASKED)
    scores = low_back(scores)
    highest = lax.optimization_barrier(jnp.max(scores, -1, keepdims=True))
    exponent = jnp.exp(scores - highest)
    weights = low(exponent / lax.optimization_barrier(jnp.sum(exponent, -1, keepdims=True)))
    outputs = jnp.einsum('kgcl,lkd->ckgd', weights, value_rows, precision=lax.Precision.HIGHEST).reshape(row_count, H * HD)
    outputs = low(low_back(outputs))
    x_mid = x_in + low_back(product(outputs, out_weight))
    normed_ffn = low(rms_norm(x_mid, gain_rows[1]))
    gate_up = low_back(product(normed_ffn, gate_weight))
    activated = low(jax.nn.silu(gate_up[:, :FF]) * gate_up[:, FF:])
    return x_mid + low_back(product(activated, down_weight))

def adam_update(weight, first, second, grad, decay):
    next_first = BETA_ONE * first + (1.0 - BETA_ONE) * grad
    next_second = BETA_TWO * second + (1.0 - BETA_TWO) * grad * grad
    corrected = next_first / (1.0 - BETA_ONE ** STEP_NO)
    scaled = jnp.sqrt(next_second / (1.0 - BETA_TWO ** STEP_NO)) + ADAM_EPSILON
    return (weight - RATE * (corrected / scaled + decay * weight), next_first, next_second)

def reference(token_ids, response_mask, deal_order, owners, embed_table, w_query, w_kv, w_out, w_gate_up, w_down, gains, first_embed, first_query, first_kv, first_out, first_gate_up, first_down, first_gains, second_embed, second_query, second_kv, second_out, second_gate_up, second_down, second_gains):
    masters = (embed_table, w_query, w_kv, w_out, w_gate_up, w_down, gains)
    firsts = (first_embed, first_query, first_kv, first_out, first_gate_up, first_down, first_gains)
    seconds = (second_embed, second_query, second_kv, second_out, second_gate_up, second_down, second_gains)
    positions = jnp.arange(LEN)
    valid = response_mask.astype(jnp.float32) * (positions < LEN - 1).astype(jnp.float32)[None, :]
    counted = jnp.sum(valid)
    targets = jnp.concatenate([token_ids[:, 1:], jnp.zeros((token_ids.shape[0], 1), jnp.int32)], 1)
    inverse = 10000.0 ** (-jnp.arange(HD // 2).astype(jnp.float32) * 2.0 / HD)
    phases = positions.astype(jnp.float32)[:, None] * inverse[None, :]
    cosine = jnp.cos(phases)
    sine_wave = jnp.sin(phases)

    def one_sequence(lowered, seq_items):
        ids_row, target_row, valid_row = seq_items
        table_low = lowered[0]
        block = lowered[1:]
        hidden = low_back(table_low[ids_row])
        for layer in range(LAYERS):
            hidden = block_forward(hidden, block, cosine, sine_wave)
        final = low(rms_norm(hidden, block[5][2]))
        logits = low_back(product(final, table_low.T))
        highest = lax.optimization_barrier(jnp.max(logits, -1, keepdims=True))
        log_norm = highest[:, 0] + jnp.log(lax.optimization_barrier(jnp.sum(jnp.exp(logits - highest), -1)))
        picked = jnp.take_along_axis(logits, target_row[:, None], 1)[:, 0]
        return jnp.sum((log_norm - picked) * valid_row)
    checked = jax.checkpoint(one_sequence)

    def total_loss(params):
        lowered = tuple((low(weight) for weight in params))

        def scan_step(carry, seq_items):
            return (carry + checked(lowered, seq_items), None)
        total, _ = lax.scan(scan_step, jnp.zeros((), jnp.float32), (token_ids, targets, valid))
        return total / counted
    loss, pull = jax.vjp(total_loss, masters)
    grads, = pull(jnp.ones((), jnp.float32))
    squares = jnp.zeros((), jnp.float32)
    for grad in grads:
        squares = squares + jnp.sum(grad * grad)
    grad_norm = jnp.sqrt(squares)
    factor = CLIP / jnp.maximum(grad_norm, CLIP)
    new_weights = []
    new_firsts = []
    new_seconds = []
    for item in range(7):
        decay = DECAY if item < 6 else 0.0
        weight, first, second = adam_update(masters[item], firsts[item], seconds[item], grads[item] * factor, decay)
        new_weights.append(weight)
        new_firsts.append(first)
        new_seconds.append(second)
    return (new_weights[0], new_weights[1], new_weights[2], new_weights[3], new_weights[4], new_weights[5], new_weights[6], new_firsts[0], new_firsts[1], new_firsts[2], new_firsts[3], new_firsts[4], new_firsts[5], new_firsts[6], new_seconds[0], new_seconds[1], new_seconds[2], new_seconds[3], new_seconds[4], new_seconds[5], new_seconds[6], loss, grad_norm)
```

```python
import functools

import jax
import jax.numpy as jnp
from jax import lax
from jax.experimental import pallas as pl
from jax.experimental.pallas import tpu as pltpu
from jax.sharding import PartitionSpec as P

H = 9
KVH = 3
GROUP = H // KVH
HD = 64
HALF = HD // 2
FF = 1536
LAYERS = 2
STEP_NO = 10
EPSILON = 1e-05
CLIP = 0.01
RATE = 0.1
BETA_ONE = 0.9
BETA_TWO = 0.95
ADAM_EPSILON = 1e-08
DECAY = 0.1
MASKED = -1000000000.0
BF = jnp.bfloat16
F32 = jnp.float32
MIB = 1024 * 1024

KV_AT, GU_AT, Q_AT, OUT_AT, GAIN_AT, PACKED = 0, 384, 3456, 4096, 4672, 4736
CHUNK = 512
VTILE = 1024


def bit_orders(n):
    bits = [1 << k for k in range(n.bit_length() - 1)]
    rest = bits[1:]
    return (rest + bits[:1], rest[::-1] + bits[:1])


def stack_order(order):
    listed = [0]
    for bit in order:
        listed = listed + [r | bit for r in listed]
    return listed


def swap(x, axis, bit):
    n = lax.axis_size(axis)
    return lax.ppermute(x, axis, [(i, i ^ bit) for i in range(n)])


def gather_half(x, axis, order):
    held = {0: x}
    for bit in order:
        held.update({r ^ bit: swap(v, axis, bit) for r, v in list(held.items())})
    return [held[r] for r in range(len(held))]


def gather_pair(a, b, axis):
    first, second = bit_orders(lax.axis_size(axis))
    return gather_half(a, axis, first), gather_half(b, axis, second)


def scatter_stack(keep, send, axis, order, exact=False):
    bits = order[::-1]
    for k, bit in enumerate(bits):
        got = swap(send, axis, bit)
        if k == len(bits) - 1:
            return keep[0], got[0]
        half = keep.shape[0] // 2
        if exact:
            keep, send = keep[:half] + got[:half], keep[half:] + got[half:]
        else:
            low = keep[:half].astype(F32) + got[:half].astype(F32)
            high = keep[half:].astype(F32) + got[half:].astype(F32)
            keep, send = low, high.astype(BF)


def ring(x, axis):
    n = lax.axis_size(axis)
    slots = [x]
    for _ in range(n - 1):
        slots.append(lax.ppermute(slots[-1], axis, [(i, (i + 1) % n) for i in range(n)]))
    return slots


def total_over(x, axis):
    bit = 1
    while bit < lax.axis_size(axis):
        x = x + swap(x, axis, bit)
        bit *= 2
    return x


def after(x, *needs):
    return lax.optimization_barrier((x,) + needs)[0]


def dot(a, b):
    return jnp.dot(a, b, preferred_element_type=F32)


def dot_t(a, b):
    return lax.dot_general(a, b, (((1,), (1,)), ((), ())), preferred_element_type=F32)


def dot_w(a, b):
    return lax.dot_general(a, b, (((0,), (0,)), ((), ())), preferred_element_type=F32)


def inverse_rms(values):
    return lax.rsqrt(jnp.mean(values * values, -1, keepdims=True) + EPSILON)


def rms_back(values, gain_row, d_out):
    r = inverse_rms(values)
    scaled = gain_row * d_out
    d_values = r * scaled - values * (r * r * r * jnp.mean(values * scaled, -1, keepdims=True))
    return d_values, jnp.sum(d_out * values * r, 0, keepdims=True)


def column(row):
    return jnp.transpose(jnp.broadcast_to(row, (8, row.shape[1])))[:, 0:1]


def call(kernel, name, inputs, outputs, scratch=(), scalars=0, limit=40, flops=0, aliases=None):
    vmem = pl.BlockSpec(memory_space=pltpu.VMEM)
    smem = pl.BlockSpec(memory_space=pltpu.SMEM)
    moved = sum(v.size * v.dtype.itemsize for v in inputs) + sum(
        o.size * o.dtype.itemsize for o in outputs
    )
    return pl.pallas_call(
        kernel,
        in_specs=[smem] * scalars + [vmem] * (len(inputs) - scalars),
        out_specs=[vmem] * len(outputs),
        out_shape=list(outputs),
        scratch_shapes=list(scratch),
        compiler_params=pltpu.CompilerParams(vmem_limit_bytes=limit * MIB),
        cost_estimate=pl.CostEstimate(flops=flops, bytes_accessed=moved, transcendentals=0),
        input_output_aliases=aliases or {},
        name=name,
    )(*inputs)


def shape(dims, dtype):
    return jax.ShapeDtypeStruct(tuple(dims), dtype)


def table_kernel(vocab, wide_ref, out_ref):
    tile = out_ref.shape[0]
    at = pl.program_id(0) * tile
    x = wide_ref[...]
    cols = lax.broadcasted_iota(jnp.int32, x.shape, 1) + at
    out_ref[...] = jnp.transpose(jnp.where(cols < vocab, x, 0.0)).astype(BF)


def low_table(embed_table, padded):
    vocab, width = embed_table.shape
    tile = 512
    return pl.pallas_call(
        functools.partial(table_kernel, vocab),
        grid=(padded // tile,),
        in_specs=[pl.BlockSpec((width, tile), lambda i: (0, i))],
        out_specs=pl.BlockSpec((tile, width), lambda i: (i, 0)),
        out_shape=shape((padded, width), BF),
        compiler_params=pltpu.CompilerParams(vmem_limit_bytes=24 * MIB),
        cost_estimate=pl.CostEstimate(flops=0, bytes_accessed=6 * padded * width, transcendentals=0),
        name="low_table",
    )(embed_table.T)


def lookup_kernel(ids_ref, table_ref, out_ref):
    rows = out_ref.shape[0]
    total = jnp.zeros(out_ref.shape, F32)
    for at in range(0, table_ref.shape[0], VTILE):
        cols = lax.broadcasted_iota(jnp.int32, (rows, VTILE), 1) + at
        hot = jnp.where(cols == ids_ref[...], 1.0, 0.0).astype(BF)
        total += dot(hot, table_ref[at : at + VTILE, :])
    out_ref[...] = total.astype(BF)


def lookup(ids, table, block):
    count = ids.shape[0]
    width = table.shape[1]
    return pl.pallas_call(
        lookup_kernel,
        grid=(count // block,),
        in_specs=[
            pl.BlockSpec((block, 1), lambda i: (i, 0)),
            pl.BlockSpec(table.shape, lambda i: (0, 0)),
        ],
        out_specs=pl.BlockSpec((block, width), lambda i: (i, 0)),
        out_shape=shape((count, width), BF),
        compiler_params=pltpu.CompilerParams(vmem_limit_bytes=40 * MIB),
        cost_estimate=pl.CostEstimate(
            flops=2 * count * table.size, bytes_accessed=2 * table.size, transcendentals=0
        ),
        name="lookup",
    )(ids.reshape(count, 1), table)


def project(x, gain, packed_ref, c, s, normed_ref, q_ref, kv_a_ref, kv_b_ref):
    piece = x.shape[0] // 2
    normed = (x * inverse_rms(x) * gain).astype(BF)
    normed_ref[...] = normed
    q = dot(normed, packed_ref[:, Q_AT : Q_AT + H * HD])
    kv = dot(normed, packed_ref[:, KV_AT : KV_AT + 2 * KVH * HD])
    nothing = jnp.zeros((x.shape[0], HD), F32)
    for h in range(H):
        g, j = divmod(h, GROUP)
        a = q[:, h * HD : h * HD + HALF]
        b = q[:, h * HD + HALF : (h + 1) * HD]
        turned = jnp.concatenate([(a * c - b * s) * 0.125, (a * s + b * c) * 0.125, nothing], 1).astype(BF)
        for p in range(2):
            q_ref[g, p, j * piece : (j + 1) * piece, :] = turned[p * piece : (p + 1) * piece]
    for g in range(KVH):
        a = kv[:, g * HD : g * HD + HALF]
        b = kv[:, g * HD + HALF : (g + 1) * HD]
        v = kv[:, (KVH + g) * HD : (KVH + g + 1) * HD]
        turned = jnp.concatenate([a * c - b * s, a * s + b * c, v], 1).astype(BF)
        kv_a_ref[g] = turned[:piece]
        kv_b_ref[g] = turned[piece:]


def feed(x, o_ref, gain, packed_ref, down_ref, mid_ref, nf_ref, gu_ref, act_ref):
    x_mid = x + dot(o_ref[...], packed_ref[:, OUT_AT : OUT_AT + x.shape[1]])
    mid_ref[...] = x_mid
    nf = (x_mid * inverse_rms(x_mid) * gain).astype(BF)
    nf_ref[...] = nf
    total = x_mid
    for at in range(0, FF, CHUNK):
        gate = dot(nf, packed_ref[:, GU_AT + at : GU_AT + at + CHUNK])
        up = dot(nf, packed_ref[:, GU_AT + FF + at : GU_AT + FF + at + CHUNK])
        gu_ref[:, at : at + CHUNK] = gate
        gu_ref[:, FF + at : FF + at + CHUNK] = up
        act = (gate * lax.logistic(gate) * up).astype(BF)
        act_ref[:, at : at + CHUNK] = act
        total = total + dot(act, down_ref[at : at + CHUNK, :])
    return total


def pre_kernel(x_ref, gain_ref, packed_ref, c_ref, s_ref, normed_ref, q_ref, kv_a_ref, kv_b_ref):
    project(x_ref[...], gain_ref[0:1, :], packed_ref, c_ref[...], s_ref[...], normed_ref, q_ref, kv_a_ref, kv_b_ref)


def mid_kernel(
    x_ref, o_ref, gain_ref, packed_ref, down_ref, c_ref, s_ref,
    mid_ref, nf_ref, gu_ref, act_ref, next_ref, normed_ref, q_ref, kv_a_ref, kv_b_ref,
):
    x = feed(x_ref[...], o_ref, gain_ref[1:2, :], packed_ref, down_ref, mid_ref, nf_ref, gu_ref, act_ref)
    next_ref[...] = x
    project(x, gain_ref[0:1, :], packed_ref, c_ref[...], s_ref[...], normed_ref, q_ref, kv_a_ref, kv_b_ref)


def post_kernel(
    x_ref, o_ref, gain_ref, packed_ref, down_ref,
    mid_ref, nf_ref, gu_ref, act_ref, next_ref, final_a_ref, final_b_ref,
):
    x = feed(x_ref[...], o_ref, gain_ref[1:2, :], packed_ref, down_ref, mid_ref, nf_ref, gu_ref, act_ref)
    next_ref[...] = x
    final = (x * inverse_rms(x) * gain_ref[2:3, :]).astype(BF)
    piece = x.shape[0] // 2
    final_a_ref[...] = final[:piece]
    final_b_ref[...] = final[piece:]


def projected_shapes(rows, width):
    piece = rows // 2
    return [
        shape((rows, width), BF),
        shape((KVH, 2, GROUP * piece, 2 * HD), BF),
        shape((KVH, piece, 2 * HD), BF),
        shape((KVH, piece, 2 * HD), BF),
    ]


def fed_shapes(rows, width):
    return [
        shape((rows, width), F32),
        shape((rows, width), BF),
        shape((rows, 2 * FF), F32),
        shape((rows, FF), BF),
        shape((rows, width), F32),
    ]


def causal(scores, piece):
    row = lax.broadcasted_iota(jnp.int32, scores.shape, 0) & (piece - 1)
    col = lax.broadcasted_iota(jnp.int32, scores.shape, 1)
    return jnp.where(row >= col, scores, MASKED)


def attend_kernel(n, me_ref, q_ref, *refs):
    kvs, (o_ref, lse_ref), (all_ref,) = refs[: 2 * n], refs[2 * n : 2 * n + 2], refs[2 * n + 2 :]
    me = me_ref[0]
    piece = kvs[0].shape[1]
    lows = [None] + [(me ^ r) < me for r in range(1, n)]
    for g in range(KVH):
        for r in range(n):
            all_ref[r * piece : (r + 1) * piece, :] = kvs[r][g]
        q_a = q_ref[g, 0]
        q_b = q_ref[g, 1]
        wide = dot_t(q_b, all_ref[...])
        own_a = causal(dot_t(q_a, kvs[0][g]), piece)
        own_b = causal(dot_t(q_b, kvs[n][g]), piece)
        m_a = jnp.max(own_a, -1, keepdims=True)
        m_b = jnp.maximum(jnp.max(own_b, -1, keepdims=True), jnp.max(wide, -1, keepdims=True))
        tiles = [None]
        for r in range(1, n):
            low = lows[r]
            tile = dot_t(jnp.where(low, q_a, q_b), jnp.where(low, kvs[r][g], kvs[n + r][g]))
            top = jnp.max(tile, -1, keepdims=True)
            m_a = jnp.maximum(m_a, top + jnp.where(low, 0.0, -jnp.inf))
            m_b = jnp.maximum(m_b, top + jnp.where(low, -jnp.inf, 0.0))
            tiles.append(tile)
        e = jnp.exp(wide - m_b)
        l_b = jnp.sum(e, -1, keepdims=True)
        o_b = dot(e.astype(BF), all_ref[...])
        e = jnp.exp(own_b - m_b)
        l_b += jnp.sum(e, -1, keepdims=True)
        o_b += dot(e.astype(BF), kvs[n][g])
        e = jnp.exp(own_a - m_a)
        l_a = jnp.sum(e, -1, keepdims=True)
        o_a = dot(e.astype(BF), kvs[0][g])
        for r in range(1, n):
            low = lows[r]
            in_a = jnp.where(low, 1.0, 0.0)
            in_b = 1.0 - in_a
            e = jnp.exp(tiles[r] - (m_a * in_a + m_b * in_b))
            total = jnp.sum(e, -1, keepdims=True)
            o = dot(e.astype(BF), jnp.where(low, kvs[r][g], kvs[n + r][g]))
            l_a += total * in_a
            l_b += total * in_b
            o_a += o * in_a
            o_b += o * in_b
        lse_ref[g, 0] = m_a + jnp.log(l_a)
        lse_ref[g, 1] = m_b + jnp.log(l_b)
        out = [(o_a / l_a).astype(BF), (o_b / l_b).astype(BF)]
        for p in range(2):
            for j in range(GROUP):
                h = g * GROUP + j
                o_ref[p * piece : (p + 1) * piece, h * HD : (h + 1) * HD] = out[p][
                    j * piece : (j + 1) * piece, HD:
                ]


def attend(me, queries, kv_a, kv_b):
    n = len(kv_a)
    piece = kv_a[0].shape[1]
    stacked = GROUP * piece
    return call(
        functools.partial(attend_kernel, n),
        "attend",
        [me, queries] + kv_a + kv_b,
        [shape((2 * piece, H * HD), BF), shape((KVH, 2, stacked, 1), F32)],
        [pltpu.VMEM((n * piece, 2 * HD), BF)],
        scalars=1,
        flops=2 * 2 * H * HD * piece * piece * (2 * n + 1) * 2,
    )


def attend_back_kernel(n, orders, me_ref, q_ref, do_ref, lse_ref, *refs):
    kvs, outs, (all_ref, sum_ref) = refs[: 2 * n], refs[2 * n : 2 * n + 5], refs[2 * n + 5 :]
    dq_ref, halves = outs[0], (outs[1:3], outs[3:5])
    me = me_ref[0]
    piece = kvs[0].shape[1]
    lows = [None] + [(me ^ r) < me for r in range(1, n)]
    for g in range(KVH):
        for r in range(n):
            all_ref[r * piece : (r + 1) * piece, :] = kvs[r][g]
        q_a, q_b = q_ref[g, 0], q_ref[g, 1]
        do_a, do_b = do_ref[g, 0], do_ref[g, 1]
        lse_a, lse_b = lse_ref[g, 0], lse_ref[g, 1]
        p_wide = jnp.exp(dot_t(q_b, all_ref[...]) - lse_b)
        w_wide = dot_t(do_b, all_ref[...])
        d_b = jnp.sum(p_wide * w_wide, -1, keepdims=True)
        p_own_a = jnp.exp(causal(dot_t(q_a, kvs[0][g]), piece) - lse_a)
        w_own_a = dot_t(do_a, kvs[0][g])
        d_a = jnp.sum(p_own_a * w_own_a, -1, keepdims=True)
        p_own_b = jnp.exp(causal(dot_t(q_b, kvs[n][g]), piece) - lse_b)
        w_own_b = dot_t(do_b, kvs[n][g])
        d_b += jnp.sum(p_own_b * w_own_b, -1, keepdims=True)
        tiles = [None]
        for r in range(1, n):
            low = lows[r]
            in_a = jnp.where(low, 1.0, 0.0)
            in_b = 1.0 - in_a
            k = jnp.where(low, kvs[r][g], kvs[n + r][g])
            p = jnp.exp(dot_t(jnp.where(low, q_a, q_b), k) - (lse_a * in_a + lse_b * in_b))
            w = dot_t(jnp.where(low, do_a, do_b), k)
            total = jnp.sum(p * w, -1, keepdims=True)
            d_a += total * in_a
            d_b += total * in_b
            tiles.append((p, w))

        def both(p, w, inner, q, do, k):
            ds = (p * (w - inner)).astype(BF)
            dq = dot(ds, k)
            dkv = dot_w(ds, q) + dot_w(p.astype(BF), do)
            return dq, dkv

        dq_b, dkv = both(p_wide, w_wide, d_b, q_b, do_b, all_ref[...])
        sum_ref[...] = dkv
        dq, dkv_b0 = both(p_own_b, w_own_b, d_b, q_b, do_b, kvs[n][g])
        dq_b += dq
        dq_a, dkv_a0 = both(p_own_a, w_own_a, d_a, q_a, do_a, kvs[0][g])
        sum_ref[0:piece, :] += dkv_a0
        spots = [{r: (k // (n // 2), k % (n // 2)) for k, r in enumerate(o)} for o in orders]

        def put(half, r, value):
            side, at = spots[half][r]
            ref = halves[half][side]
            ref[at, g] = value.astype(ref.dtype)

        put(1, 0, dkv_b0)
        for r in range(1, n):
            low = lows[r]
            in_a = jnp.where(low, 1.0, 0.0)
            in_b = 1.0 - in_a
            p, w = tiles[r]
            k = jnp.where(low, kvs[r][g], kvs[n + r][g])
            dq, dkv = both(p, w, d_a * in_a + d_b * in_b, jnp.where(low, q_a, q_b), jnp.where(low, do_a, do_b), k)
            dq_a += dq * in_a
            dq_b += dq * in_b
            sum_ref[r * piece : (r + 1) * piece, :] += dkv * in_a
            put(1, r, dkv * in_b)
        for r in range(n):
            put(0, r, sum_ref[r * piece : (r + 1) * piece, :])
        out = [(dq_a * 0.125).astype(BF), (dq_b * 0.125).astype(BF)]
        for p in range(2):
            for j in range(GROUP):
                h = g * GROUP + j
                dq_ref[p * piece : (p + 1) * piece, h * HD : (h + 1) * HD] = out[p][
                    j * piece : (j + 1) * piece, :HD
                ]


def attend_back(me, queries, d_out, lse, kv_a, kv_b, orders):
    n = len(kv_a)
    piece = kv_a[0].shape[1]
    block = (n // 2, KVH, piece, 2 * HD)
    return call(
        functools.partial(attend_back_kernel, n, orders),
        "attend_back",
        [me, queries, d_out, lse] + kv_a + kv_b,
        [shape((2 * piece, H * HD), BF)] + [shape(block, F32), shape(block, BF)] * 2,
        [pltpu.VMEM((n * piece, 2 * HD), BF), pltpu.VMEM((n * piece, 2 * HD), F32)],
        scalars=1,
        flops=5 * 2 * H * HD * piece * piece * (2 * n + 1) * 2,
    )


def feed_back(d_x, gain, packed_ref, down_ref, mid_ref, gu_ref, outs):
    db_ref, dgu_ref, dmid_ref, da_ref, do_ref, gain_ref = outs
    rows, width = d_x.shape
    piece = rows // 2
    d_branch = d_x.astype(BF)
    db_ref[...] = d_branch
    d_nf = jnp.zeros(d_x.shape, F32)
    for at in range(0, FF, CHUNK):
        d_act = dot_t(d_branch, down_ref[at : at + CHUNK, :])
        gate = gu_ref[:, at : at + CHUNK]
        up = gu_ref[:, FF + at : FF + at + CHUNK]
        sig = lax.logistic(gate)
        d_gate = (d_act * up * (sig * (1.0 + gate * (1.0 - sig)))).astype(BF)
        d_up = (d_act * (gate * sig)).astype(BF)
        dgu_ref[:, at : at + CHUNK] = d_gate
        dgu_ref[:, FF + at : FF + at + CHUNK] = d_up
        d_nf += dot_t(d_gate, packed_ref[:, GU_AT + at : GU_AT + at + CHUNK])
        d_nf += dot_t(d_up, packed_ref[:, GU_AT + FF + at : GU_AT + FF + at + CHUNK])
    d_norm, gain_ref[...] = rms_back(mid_ref[...], gain, d_nf)
    d_mid = d_x + d_norm
    dmid_ref[...] = d_mid
    d_attn = d_mid.astype(BF)
    da_ref[...] = d_attn
    d_att = dot_t(d_attn, packed_ref[:, OUT_AT : OUT_AT + width])
    nothing = jnp.zeros((rows, HD), F32)
    for h in range(H):
        g, j = divmod(h, GROUP)
        part = jnp.concatenate([nothing, d_att[:, h * HD : (h + 1) * HD]], 1).astype(BF)
        for p in range(2):
            do_ref[g, p, j * piece : (j + 1) * piece, :] = part[p * piece : (p + 1) * piece]


def fed_back_shapes(rows, width):
    piece = rows // 2
    return [
        shape((rows, width), BF),
        shape((rows, 2 * FF), BF),
        shape((rows, width), F32),
        shape((rows, width), BF),
        shape((KVH, 2, GROUP * piece, 2 * HD), BF),
        shape((1, width), F32),
    ]


def project_back(d_mid, dq_ref, parts, gain, packed_ref, x, c, s, outs):
    dq_raw_ref, dkv_raw_ref, gain_ref = outs
    dq = dq_ref[...].astype(F32)
    for h in range(H):
        a = dq[:, h * HD : h * HD + HALF]
        b = dq[:, h * HD + HALF : (h + 1) * HD]
        dq_raw_ref[:, h * HD : (h + 1) * HD] = jnp.concatenate([a * c + b * s, b * c - a * s], 1).astype(BF)
    for g in range(KVH):
        d = jnp.concatenate(
            [parts[0][g].astype(F32) + parts[1][g].astype(F32), parts[2][g].astype(F32) + parts[3][g].astype(F32)], 0
        ).astype(BF).astype(F32)
        a = d[:, :HALF]
        b = d[:, HALF:HD]
        dkv_raw_ref[:, g * HD : (g + 1) * HD] = jnp.concatenate([a * c + b * s, b * c - a * s], 1).astype(BF)
        dkv_raw_ref[:, (KVH + g) * HD : (KVH + g + 1) * HD] = d[:, HD:].astype(BF)
    d_normed = dot_t(dq_raw_ref[...], packed_ref[:, Q_AT : Q_AT + H * HD])
    d_normed += dot_t(dkv_raw_ref[...], packed_ref[:, KV_AT : KV_AT + 2 * KVH * HD])
    d_in, gain_ref[...] = rms_back(x, gain, d_normed)
    return d_mid + d_in


def back_first_kernel(
    da0_ref, da1_ref, db0_ref, db1_ref, x_ref, target_ref, weight_ref, gain_ref, packed_ref, down_ref, mid_ref, gu_ref,
    *outs,
):
    d_a = da0_ref[...].astype(F32) + da1_ref[...].astype(F32)
    d_b = db0_ref[...].astype(F32) + db1_ref[...].astype(F32)
    d_final = jnp.concatenate([d_a, d_b], 0) + column(weight_ref[...]) * target_ref[...].astype(F32)
    d_x, outs[0][...] = rms_back(x_ref[...], gain_ref[2:3, :], d_final)
    feed_back(d_x, gain_ref[1:2, :], packed_ref, down_ref, mid_ref, gu_ref, outs[1:])


def back_mid_kernel(
    dmid_ref, dq_ref, a0_ref, a1_ref, b0_ref, b1_ref, x_ref, c_ref, s_ref, gain_ref, packed_ref, down_ref, mid_ref, gu_ref,
    *outs,
):
    d_x = project_back(
        dmid_ref[...], dq_ref, (a0_ref, a1_ref, b0_ref, b1_ref), gain_ref[0:1, :], packed_ref,
        x_ref[...], c_ref[...], s_ref[...], outs[:3],
    )
    feed_back(d_x, gain_ref[1:2, :], packed_ref, down_ref, mid_ref, gu_ref, outs[3:])


def back_last_kernel(
    dmid_ref, dq_ref, a0_ref, a1_ref, b0_ref, b1_ref, x_ref, c_ref, s_ref, gain_ref, packed_ref, *outs
):
    d_x = project_back(
        dmid_ref[...], dq_ref, (a0_ref, a1_ref, b0_ref, b1_ref), gain_ref[0:1, :], packed_ref,
        x_ref[...], c_ref[...], s_ref[...], outs[:3],
    ).astype(BF)
    outs[3][...] = d_x


def head_kernel(vocab, active_ref, hit_ref, table_ref, *refs):
    pieces, (u_ref, stat_ref), (rows_ref, s_ref) = refs[:-4], refs[-4:-2], refs[-2:]
    piece = pieces[0].shape[0]
    rows = 2 * piece
    for k, ref in enumerate(pieces):
        rows_ref[k * piece : (k + 1) * piece, :] = ref[...]
    padded = table_ref.shape[0]

    def block(i, _):
        at_row = pl.multiple_of(i * rows, rows)

        @pl.when(active_ref[i] == 0)
        def _():
            u_ref[pl.ds(at_row, rows), :] = jnp.zeros((rows, u_ref.shape[1]), F32)
            stat_ref[i] = jnp.concatenate([jnp.zeros((1, rows), F32), jnp.ones((1, rows), F32)], 0)

        @pl.when(active_ref[i] != 0)
        def _():
            mine = rows_ref[pl.ds(at_row, rows), :]
            hits = column(hit_ref[i])
            highest = jnp.full((rows, 1), -jnp.inf, F32)
            for at in range(0, padded, VTILE):
                s = dot_t(mine, table_ref[at : at + VTILE, :])
                if at + VTILE > vocab:
                    cols = lax.broadcasted_iota(jnp.int32, (rows, VTILE), 1) + at
                    s = jnp.where(cols < vocab, s, -jnp.inf)
                s_ref[:, at : at + VTILE] = s
                highest = jnp.maximum(highest, jnp.max(s, -1, keepdims=True))
            total = jnp.zeros((rows, 1), F32)
            u = jnp.zeros((rows, u_ref.shape[1]), F32)
            for at in range(0, padded, VTILE):
                e = jnp.exp(s_ref[:, at : at + VTILE] - highest)
                total += jnp.sum(e, -1, keepdims=True)
                cols = lax.broadcasted_iota(jnp.int32, (rows, VTILE), 1) + at
                e = jnp.where(cols == hits, 0.0, e).astype(BF)
                u += dot(e, table_ref[at : at + VTILE, :])
            u_ref[pl.ds(at_row, rows), :] = u
            lane = lax.broadcasted_iota(jnp.int32, (rows, 8), 1)
            stat_ref[i] = jnp.transpose(jnp.where(lane == 0, highest, total))[0:2, :]

        return 0

    lax.fori_loop(0, u_ref.shape[0] // rows, block, 0)


def head_forward(active, hits, table, pieces, vocab):
    piece, width = pieces[0].shape
    count = piece * len(pieces)
    rows = 2 * piece
    return call(
        functools.partial(head_kernel, vocab),
        "head_forward",
        [active, hits, table] + pieces,
        [shape((count, width), F32), shape((count // rows, 2, rows), F32)],
        [pltpu.VMEM((count, width), BF), pltpu.VMEM((rows, table.shape[0]), F32)],
        scalars=1,
        flops=4 * count * table.size,
    )


def scale_kernel(n, orders, u_ref, scale_ref, *refs):
    stats, (norm_ref, *outs) = refs[:n], refs[n:]
    blocks = norm_ref.shape[0]
    rows = norm_ref.shape[2]
    piece = rows // 2
    halves = (outs[0:2], outs[2:4])
    spots = [{r: (k // (n // 2), k % (n // 2)) for k, r in enumerate(o)} for o in orders]
    per_half = blocks // 2
    for j in range(blocks):
        half, jj = divmod(j, per_half)
        found = []
        for b in range(n):
            st = stats[b][half * per_half + (jj ^ (b >> 1))]
            if b & 1:
                st = jnp.concatenate([st[:, piece:], st[:, :piece]], 1)
            found.append(st)
        top = found[0][0:1]
        for st in found[1:]:
            top = jnp.maximum(top, st[0:1])
        total = jnp.zeros_like(top)
        for st in found:
            total += st[1:2] * jnp.exp(st[0:1] - top)
        log_norm = top + jnp.log(total)
        norm_ref[j] = log_norm
        factor = column(jnp.exp(found[0][0:1] - log_norm) * scale_ref[j])
        scaled = u_ref[j * rows : (j + 1) * rows, :] * factor
        for k in range(2):
            side, at = spots[half][2 * jj + k]
            ref = halves[half][side]
            ref[at] = scaled[k * piece : (k + 1) * piece].astype(ref.dtype)


def head_scale(u, scale, stats, orders):
    n = len(stats)
    count, width = u.shape
    piece = count // (2 * n)
    block = (n // 2, piece, width)
    return call(
        functools.partial(scale_kernel, n, orders),
        "head_scale",
        [u, scale] + stats,
        [shape(scale.shape, F32)] + [shape(block, F32), shape(block, BF)] * 2,
        flops=2 * u.size,
    )


def head_grad_kernel(first, active_ref, stat_ref, hit_ref, table_ref, *refs):
    if first:
        pieces, grad_ref, rows_ref = refs[:-2], refs[-2], refs[-1]
        grad_ref[...] = jnp.zeros_like(grad_ref)
    else:
        pieces, grad_ref, rows_ref = refs[1:-2], refs[-2], refs[-1]
        grad_ref[...] = refs[0][...]
    piece = pieces[0].shape[0]
    rows = 2 * piece
    for k, ref in enumerate(pieces):
        rows_ref[k * piece : (k + 1) * piece, :] = ref[...]
    vocab = grad_ref.shape[0]
    tile = vocab // 5

    def block(i, _):
        @pl.when(active_ref[i] != 0)
        def _():
            mine = rows_ref[pl.ds(pl.multiple_of(i * rows, rows), rows), :]
            log_norm = stat_ref[i, 0:1, :]
            scale = stat_ref[i, 1:2, :]
            hits = hit_ref[i]
            for at in range(0, vocab, tile):
                s = dot_t(table_ref[at : at + tile, :], mine)
                d = jnp.exp(s - log_norm) * scale
                index = lax.broadcasted_iota(jnp.int32, (tile, rows), 0) + at
                d = jnp.where(index == hits, d - scale, d).astype(BF)
                grad_ref[at : at + tile, :] += dot(d, mine)

        return 0

    lax.fori_loop(0, rows_ref.shape[0] // rows, block, 0)


def head_grad(active, stats, hits, table, pieces, vocab, so_far):
    piece, width = pieces[0].shape
    count = piece * len(pieces)
    first = so_far is None
    return call(
        functools.partial(head_grad_kernel, first),
        "head_grad",
        [active, stats, hits, table] + ([] if first else [so_far]) + pieces,
        [shape((vocab, width), F32)],
        [pltpu.VMEM((count, width), BF)],
        scalars=1,
        limit=48,
        flops=2 * count * table.size,
        aliases={} if first else {4: 0},
    )[0]


def add_rows_kernel(bits, slots, count_ref, key_ref, grad_ref, *refs):
    pieces, (out_ref, square_ref, wide_ref) = refs[:-3], refs[-3:]
    out_ref[...] = grad_ref[...]
    piece = pieces[0].shape[0]
    per_slot = len(pieces) // slots
    for slot in range(slots):
        for k in range(per_slot):
            wide_ref[k * piece : (k + 1) * piece, :] = pieces[slot * per_slot + k][...].astype(F32)

        def add(i, _):
            key = key_ref[slot, i]
            row = key >> bits
            at = key & ((1 << bits) - 1)
            out_ref[pl.ds(row, 1), :] += wide_ref[pl.ds(at, 1), :]
            return 0

        lax.fori_loop(0, count_ref[slot], add, 0)
    tile = 80
    width = out_ref.shape[1]

    def squares(i, total):
        v = out_ref[pl.ds(pl.multiple_of(i * tile, 8), tile), :]
        return total + jnp.sum((v * v).reshape(tile // 8, 8, width), 0)

    square_ref[...] = lax.fori_loop(0, out_ref.shape[0] // tile, squares, jnp.zeros((8, width), F32))


def add_rows(counts, keys, grad, slots, bits):
    pieces = [p for slot in slots for p in slot]
    piece, width = pieces[0].shape
    return call(
        functools.partial(add_rows_kernel, bits, len(slots)),
        "add_rows",
        [counts, keys, grad] + pieces,
        [shape(grad.shape, F32), shape((8, width), F32)],
        [pltpu.VMEM((piece * len(slots[0]), width), F32)],
        scalars=2,
        limit=56,
        flops=2 * grad.size,
        aliases={2: 0},
    )


def adam_update(weight, first, second, grad, decay):
    next_first = BETA_ONE * first + (1.0 - BETA_ONE) * grad
    next_second = BETA_TWO * second + (1.0 - BETA_TWO) * grad * grad
    corrected = next_first / (1.0 - BETA_ONE**STEP_NO)
    scaled = jnp.sqrt(next_second / (1.0 - BETA_TWO**STEP_NO)) + ADAM_EPSILON
    return (weight - RATE * (corrected / scaled + decay * weight), next_first, next_second)


def table_adam_kernel(factor_ref, grad_ref, w_ref, m_ref, v_ref, new_w_ref, new_m_ref, new_v_ref):
    grad = jnp.transpose(grad_ref[...]) * factor_ref[0]
    new_w_ref[...], new_m_ref[...], new_v_ref[...] = adam_update(
        w_ref[...], m_ref[...], v_ref[...], grad, DECAY
    )


def table_adam(factor, grad, weight, first, second):
    vocab, width = grad.shape
    tile = 512
    spec = pl.BlockSpec((width, tile), lambda i: (0, i))
    outs = pl.pallas_call(
        table_adam_kernel,
        grid=(pl.cdiv(vocab, tile),),
        in_specs=[
            pl.BlockSpec(memory_space=pltpu.SMEM),
            pl.BlockSpec((tile, width), lambda i: (i, 0)),
            spec,
            spec,
            spec,
        ],
        out_specs=[spec] * 3,
        out_shape=[shape((width, vocab), F32)] * 3,
        compiler_params=pltpu.CompilerParams(vmem_limit_bytes=40 * MIB),
        cost_estimate=pl.CostEstimate(flops=20 * vocab * width, bytes_accessed=28 * vocab * width, transcendentals=0),
        name="table_adam",
    )(factor.reshape(1), grad, weight.T, first.T, second.T)
    return tuple(o.T for o in outs)


def body(*arguments):
    token_ids, response_mask = arguments[0], arguments[1]
    masters, firsts, seconds = arguments[4:11], arguments[11:18], arguments[18:25]
    embed_table, w_query, w_kv, w_out, w_gate_up, w_down, gains = masters
    groups = lax.axis_size("seq")
    batch = lax.axis_size("dp")
    me = lax.axis_index("seq")
    local_len = token_ids.shape[1]
    seq_len = groups * local_len
    piece = local_len // 2
    pieces = 2 * groups
    vocab, width = embed_table.shape
    base = me * vocab
    rows = local_len
    first_order, second_order = bit_orders(groups)
    orders = (stack_order(first_order), stack_order(second_order))

    packed = jnp.concatenate(
        [
            w_kv.astype(BF),
            w_gate_up.astype(BF),
            w_query.astype(BF),
            jnp.zeros((w_query.shape[0], OUT_AT - Q_AT - w_query.shape[1]), BF),
            w_out.astype(BF),
            gains.T.astype(BF),
            jnp.zeros((w_query.shape[0], PACKED - GAIN_AT - 3), BF),
        ],
        1,
    )
    packed_full = lax.all_gather(packed, "seq", axis=0, tiled=True)
    down_full = lax.all_gather(w_down.astype(BF), "seq", axis=0, tiled=True)
    gain_rows = packed_full[:, GAIN_AT : GAIN_AT + 3].T.astype(F32)
    padded = (vocab + VTILE - 1) // VTILE * VTILE
    table = low_table(embed_table, padded)

    meta = jnp.concatenate([token_ids, response_mask], 0)
    held = {0: meta}
    for bit in first_order:
        held.update({r ^ bit: swap(v, "seq", bit) for r, v in list(held.items())})
    relative = jnp.stack([held[r] for r in range(groups)], 0)
    who = jnp.arange(groups) ^ me
    spots = (who[None, :] == jnp.arange(groups)[:, None]).astype(jnp.int32)
    ordered = jnp.sum(spots[:, :, None, None] * relative[None], 1)
    ordered = jnp.swapaxes(ordered, 0, 1).reshape(2, seq_len)

    order = jnp.concatenate([who, pieces - 1 - who])
    pick = order[:, None] == jnp.arange(pieces)[None, :]

    def met(values):
        cut = values.reshape(values.shape[0], 1, pieces, piece)
        chosen = jnp.sum(jnp.where(pick[None, :, :, None], cut, jnp.zeros((), values.dtype)), 2)
        return chosen.reshape(values.shape[0], pieces * piece)

    extra = 16
    ids_row = ordered[0]
    follow = jnp.concatenate([ids_row, jnp.zeros((piece,), jnp.int32)]).reshape(pieces + 1, piece)
    ids_wide = jnp.concatenate([ids_row.reshape(pieces, piece), follow[1:, :extra]], 1)
    wanted = jnp.concatenate([who[jnp.array(orders[0])], pieces - 1 - who[jnp.array(orders[1])]])
    ids_wide = jnp.sum(
        jnp.where((wanted[:, None] == jnp.arange(pieces)[None, :])[:, :, None], ids_wide[None], 0), 1
    )
    found = lookup((ids_wide - base).reshape(-1), table, 4 * (piece + extra))
    found = found.reshape(4, groups // 2, piece + extra, width)
    keep, got = scatter_stack(found[0], found[1], "seq", first_order, True)
    got_a = keep + got
    keep, got = scatter_stack(found[2], found[3], "seq", second_order, True)
    got_b = keep + got
    hidden = jnp.concatenate([got_a[:piece], got_b[:piece]], 0).astype(F32)
    target_rows = jnp.concatenate([got_a[1 : piece + 1], got_b[1 : piece + 1]], 0)

    all_meta = jnp.stack(ring(ordered, "dp"), 0)
    ids_all, mask_all = all_meta[:, 0], all_meta[:, 1]
    valid_all = mask_all.astype(F32) * (jnp.arange(seq_len) < seq_len - 1).astype(F32)[None]
    counted = jnp.sum(valid_all)
    targets_all = jnp.concatenate([ids_all[:, 1:], jnp.zeros((batch, 1), jnp.int32)], 1)
    own_pos = jnp.concatenate(
        [order[0] * piece + jnp.arange(piece), order[groups] * piece + jnp.arange(piece)]
    )
    inverse = 10000.0 ** (-jnp.arange(HALF).astype(F32) * 2.0 / HD)
    phases = own_pos.astype(F32)[:, None] * inverse[None, :]
    cosine, sine_wave = jnp.cos(phases), jnp.sin(phases)
    me_one = me.reshape(1).astype(jnp.int32)

    layer_flops = 2 * rows * width * (2 * H * HD + 2 * KVH * HD + 3 * FF)
    x0 = hidden
    normed0, q0, kv_a, kv_b = call(
        pre_kernel, "pre", [x0, gain_rows, packed_full, cosine, sine_wave], projected_shapes(rows, width),
        flops=layer_flops // 4,
    )
    kv0 = gather_pair(kv_a, kv_b, "seq")
    o0, lse0 = attend(me_one, q0, *kv0)
    mid0, nf0, gu0, act0, x1, normed1, q1, kv_a, kv_b = call(
        mid_kernel, "mid", [x0, o0, gain_rows, packed_full, down_full, cosine, sine_wave],
        fed_shapes(rows, width) + projected_shapes(rows, width), flops=layer_flops,
    )
    kv1 = gather_pair(kv_a, kv_b, "seq")
    o1, lse1 = attend(me_one, q1, *kv1)
    mid1, nf1, gu1, act1, x2, final_a, final_b = call(
        post_kernel, "post", [x1, o1, gain_rows, packed_full, down_full],
        fed_shapes(rows, width) + [shape((piece, width), BF)] * 2, flops=layer_flops,
    )
    rows_a, rows_b = gather_pair(final_a, final_b, "seq")
    others = list(zip(ring(final_a, "dp")[1:], ring(final_b, "dp")[1:]))

    blocks = seq_len // rows
    met_valid = met(valid_all)
    met_target = (met(targets_all) - base).reshape(batch, blocks, 1, rows)
    scale_all = (met_valid / counted).reshape(batch, blocks, 1, rows)
    active = (jnp.max(met_valid.reshape(batch, blocks, rows), -1) > 0).astype(jnp.int32)
    u, stats = head_forward(active[0], met_target[0], table, rows_a + rows_b, vocab)
    all_stats = [stats] + [swap(stats, "seq", b) for b in range(1, groups)]
    log_norm, keep_a, send_a, keep_b, send_b = head_scale(u, scale_all[0], all_stats, orders)
    part_a = scatter_stack(keep_a, send_a, "seq", first_order)
    part_b = scatter_stack(keep_b, send_b, "seq", second_order)
    norms = ring(log_norm, "dp")

    def add_head_grad(slot, row_pieces, so_far):
        both = jnp.concatenate([norms[slot], scale_all[slot]], 1)
        return head_grad(active[slot], both, met_target[slot], table, row_pieces, vocab, so_far)

    own_norm = jnp.concatenate([log_norm[0, 0, :piece], log_norm[blocks // 2, 0, :piece]])
    own_scale = jnp.concatenate([scale_all[0, 0, 0, :piece], scale_all[0, blocks // 2, 0, :piece]])
    own_valid = jnp.concatenate([met_valid[0, :piece], met_valid[0, groups * piece : (groups + 1) * piece]])
    final = jnp.concatenate([final_a, final_b], 0)
    picked = jnp.sum(final.astype(F32) * target_rows.astype(F32), -1)
    loss_part = jnp.sum((own_norm - picked) * own_valid)
    at_target = ((jnp.exp(picked - own_norm) - 1.0) * own_scale).astype(BF).astype(F32).reshape(1, rows)

    grad_table = add_head_grad(0, rows_a + rows_b, None)
    other_rows = []
    for a, b in others:
        got_rows = gather_pair(a, b, "seq")
        other_rows.append(got_rows[0] + got_rows[1])

    last_a = after(part_a[0], grad_table)
    outs = call(
        back_first_kernel, "back_first",
        [last_a, part_a[1], part_b[0], part_b[1], x2, target_rows, at_target, gain_rows, packed_full, down_full, mid1, gu1],
        [shape((1, width), F32)] + fed_back_shapes(rows, width), flops=2 * layer_flops,
    )
    gain_final, db1, dgu1, dmid1, da1, do1, gain_ffn1 = outs
    dq1, keep_a, send_a, keep_b, send_b = attend_back(me_one, q1, do1, lse1, *kv1, orders)
    part_a = scatter_stack(keep_a, send_a, "seq", first_order)
    part_b = scatter_stack(keep_b, send_b, "seq", second_order)
    grad_table = add_head_grad(1, other_rows[0], grad_table)
    last_a = after(part_a[0], grad_table)
    outs = call(
        back_mid_kernel, "back_mid",
        [dmid1, dq1, last_a, part_a[1], part_b[0], part_b[1], x1, cosine, sine_wave, gain_rows, packed_full, down_full, mid0, gu0],
        [shape((rows, H * HD), BF), shape((rows, 2 * KVH * HD), BF), shape((1, width), F32)] + fed_back_shapes(rows, width),
        flops=2 * layer_flops,
    )
    dq_raw1, dkv_raw1, gain_attn1, db0, dgu0, dmid0, da0, do0, gain_ffn0 = outs
    dq0, keep_a, send_a, keep_b, send_b = attend_back(me_one, q0, do0, lse0, *kv0, orders)

    def two(left0, left1, right0, right1):
        return dot_w(jnp.concatenate([left0, left1], 0), jnp.concatenate([right0, right1], 0))

    grad_down = two(act0, act1, db0, db1)
    grad_gate = two(nf0, nf1, dgu0, dgu1)
    grad_out = two(o0, o1, da0, da1)
    early = jnp.concatenate([grad_gate, grad_out], 1)
    early_part = lax.psum_scatter(early, "seq", scatter_dimension=0, tiled=True)
    down_part = lax.psum_scatter(grad_down, "seq", scatter_dimension=0, tiled=True)
    early_part, down_part = lax.psum((early_part, down_part), "dp")

    part_a = scatter_stack(keep_a, send_a, "seq", first_order)
    part_b = scatter_stack(keep_b, send_b, "seq", second_order)
    grad_table = add_head_grad(2, other_rows[1], grad_table)
    last_a = after(part_a[0], grad_table)
    outs = call(
        back_last_kernel, "back_last",
        [dmid0, dq0, last_a, part_a[1], part_b[0], part_b[1], x0, cosine, sine_wave, gain_rows, packed_full],
        [shape((rows, H * HD), BF), shape((rows, 2 * KVH * HD), BF), shape((1, width), F32), shape((rows, width), BF)],
        flops=layer_flops // 2,
    )
    dq_raw0, dkv_raw0, gain_attn0, d_low = outs

    slots = []
    for x in ring(d_low, "dp"):
        got_rows = gather_pair(x[:piece], x[piece:], "seq")
        slots.append(got_rows[0] + got_rows[1])
    for slot in range(3, batch):
        grad_table = add_head_grad(slot, other_rows[slot - 1], grad_table)
    bits = (seq_len - 1).bit_length()
    met_ids = met(ids_all) - base
    inside = (met_ids >= 0) & (met_ids < vocab)
    keys = jnp.where(inside, met_ids * (1 << bits) + jnp.arange(seq_len)[None], 2147483647)
    keys = jnp.sort(keys, -1)
    counts = jnp.sum(inside.astype(jnp.int32), -1)
    grad_table, table_squares = add_rows(counts, keys, grad_table, slots, bits)

    grad_query = two(normed0, normed1, dq_raw0, dq_raw1)
    grad_kv = two(normed0, normed1, dkv_raw0, dkv_raw1)
    gain_cols = jnp.concatenate([gain_attn0 + gain_attn1, gain_ffn0 + gain_ffn1, gain_final], 0).T
    late = jnp.concatenate([grad_kv, grad_query, gain_cols], 1)
    late_part = lax.psum(lax.psum_scatter(late, "seq", scatter_dimension=0, tiled=True), "dp")

    kv_width = w_kv.shape[1]
    g_kv, g_query, g_gain = (
        late_part[:, :kv_width],
        late_part[:, kv_width : kv_width + w_query.shape[1]],
        late_part[:, kv_width + w_query.shape[1] :],
    )
    g_gate, g_out = early_part[:, : 2 * FF], early_part[:, 2 * FF :]
    reduced = (None, g_query, g_kv, g_out, g_gate, down_part, g_gain.T)
    squares = jnp.sum(table_squares)
    for part in (early_part, late_part, down_part):
        squares = squares + jnp.sum(part * part)
    both = total_over(jnp.stack([squares, loss_part]), "seq")
    grad_norm = jnp.sqrt(both[0])
    loss = sum(ring(both[1], "dp")) / counted
    factor = CLIP / jnp.maximum(grad_norm, CLIP)
    news = [table_adam(factor, grad_table, masters[0], firsts[0], seconds[0])] + [
        adam_update(masters[i], firsts[i], seconds[i], reduced[i] * factor, DECAY if i < 6 else 0.0)
        for i in range(1, 7)
    ]
    return tuple(n[0] for n in news) + tuple(n[1] for n in news) + tuple(n[2] for n in news) + (loss, grad_norm)


def solution(mesh):
    rows, cols, whole = P("seq", None), P(None, "seq"), P()
    group = (rows,) * 6 + (cols,)
    return jax.shard_map(
        body,
        mesh=mesh,
        in_specs=(P("dp", "seq"), P("dp", "seq"), whole, whole) + group * 3,
        out_specs=group * 3 + (whole, whole),
        check_vma=False,
    )
```

```python
import functools

import jax
import jax.numpy as jnp
from jax import lax
from jax.experimental import pallas as pl
from jax.experimental.pallas import tpu as pltpu
from jax.sharding import PartitionSpec as P

H = 9
KVH = 3
GROUP = H // KVH
HD = 64
HALF = HD // 2
FF = 1536
LAYERS = 2
STEP_NO = 10
EPSILON = 1e-05
CLIP = 0.01
RATE = 0.1
BETA_ONE = 0.9
BETA_TWO = 0.95
ADAM_EPSILON = 1e-08
DECAY = 0.1
MASKED = -1000000000.0
BF = jnp.bfloat16
F32 = jnp.float32
MIB = 1024 * 1024

KV_AT, Q_AT, GAIN_AT, EARLY = 0, 384, 960, 1024
GU_AT, OUT_AT = 0, 3072
CHUNK = 512
VTILE = 1024


def swap(x, axis, bit):
    n = lax.axis_size(axis)
    return lax.ppermute(x, axis, [(i, i ^ bit) for i in range(n)])


def gather_all(x, axis):
    n = lax.axis_size(axis)
    held = {0: x}
    for r in range(2, n, 2):
        held[r] = swap(x, axis, r)
    for r in range(0, n, 2):
        held[r + 1] = swap(held[r], axis, 1)
    return [held[r] for r in range(n)]


def merge_kernel(keep_ref, got_ref, own_ref, *others):
    for k in range(keep_ref.shape[0]):
        ref = others[k - 1] if k else own_ref
        ref[...] = (keep_ref[k].astype(F32) + got_ref[k].astype(F32)).astype(ref.dtype)


def scatter_all(keep, send, axis, wire, own=F32, between=None, until=None):
    got = swap(send, axis, 1)
    if between is not None:
        got = after(got, between())
    block = keep.shape[1:]
    outs = call(
        merge_kernel, "merge", [keep, got],
        [shape(block, own)] + [shape(block, wire)] * (keep.shape[0] - 1), limit=32,
    )
    arrived = [swap(x, axis, 2 * k) for k, x in enumerate(outs) if k]
    if until is not None:
        arrived = all_after(arrived, until())
    return [outs[0]] + arrived


def everyone(x, axis):
    return [x] + [swap(x, axis, r) for r in range(1, lax.axis_size(axis))]


def tree(terms):
    while len(terms) > 1:
        terms = [a + b for a, b in zip(terms[::2], terms[1::2])]
    return terms[0]


def after(x, *needs):
    return lax.optimization_barrier((x,) + needs)[0]


def all_after(xs, *needs):
    return list(lax.optimization_barrier(tuple(xs) + needs)[: len(xs)])


def dot(a, b):
    return jnp.dot(a, b, preferred_element_type=F32)


def dot_t(a, b):
    return lax.dot_general(a, b, (((1,), (1,)), ((), ())), preferred_element_type=F32)


def dot_w(a, b):
    return lax.dot_general(a, b, (((0,), (0,)), ((), ())), preferred_element_type=F32)


def inverse_rms(values):
    return lax.rsqrt(jnp.mean(values * values, -1, keepdims=True) + EPSILON)


def rms_back(values, gain_row, d_out):
    r = inverse_rms(values)
    scaled = gain_row * d_out
    d_values = r * scaled - values * (r * r * r * jnp.mean(values * scaled, -1, keepdims=True))
    return d_values, jnp.sum(d_out * values * r, 0, keepdims=True)


def pack(x):
    p, width = x.shape
    full = width // 128 * 128
    last = x[:, full:]
    return jnp.concatenate(
        [x[:, at : at + 128] for at in range(0, full, 128)] + [jnp.concatenate([last[: p // 2], last[p // 2 :]], 1)], 0
    )


def unpack(x, p):
    full = x.shape[0] // p
    last = x[full * p :]
    side = last.shape[1] // 2
    return jnp.concatenate(
        [x[k * p : (k + 1) * p] for k in range(full)] + [jnp.concatenate([last[:, :side], last[:, side:]], 0)], 1
    )


def column(row):
    return jnp.transpose(jnp.broadcast_to(row, (8, row.shape[1])))[:, 0:1]


def staged(v):
    return v.dtype != BF or v.shape[-2] % 16 == 0


def staging_kernel(kernel, scalars, count_in, count_out, moved_in, moved_out, *refs):
    ins, outs, rest = refs[:count_in], refs[count_in : count_in + count_out], refs[count_in + count_out :]
    extra = len(moved_in) + len(moved_out) + 1
    own, buffers, sems = rest[: len(rest) - extra], rest[len(rest) - extra : -1], rest[-1]
    ins, outs = list(ins), list(outs)
    copies = []
    for k, at in enumerate(moved_in):
        copies.append(pltpu.make_async_copy(ins[at], buffers[k], sems.at[k]))
        ins[at] = buffers[k]
    backs = []
    for k, at in enumerate(moved_out):
        k = k + len(moved_in)
        backs.append(pltpu.make_async_copy(buffers[k], outs[at], sems.at[k]))
        outs[at] = buffers[k]
    for copy in copies:
        copy.start()
    for copy in copies:
        copy.wait()
    kernel(*ins, *outs, *own)
    for copy in backs:
        copy.start()
    for copy in backs:
        copy.wait()


def call(kernel, name, inputs, outputs, scratch=(), scalars=0, limit=40, flops=0, managed=()):
    smem = pl.BlockSpec(memory_space=pltpu.SMEM)
    far = pl.BlockSpec(memory_space=pltpu.HBM)

    def whole(v):
        dims = len(v.shape)
        return pl.BlockSpec(v.shape, lambda i: (0,) * dims, pipeline_mode=pl.Buffered(1))

    moved_in = [k for k, v in enumerate(inputs) if k >= scalars and k not in managed and staged(v)]
    moved_out = [k for k, v in enumerate(outputs) if staged(v)]
    buffers = [pltpu.VMEM(inputs[k].shape, inputs[k].dtype) for k in moved_in]
    buffers += [pltpu.VMEM(outputs[k].shape, outputs[k].dtype) for k in moved_out]
    bytes_moved = sum(v.size * v.dtype.itemsize for v in list(inputs) + list(outputs))
    return pl.pallas_call(
        functools.partial(
            staging_kernel, kernel, scalars, len(inputs), len(outputs), moved_in, moved_out
        ),
        grid=(1,),
        in_specs=[smem if k < scalars else far if k in moved_in else whole(v) for k, v in enumerate(inputs)],
        out_specs=[far if k in moved_out else whole(v) for k, v in enumerate(outputs)],
        out_shape=list(outputs),
        scratch_shapes=list(scratch) + buffers + [pltpu.SemaphoreType.DMA((len(buffers),))],
        compiler_params=pltpu.CompilerParams(vmem_limit_bytes=limit * MIB),
        cost_estimate=pl.CostEstimate(flops=flops, bytes_accessed=bytes_moved, transcendentals=0),
        name=name,
    )(*inputs)


def shape(dims, dtype):
    return jax.ShapeDtypeStruct(tuple(dims), dtype)


def table_kernel(vocab, wide_ref, out_ref):
    tile = out_ref.shape[0]
    at = pl.program_id(0) * tile
    x = wide_ref[...]
    cols = lax.broadcasted_iota(jnp.int32, x.shape, 1) + at
    out_ref[...] = jnp.transpose(jnp.where(cols < vocab, x, 0.0)).astype(BF)


def low_table(embed_table, padded):
    vocab, width = embed_table.shape
    tile = 512
    return pl.pallas_call(
        functools.partial(table_kernel, vocab),
        grid=(padded // tile,),
        in_specs=[pl.BlockSpec((width, tile), lambda i: (0, i))],
        out_specs=pl.BlockSpec((tile, width), lambda i: (i, 0)),
        out_shape=shape((padded, width), BF),
        compiler_params=pltpu.CompilerParams(vmem_limit_bytes=24 * MIB),
        cost_estimate=pl.CostEstimate(flops=0, bytes_accessed=6 * padded * width, transcendentals=0),
        name="low_table",
    )(embed_table.T)


def lookup_kernel(ids_ref, table_ref, out_ref):
    rows = out_ref.shape[0]
    total = jnp.zeros(out_ref.shape, F32)
    for at in range(0, table_ref.shape[0], VTILE):
        cols = lax.broadcasted_iota(jnp.int32, (rows, VTILE), 1) + at
        hot = jnp.where(cols == ids_ref[...], 1.0, 0.0).astype(BF)
        total += dot(hot, table_ref[at : at + VTILE, :])
    out_ref[...] = total.astype(BF)


def lookup(ids, table, block):
    count = ids.shape[0]
    width = table.shape[1]
    return pl.pallas_call(
        lookup_kernel,
        grid=(count // block,),
        in_specs=[
            pl.BlockSpec((block, 1), lambda i: (i, 0)),
            pl.BlockSpec(table.shape, lambda i: (0, 0)),
        ],
        out_specs=pl.BlockSpec((block, width), lambda i: (i, 0)),
        out_shape=shape((count, width), BF),
        compiler_params=pltpu.CompilerParams(vmem_limit_bytes=40 * MIB),
        cost_estimate=pl.CostEstimate(
            flops=2 * count * table.size, bytes_accessed=2 * table.size, transcendentals=0
        ),
        name="lookup",
    )(ids.reshape(count, 1), table)


def project(x, gain, packed_ref, c, s, normed_ref, q_ref, kv_ref):
    piece = x.shape[0] // 2
    normed = (x * inverse_rms(x) * gain).astype(BF)
    normed_ref[...] = normed
    q = dot(normed, packed_ref[:, Q_AT : Q_AT + H * HD])
    kv = dot(normed, packed_ref[:, KV_AT : KV_AT + 2 * KVH * HD])
    nothing = jnp.zeros((x.shape[0], HD), F32)
    for h in range(H):
        g, j = divmod(h, GROUP)
        a = q[:, h * HD : h * HD + HALF]
        b = q[:, h * HD + HALF : (h + 1) * HD]
        turned = jnp.concatenate([(a * c - b * s) * 0.125, (a * s + b * c) * 0.125, nothing], 1).astype(BF)
        for p in range(2):
            q_ref[g, p, j * piece : (j + 1) * piece, :] = turned[p * piece : (p + 1) * piece]
    for g in range(KVH):
        a = kv[:, g * HD : g * HD + HALF]
        b = kv[:, g * HD + HALF : (g + 1) * HD]
        v = kv[:, (KVH + g) * HD : (KVH + g + 1) * HD]
        turned = jnp.concatenate([a * c - b * s, a * s + b * c, v], 1).astype(BF)
        kv_ref[0, g] = turned[:piece]
        kv_ref[1, g] = turned[piece:]


def feed(x, o_ref, gain, packed_ref, down_ref, mid_ref, nf_ref, gu_ref, act_ref):
    x_mid = x + dot(o_ref[...], packed_ref[:, OUT_AT : OUT_AT + x.shape[1]])
    mid_ref[...] = x_mid
    nf = (x_mid * inverse_rms(x_mid) * gain).astype(BF)
    nf_ref[...] = nf
    total = x_mid
    for at in range(0, FF, CHUNK):
        gate = dot(nf, packed_ref[:, GU_AT + at : GU_AT + at + CHUNK])
        up = dot(nf, packed_ref[:, GU_AT + FF + at : GU_AT + FF + at + CHUNK])
        gu_ref[:, at : at + CHUNK] = gate
        gu_ref[:, FF + at : FF + at + CHUNK] = up
        act = (gate * lax.logistic(gate) * up).astype(BF)
        act_ref[:, at : at + CHUNK] = act
        total = total + dot(act, down_ref[at : at + CHUNK, :])
    return total


def pre_kernel(x_ref, gain_ref, first_ref, c_ref, s_ref, normed_ref, q_ref, kv_ref):
    project(x_ref[...], gain_ref[0:1, :], first_ref, c_ref[...], s_ref[...], normed_ref, q_ref, kv_ref)


def mid_kernel(
    x_ref, o_ref, gain_ref, first_ref, packed_ref, down_ref, c_ref, s_ref,
    mid_ref, nf_ref, gu_ref, act_ref, next_ref, normed_ref, q_ref, kv_ref,
):
    x = feed(x_ref[...], o_ref, gain_ref[1:2, :], packed_ref, down_ref, mid_ref, nf_ref, gu_ref, act_ref)
    next_ref[...] = x
    project(x, gain_ref[0:1, :], first_ref, c_ref[...], s_ref[...], normed_ref, q_ref, kv_ref)


def post_kernel(
    x_ref, o_ref, gain_ref, packed_ref, down_ref,
    mid_ref, nf_ref, gu_ref, act_ref, next_ref, both_ref,
):
    x = feed(x_ref[...], o_ref, gain_ref[1:2, :], packed_ref, down_ref, mid_ref, nf_ref, gu_ref, act_ref)
    next_ref[...] = x
    final = x * inverse_rms(x) * gain_ref[2:3, :]
    piece = x.shape[0] // 2
    for p in range(2):
        both_ref[p] = pack(final[p * piece : (p + 1) * piece]).astype(BF)


def projected_shapes(rows, width):
    piece = rows // 2
    return [
        shape((rows, width), BF),
        shape((KVH, 2, GROUP * piece, 2 * HD), BF),
        shape((2, KVH, piece, 2 * HD), BF),
    ]


def fed_shapes(rows, width):
    return [
        shape((rows, width), F32),
        shape((rows, width), BF),
        shape((rows, 2 * FF), F32),
        shape((rows, FF), BF),
        shape((rows, width), F32),
    ]


def causal(scores, piece):
    row = lax.broadcasted_iota(jnp.int32, scores.shape, 0) & (piece - 1)
    col = lax.broadcasted_iota(jnp.int32, scores.shape, 1)
    return jnp.where(row >= col, scores, MASKED)


def attend_kernel(n, me_ref, q_ref, *refs):
    kvs, (o_ref, lse_ref, kv_ref) = refs[:n], refs[n:]
    me = me_ref[0]
    piece = kvs[0].shape[2]
    lows = [None] + [(me ^ r) < me for r in range(1, n)]
    for g in range(KVH):
        for r in range(n):
            kv_ref[g, r * piece : (r + 1) * piece, :] = kvs[r][0, g]
            kv_ref[g, (n + r) * piece : (n + r + 1) * piece, :] = kvs[r][1, g]
        wide_kv = kv_ref[g, 0 : n * piece, :]
        q_a = q_ref[g, 0]
        q_b = q_ref[g, 1]
        wide = dot_t(q_b, wide_kv)
        own_a = causal(dot_t(q_a, kvs[0][0, g]), piece)
        own_b = causal(dot_t(q_b, kvs[0][1, g]), piece)
        m_a = jnp.max(own_a, -1, keepdims=True)
        m_b = jnp.maximum(jnp.max(own_b, -1, keepdims=True), jnp.max(wide, -1, keepdims=True))
        tiles = [None]
        for r in range(1, n):
            low = lows[r]
            tile = dot_t(jnp.where(low, q_a, q_b), jnp.where(low, kvs[r][0, g], kvs[r][1, g]))
            top = jnp.max(tile, -1, keepdims=True)
            m_a = jnp.maximum(m_a, top + jnp.where(low, 0.0, -jnp.inf))
            m_b = jnp.maximum(m_b, top + jnp.where(low, -jnp.inf, 0.0))
            tiles.append(tile)
        e = jnp.exp(wide - m_b)
        l_b = jnp.sum(e, -1, keepdims=True)
        o_b = dot(e.astype(BF), wide_kv)
        e = jnp.exp(own_b - m_b)
        l_b += jnp.sum(e, -1, keepdims=True)
        o_b += dot(e.astype(BF), kvs[0][1, g])
        e = jnp.exp(own_a - m_a)
        l_a = jnp.sum(e, -1, keepdims=True)
        o_a = dot(e.astype(BF), kvs[0][0, g])
        for r in range(1, n):
            low = lows[r]
            in_a = jnp.where(low, 1.0, 0.0)
            in_b = 1.0 - in_a
            e = jnp.exp(tiles[r] - (m_a * in_a + m_b * in_b))
            total = jnp.sum(e, -1, keepdims=True)
            o = dot(e.astype(BF), jnp.where(low, kvs[r][0, g], kvs[r][1, g]))
            l_a += total * in_a
            l_b += total * in_b
            o_a += o * in_a
            o_b += o * in_b
        lse_ref[g, 0] = m_a + jnp.log(l_a)
        lse_ref[g, 1] = m_b + jnp.log(l_b)
        out = [(o_a / l_a).astype(BF), (o_b / l_b).astype(BF)]
        for p in range(2):
            for j in range(GROUP):
                h = g * GROUP + j
                o_ref[p * piece : (p + 1) * piece, h * HD : (h + 1) * HD] = out[p][
                    j * piece : (j + 1) * piece, HD:
                ]


def attend(me, queries, kvs):
    n = len(kvs)
    piece = kvs[0].shape[2]
    stacked = GROUP * piece
    return call(
        functools.partial(attend_kernel, n),
        "attend",
        [me, queries] + kvs,
        [shape((2 * piece, H * HD), BF), shape((KVH, 2, stacked, 1), F32), shape((KVH, 2 * n * piece, 2 * HD), BF)],
        scalars=1,
        flops=2 * 2 * H * HD * piece * piece * (2 * n + 1) * 2,
    )


def attend_back_kernel(n, me_ref, q_ref, do_ref, lse_ref, kv_ref, *refs):
    (dq_ref, keep_ref, send_ref), (sum_ref,) = refs[:3], refs[3:]
    me = me_ref[0]
    piece = kv_ref.shape[1] // (2 * n)
    lows = [None] + [(me ^ r) < me for r in range(1, n)]
    for g in range(KVH):
        wide_kv = kv_ref[g, 0 : n * piece, :]
        kv_a0 = kv_ref[g, 0:piece, :]
        kv_b0 = kv_ref[g, n * piece : (n + 1) * piece, :]
        q_a, q_b = q_ref[g, 0], q_ref[g, 1]
        do_a, do_b = do_ref[g, 0], do_ref[g, 1]
        lse_a, lse_b = lse_ref[g, 0], lse_ref[g, 1]
        p_wide = jnp.exp(dot_t(q_b, wide_kv) - lse_b)
        w_wide = dot_t(do_b, wide_kv)
        d_b = jnp.sum(p_wide * w_wide, -1, keepdims=True)
        p_own_a = jnp.exp(causal(dot_t(q_a, kv_a0), piece) - lse_a)
        w_own_a = dot_t(do_a, kv_a0)
        d_a = jnp.sum(p_own_a * w_own_a, -1, keepdims=True)
        p_own_b = jnp.exp(causal(dot_t(q_b, kv_b0), piece) - lse_b)
        w_own_b = dot_t(do_b, kv_b0)
        d_b += jnp.sum(p_own_b * w_own_b, -1, keepdims=True)
        tiles = [None]
        for r in range(1, n):
            low = lows[r]
            in_a = jnp.where(low, 1.0, 0.0)
            in_b = 1.0 - in_a
            k = jnp.where(low, kv_ref[g, r * piece : (r + 1) * piece, :], kv_ref[g, (n + r) * piece : (n + r + 1) * piece, :])
            p = jnp.exp(dot_t(jnp.where(low, q_a, q_b), k) - (lse_a * in_a + lse_b * in_b))
            w = dot_t(jnp.where(low, do_a, do_b), k)
            total = jnp.sum(p * w, -1, keepdims=True)
            d_a += total * in_a
            d_b += total * in_b
            tiles.append((p, w))

        def both(p, w, inner, q, do, k):
            ds = (p * (w - inner)).astype(BF)
            dq = dot(ds, k)
            dkv = dot_w(ds, q) + dot_w(p.astype(BF), do)
            return dq, dkv

        dq_b, dkv = both(p_wide, w_wide, d_b, q_b, do_b, wide_kv)
        sum_ref[...] = dkv
        dq, dkv_b0 = both(p_own_b, w_own_b, d_b, q_b, do_b, kv_b0)
        dq_b += dq
        dq_a, dkv_a0 = both(p_own_a, w_own_a, d_a, q_a, do_a, kv_a0)
        sum_ref[0:piece, :] += dkv_a0

        def put(half, r, value):
            ref = send_ref if r & 1 else keep_ref
            ref[r // 2, half, g] = value

        put(1, 0, dkv_b0)
        for r in range(1, n):
            low = lows[r]
            in_a = jnp.where(low, 1.0, 0.0)
            in_b = 1.0 - in_a
            p, w = tiles[r]
            k = jnp.where(low, kv_ref[g, r * piece : (r + 1) * piece, :], kv_ref[g, (n + r) * piece : (n + r + 1) * piece, :])
            dq, dkv = both(p, w, d_a * in_a + d_b * in_b, jnp.where(low, q_a, q_b), jnp.where(low, do_a, do_b), k)
            dq_a += dq * in_a
            dq_b += dq * in_b
            sum_ref[r * piece : (r + 1) * piece, :] += dkv * in_a
            put(1, r, dkv * in_b)
        for r in range(n):
            put(0, r, sum_ref[r * piece : (r + 1) * piece, :])
        out = [(dq_a * 0.125).astype(BF), (dq_b * 0.125).astype(BF)]
        for p in range(2):
            for j in range(GROUP):
                h = g * GROUP + j
                dq_ref[p * piece : (p + 1) * piece, h * HD : (h + 1) * HD] = out[p][
                    j * piece : (j + 1) * piece, :HD
                ]


def attend_back(me, queries, d_out, lse, kv_all, n):
    piece = kv_all.shape[1] // (2 * n)
    block = (n // 2, 2, KVH, piece, 2 * HD)
    return call(
        functools.partial(attend_back_kernel, n),
        "attend_back",
        [me, queries, d_out, lse, kv_all],
        [shape((2 * piece, H * HD), BF), shape(block, F32), shape(block, F32)],
        [pltpu.VMEM((n * piece, 2 * HD), F32)],
        scalars=1,
        flops=5 * 2 * H * HD * piece * piece * (2 * n + 1) * 2,
    )


def feed_back(d_x, gain, packed_ref, down_ref, mid_ref, gu_ref, outs):
    db_ref, dgu_ref, dmid_ref, da_ref, do_ref, gain_ref = outs
    rows, width = d_x.shape
    piece = rows // 2
    d_branch = d_x.astype(BF)
    db_ref[...] = d_branch
    d_nf = jnp.zeros(d_x.shape, F32)
    for at in range(0, FF, CHUNK):
        d_act = dot_t(d_branch, down_ref[at : at + CHUNK, :])
        gate = gu_ref[:, at : at + CHUNK]
        up = gu_ref[:, FF + at : FF + at + CHUNK]
        sig = lax.logistic(gate)
        d_gate = (d_act * up * (sig * (1.0 + gate * (1.0 - sig)))).astype(BF)
        d_up = (d_act * (gate * sig)).astype(BF)
        dgu_ref[:, at : at + CHUNK] = d_gate
        dgu_ref[:, FF + at : FF + at + CHUNK] = d_up
        d_nf += dot_t(d_gate, packed_ref[:, GU_AT + at : GU_AT + at + CHUNK])
        d_nf += dot_t(d_up, packed_ref[:, GU_AT + FF + at : GU_AT + FF + at + CHUNK])
    d_norm, gain_ref[...] = rms_back(mid_ref[...], gain, d_nf)
    d_mid = d_x + d_norm
    dmid_ref[...] = d_mid
    d_attn = d_mid.astype(BF)
    da_ref[...] = d_attn
    d_att = dot_t(d_attn, packed_ref[:, OUT_AT : OUT_AT + width])
    nothing = jnp.zeros((rows, HD), F32)
    for h in range(H):
        g, j = divmod(h, GROUP)
        part = jnp.concatenate([nothing, d_att[:, h * HD : (h + 1) * HD]], 1).astype(BF)
        for p in range(2):
            do_ref[g, p, j * piece : (j + 1) * piece, :] = part[p * piece : (p + 1) * piece]


def fed_back_shapes(rows, width):
    piece = rows // 2
    return [
        shape((rows, width), BF),
        shape((rows, 2 * FF), BF),
        shape((rows, width), F32),
        shape((rows, width), BF),
        shape((KVH, 2, GROUP * piece, 2 * HD), BF),
        shape((1, width), F32),
    ]


def sum_refs(refs, at):
    total = refs[0][at].astype(F32)
    for ref in refs[1:]:
        total += ref[at].astype(F32)
    return total


def project_back(d_mid, dq_ref, parts, gain, packed_ref, x, c, s, outs):
    dq_raw_ref, dkv_raw_ref, gain_ref = outs
    dq = dq_ref[...].astype(F32)
    for h in range(H):
        a = dq[:, h * HD : h * HD + HALF]
        b = dq[:, h * HD + HALF : (h + 1) * HD]
        dq_raw_ref[:, h * HD : (h + 1) * HD] = jnp.concatenate([a * c + b * s, b * c - a * s], 1).astype(BF)
    for g in range(KVH):
        d = jnp.concatenate(
            [sum_refs(parts, (0, g)), sum_refs(parts, (1, g))], 0
        ).astype(BF).astype(F32)
        a = d[:, :HALF]
        b = d[:, HALF:HD]
        dkv_raw_ref[:, g * HD : (g + 1) * HD] = jnp.concatenate([a * c + b * s, b * c - a * s], 1).astype(BF)
        dkv_raw_ref[:, (KVH + g) * HD : (KVH + g + 1) * HD] = d[:, HD:].astype(BF)
    d_normed = dot_t(dq_raw_ref[...], packed_ref[:, Q_AT : Q_AT + H * HD])
    d_normed += dot_t(dkv_raw_ref[...], packed_ref[:, KV_AT : KV_AT + 2 * KVH * HD])
    d_in, gain_ref[...] = rms_back(x, gain, d_normed)
    return d_mid + d_in


def back_first_kernel(terms, x_ref, target_ref, weight_ref, gain_ref, packed_ref, down_ref, mid_ref, gu_ref, *refs):
    parts, outs = refs[:terms], refs[terms:]
    piece = x_ref.shape[0] // 2
    d_final = jnp.concatenate([unpack(sum_refs(parts, 0), piece), unpack(sum_refs(parts, 1), piece)], 0)
    d_final += column(weight_ref[...]) * target_ref[...].astype(F32)
    d_x, outs[0][...] = rms_back(x_ref[...], gain_ref[2:3, :], d_final)
    feed_back(d_x, gain_ref[1:2, :], packed_ref, down_ref, mid_ref, gu_ref, outs[1:])


def back_mid_kernel(
    terms, dmid_ref, dq_ref, x_ref, c_ref, s_ref, gain_ref, first_ref, packed_ref, down_ref, mid_ref, gu_ref, *refs
):
    parts, outs = refs[:terms], refs[terms:]
    d_x = project_back(
        dmid_ref[...], dq_ref, parts, gain_ref[0:1, :], first_ref, x_ref[...], c_ref[...], s_ref[...], outs[:3]
    )
    feed_back(d_x, gain_ref[1:2, :], packed_ref, down_ref, mid_ref, gu_ref, outs[3:])


def back_last_kernel(terms, dmid_ref, dq_ref, x_ref, c_ref, s_ref, gain_ref, first_ref, *refs):
    parts, outs = refs[:terms], refs[terms:]
    d_x = project_back(
        dmid_ref[...], dq_ref, parts, gain_ref[0:1, :], first_ref, x_ref[...], c_ref[...], s_ref[...], outs[:3]
    )
    piece = d_x.shape[0] // 2
    for p in range(2):
        outs[3][p] = pack(d_x[p * piece : (p + 1) * piece]).astype(BF)


def head_kernel(vocab, active_ref, hit_ref, table_ref, *refs):
    pieces, (u_ref, stat_ref), (rows_ref, s_ref) = refs[:-4], refs[-4:-2], refs[-2:]
    n = len(pieces)
    piece = rows_ref.shape[0] // (2 * n)
    rows = 2 * piece
    for k, ref in enumerate(pieces):
        for p in range(2):
            rows_ref[(p * n + k) * piece : (p * n + k + 1) * piece, :] = unpack(ref[p], piece)
    padded = table_ref.shape[0]

    def block(i, _):
        at_row = pl.multiple_of(i * rows, rows)

        @pl.when(active_ref[i] == 0)
        def _():
            u_ref[pl.ds(at_row, rows), :] = jnp.zeros((rows, u_ref.shape[1]), F32)
            stat_ref[i] = jnp.concatenate([jnp.zeros((1, rows), F32), jnp.ones((1, rows), F32), jnp.zeros((1, rows), F32)], 0)

        @pl.when(active_ref[i] != 0)
        def _():
            mine = rows_ref[pl.ds(at_row, rows), :]
            hits = column(hit_ref[i])
            highest = jnp.full((rows, 1), -jnp.inf, F32)
            for at in range(0, padded, VTILE):
                s = dot_t(mine, table_ref[at : at + VTILE, :])
                if at + VTILE > vocab:
                    cols = lax.broadcasted_iota(jnp.int32, (rows, VTILE), 1) + at
                    s = jnp.where(cols < vocab, s, -jnp.inf)
                s_ref[:, at : at + VTILE] = s
                highest = jnp.maximum(highest, jnp.max(s, -1, keepdims=True))
            total = jnp.zeros((rows, 1), F32)
            picked = jnp.zeros((rows, 1), F32)
            u = jnp.zeros((rows, u_ref.shape[1]), F32)
            for at in range(0, padded, VTILE):
                s = s_ref[:, at : at + VTILE]
                e = jnp.exp(s - highest)
                total += jnp.sum(e, -1, keepdims=True)
                hit = lax.broadcasted_iota(jnp.int32, (rows, VTILE), 1) == hits - at
                picked += jnp.sum(jnp.where(hit, s, 0.0), -1, keepdims=True)
                e = jnp.where(hit, 0.0, e).astype(BF)
                u += dot(e, table_ref[at : at + VTILE, :])
            u_ref[pl.ds(at_row, rows), :] = u
            lane = lax.broadcasted_iota(jnp.int32, (rows, 8), 1)
            found = jnp.where(lane == 0, highest, jnp.where(lane == 1, total, picked))
            stat_ref[i] = jnp.transpose(found)[0:3, :]

        return 0

    lax.fori_loop(0, u_ref.shape[0] // rows, block, 0)


def head_forward(active, hits, table, pieces, vocab):
    width = table.shape[1]
    count = pieces[0].size * len(pieces) // width
    rows = count // len(pieces)
    return call(
        functools.partial(head_kernel, vocab),
        "head_forward",
        [active, hits, table] + pieces,
        [shape((count, width), F32), shape((count // rows, 3, rows), F32)],
        [pltpu.VMEM((count, width), BF), pltpu.VMEM((rows, table.shape[0]), F32)],
        scalars=1,
        flops=4 * count * table.size,
        managed=(2,),
    )


def scale_kernel(n, u_ref, scale_ref, *refs):
    stats, (norm_ref, keep_ref, send_ref) = refs[:n], refs[n:]
    blocks = norm_ref.shape[0]
    rows = norm_ref.shape[2]
    piece = rows // 2
    per_half = blocks // 2
    for j in range(blocks):
        half, jj = divmod(j, per_half)
        found = []
        for b in range(n):
            st = stats[b][half * per_half + (jj ^ (b >> 1))]
            if b & 1:
                st = jnp.concatenate([st[:, piece:], st[:, :piece]], 1)
            found.append(st)
        top = found[0][0:1]
        for st in found[1:]:
            top = jnp.maximum(top, st[0:1])
        total = jnp.zeros_like(top)
        for st in found:
            total += st[1:2] * jnp.exp(st[0:1] - top)
        log_norm = top + jnp.log(total)
        picked = jnp.zeros_like(top)
        for st in found:
            picked += st[2:3]
        norm_ref[j] = jnp.concatenate([log_norm, picked], 0)
        factor = column(jnp.exp(found[0][0:1] - log_norm) * scale_ref[j])
        scaled = u_ref[j * rows : (j + 1) * rows, :] * factor
        for k in range(2):
            ref = send_ref if k else keep_ref
            ref[jj, half] = pack(scaled[k * piece : (k + 1) * piece]).astype(ref.dtype)


def head_scale(u, scale, stats):
    n = len(stats)
    count, width = u.shape
    piece = count // (2 * n)
    block = (n // 2, 2, piece * width // 128, 128)
    return call(
        functools.partial(scale_kernel, n),
        "head_scale",
        [u, scale] + stats,
        [shape((scale.shape[0], 2, scale.shape[2]), F32), shape(block, F32), shape(block, BF)],
        flops=2 * u.size,
    )


def head_grad_kernel(first, step, active_ref, stat_ref, hit_ref, table_ref, packed_ref, *refs):
    old_ref = None if first else refs[0]
    out_ref, grad_ref, rows_ref, sem = refs[-4:]
    turn = pl.program_id(0)
    _, n, _, packed_rows, _ = packed_ref.shape
    blocks = stat_ref.shape[1] // step
    piece = rows_ref.shape[0] // (2 * n)
    rows = 2 * piece * step
    vocab = grad_ref.shape[0]
    tile = vocab // 5

    @pl.when(turn == 0)
    def _():
        if first:
            grad_ref[...] = jnp.zeros_like(grad_ref)
        else:
            copy = pltpu.make_async_copy(old_ref, grad_ref, sem)
            copy.start()
            copy.wait()

    for b in range(n):
        for p in range(2):
            rows_ref[(p * n + b) * piece : (p * n + b + 1) * piece, :] = unpack(packed_ref[0, b, p], piece)

    def block(i, _):
        wanted = active_ref[turn, step * i]
        for k in range(1, step):
            wanted = wanted + active_ref[turn, step * i + k]

        @pl.when(wanted != 0)
        def _():
            mine = rows_ref[pl.ds(pl.multiple_of(i * rows, rows), rows), :]
            stat = jnp.concatenate([stat_ref[0, step * i + k] for k in range(step)], 1)
            log_norm, scale = stat[0:1], stat[1:2]
            hits = jnp.concatenate([hit_ref[0, step * i + k] for k in range(step)], 1)
            for at in range(0, vocab, tile):
                s = dot_t(table_ref[at : at + tile, :], mine)
                d = jnp.exp(s - log_norm) * scale
                index = lax.broadcasted_iota(jnp.int32, (tile, rows), 0)
                d = jnp.where(index == hits - at, d - scale, d).astype(BF)
                grad_ref[at : at + tile, :] += dot(d, mine)

        return 0

    lax.fori_loop(0, blocks, block, 0)

    @pl.when(turn == pl.num_programs(0) - 1)
    def _():
        back = pltpu.make_async_copy(grad_ref, out_ref, sem)
        back.start()
        back.wait()


def head_grad(active, stats, hits, table, packed, vocab, so_far, begin, end):
    width = table.shape[1]
    count = packed[0].size // width
    first = so_far is None
    part = slice(begin, end)
    inputs = [active[part], stats, hits, table, packed] + ([] if first else [so_far])
    anywhere = pl.BlockSpec(memory_space=pl.ANY)

    def sequence(v):
        dims = len(v.shape)
        return pl.BlockSpec((1,) + v.shape[1:], lambda i: (begin + i,) + (0,) * (dims - 1))

    step = 2 if stats.shape[1] % 4 == 0 else 1
    return pl.pallas_call(
        functools.partial(head_grad_kernel, first, step),
        grid=(end - begin,),
        in_specs=[
            pl.BlockSpec(memory_space=pltpu.SMEM),
            sequence(stats),
            sequence(hits),
            pl.BlockSpec(table.shape, lambda i: (0, 0), pipeline_mode=pl.Buffered(1)),
            sequence(packed),
        ] + ([] if first else [anywhere]),
        out_specs=anywhere,
        out_shape=shape((vocab, width), F32),
        scratch_shapes=[
            pltpu.VMEM((vocab, width), F32),
            pltpu.VMEM((count, width), BF),
            pltpu.SemaphoreType.DMA,
        ],
        compiler_params=pltpu.CompilerParams(vmem_limit_bytes=40 * MIB),
        cost_estimate=pl.CostEstimate(
            flops=3 * count * table.size * (end - begin), bytes_accessed=8 * vocab * width, transcendentals=0
        ),
        input_output_aliases={} if first else {5: 0},
        name="head_grad",
    )(*inputs)


def add_rows_kernel(bits, count_ref, key_ref, packed_ref, grad_ref, out_ref, square_ref, wide_ref, sem):
    turn = pl.program_id(0)
    _, n, _, _, _ = packed_ref.shape
    piece = wide_ref.shape[0] // (2 * n)

    @pl.when(turn == 0)
    def _():
        pltpu.make_async_copy(grad_ref, out_ref, sem).start()

    for b in range(n):
        for p in range(2):
            wide_ref[(p * n + b) * piece : (p * n + b + 1) * piece, :] = unpack(packed_ref[0, b, p].astype(F32), piece)

    @pl.when(turn == 0)
    def _():
        pltpu.make_async_copy(grad_ref, out_ref, sem).wait()

    def add(i):
        key = key_ref[turn, i]
        row = key >> bits
        at = key & ((1 << bits) - 1)
        out_ref[pl.ds(row, 1), :] += wide_ref[pl.ds(at, 1), :]

    def add_some(i, _):
        for k in range(8):
            add(8 * i + k)
        return 0

    def add_one(i, _):
        add(i)
        return 0

    count = count_ref[turn]
    lax.fori_loop(0, count >> 3, add_some, 0)
    lax.fori_loop((count >> 3) << 3, count, add_one, 0)

    @pl.when(turn == pl.num_programs(0) - 1)
    def _():
        tile = 80
        width = out_ref.shape[1]

        def squares(i, total):
            v = out_ref[pl.ds(pl.multiple_of(i * tile, 8), tile), :]
            return total + jnp.sum((v * v).reshape(tile // 8, 8, width), 0)

        square_ref[...] = lax.fori_loop(0, out_ref.shape[0] // tile, squares, jnp.zeros((8, width), F32))


def add_rows(counts, keys, packed, grad, bits):
    vocab, width = grad.shape
    count = packed[0].size // width
    return pl.pallas_call(
        functools.partial(add_rows_kernel, bits),
        grid=(packed.shape[0],),
        in_specs=[
            pl.BlockSpec(memory_space=pltpu.SMEM),
            pl.BlockSpec(memory_space=pltpu.SMEM),
            pl.BlockSpec((1,) + packed.shape[1:], lambda i: (i, 0, 0, 0, 0)),
            pl.BlockSpec(memory_space=pl.ANY),
        ],
        out_specs=[
            pl.BlockSpec(grad.shape, lambda i: (0, 0), pipeline_mode=pl.Buffered(1)),
            pl.BlockSpec((8, width), lambda i: (0, 0)),
        ],
        out_shape=[shape(grad.shape, F32), shape((8, width), F32)],
        scratch_shapes=[pltpu.VMEM((count, width), F32), pltpu.SemaphoreType.DMA],
        compiler_params=pltpu.CompilerParams(vmem_limit_bytes=32 * MIB),
        cost_estimate=pl.CostEstimate(flops=2 * grad.size, bytes_accessed=8 * grad.size, transcendentals=0),
        name="add_rows",
    )(counts, keys, packed, grad)


def adam_update(weight, first, second, grad, decay):
    next_first = BETA_ONE * first + (1.0 - BETA_ONE) * grad
    next_second = BETA_TWO * second + (1.0 - BETA_TWO) * grad * grad
    corrected = next_first / (1.0 - BETA_ONE**STEP_NO)
    scaled = jnp.sqrt(next_second / (1.0 - BETA_TWO**STEP_NO)) + ADAM_EPSILON
    return (weight - RATE * (corrected / scaled + decay * weight), next_first, next_second)


def deal_blocks(value_ref, rows, columns, at_row, me, keep_ref, send_ref):
    for b in range(value_ref.shape[0] // rows):
        r = me ^ b

        def put(ref):
            for k in range(columns // 128):
                ref[r >> 1, at_row + k * rows : at_row + (k + 1) * rows, :] = value_ref[
                    b * rows : (b + 1) * rows, k * 128 : (k + 1) * 128
                ]

        pl.when((r & 1) == 0)(functools.partial(put, keep_ref))
        pl.when((r & 1) == 1)(functools.partial(put, send_ref))
    return at_row + rows * (columns // 128)


def clear_end(at_row, *refs):
    for ref in refs:
        if ref.shape[1] > at_row:
            ref[:, at_row:, :] = jnp.zeros((ref.shape[0], ref.shape[1] - at_row, ref.shape[2]), F32)


def undeal(ref, at_row, rows, columns):
    count = -(-columns // 128)
    parts = [ref[at_row + k * rows : at_row + (k + 1) * rows, :] for k in range(count)]
    return jnp.concatenate(parts, 1)[:, :columns]


def early_grads_kernel(
    n, me_ref, nf0, nf1, dgu0, dgu1, act0, act1, db0, db1, o0, o1, da0, da1, keep_ref, send_ref, wide, tall
):
    me = me_ref[0]
    width = nf0.shape[1]
    padded = tall.shape[1]

    def product(l0, l1, r0, r1):
        return dot_w(l0[...], r0) + dot_w(l1[...], r1)

    at = 0
    for part in (slice(0, FF), slice(FF, 2 * FF)):
        wide[...] = product(nf0, nf1, dgu0[:, part], dgu1[:, part])
        at = deal_blocks(wide, width // n, FF, at, me, keep_ref, send_ref)
    tall[:, width:] = jnp.zeros((FF, padded - width), F32)
    tall[:, :width] = product(act0, act1, db0[...], db1[...])
    at = deal_blocks(tall, FF // n, padded, at, me, keep_ref, send_ref)
    tall[0:width, :width] = product(o0, o1, da0[...], da1[...])
    at = deal_blocks(tall.at[0:width], width // n, padded, at, me, keep_ref, send_ref)
    clear_end(at, keep_ref, send_ref)


def late_grads_kernel(n, me_ref, n0, n1, kv0, kv1, q0, q1, at0, at1, ff0, ff1, fin, keep_ref, send_ref, wide):
    me = me_ref[0]
    width = n0.shape[1]
    kv_width = kv0.shape[1]
    gains = jnp.concatenate(
        [at0[...] + at1[...], ff0[...] + ff1[...], fin[...], jnp.zeros((5, width), F32)], 0
    )
    wide[:, 0:kv_width] = dot_w(n0[...], kv0[...]) + dot_w(n1[...], kv1[...])
    wide[:, kv_width : kv_width + 128] = jnp.concatenate(
        [jnp.transpose(gains), jnp.zeros((width, 120), F32)], 1
    )
    at = deal_blocks(wide, width // n, kv_width + 128, 0, me, keep_ref, send_ref)
    wide[:, width:] = jnp.zeros((width, wide.shape[1] - width), F32)
    wide[:, :width] = dot_w(n0[...], q0[...]) + dot_w(n1[...], q1[...])
    at = deal_blocks(wide, width // n, wide.shape[1], at, me, keep_ref, send_ref)
    clear_end(at, keep_ref, send_ref)


def split_kernel(terms, place_ref, *refs):
    outs, (total_ref,) = refs[terms:-1], refs[-1:]
    total = refs[0][...].astype(F32)
    for ref in refs[1:terms]:
        total += ref[...].astype(F32)
    total_ref[...] = total
    share = outs[0].shape[0]
    for r, ref in enumerate(outs):
        at = pl.multiple_of((place_ref[0] ^ r) * share, 16)
        ref[...] = total_ref[pl.ds(at, share), :].astype(ref.dtype)


def add_kernel(*refs):
    total = refs[0][...].astype(F32)
    for ref in refs[1:-1]:
        total += ref[...].astype(F32)
    refs[-1][...] = total.astype(refs[-1].dtype)


def join_kernel(place_ref, *refs):
    out_ref = refs[-1]
    share = refs[0].shape[0]
    for r, ref in enumerate(refs[:-1]):
        at = pl.multiple_of((place_ref[0] ^ r) * share, 16)
        out_ref[pl.ds(at, share), :] = ref[...].astype(F32)


def sum_over(terms, place, axis, wire, until, finally_until):
    n = lax.axis_size(axis)
    rows, columns = terms[0].shape
    share = rows // n
    parts = call(
        functools.partial(split_kernel, len(terms)), "split", [place] + terms,
        [shape((share, columns), F32)] + [shape((share, columns), wire)] * (n - 1),
        [pltpu.VMEM((rows, columns), F32)], scalars=1, limit=24,
    )
    got = all_after([swap(v, axis, r) for r, v in enumerate(parts) if r], until())
    got = [parts[0]] + got
    (mine,) = call(add_kernel, "add_up", got, [shape((share, columns), F32)], limit=24)
    everything = [mine] + all_after(everyone(mine, axis)[1:], finally_until())
    return call(
        join_kernel, "join", [place] + everything, [shape((rows, columns), F32)], scalars=1, limit=24
    )[0]


def squares_kernel(*refs):
    out_ref = refs[-1]
    total = jnp.zeros((1, 1), F32)
    for ref in refs[:-1]:
        v = ref[...]
        v = v if ref is refs[0] else v * v
        total += jnp.sum(jnp.sum(v, 0, keepdims=True), 1, keepdims=True)
    out_ref[...] = total


def small_adam_kernel(factor_ref, early_ref, late_ref, *refs):
    states, results = refs[:18], refs[18:]
    factor = factor_ref[0]

    def update(k, grad, part=slice(None), decay=DECAY):
        olds = [states[3 * k + i][:, part] for i in range(3)]
        for i, value in enumerate(adam_update(*olds, grad * factor, decay)):
            results[3 * k + i][:, part] = value

    here, width = states[0].shape
    kv_width = states[3].shape[1]
    at = kv_width // 128 * here
    update(1, undeal(late_ref, 0, here, kv_width))
    update(5, jnp.transpose(late_ref[at : at + here, :])[0:3], decay=0.0)
    update(0, undeal(late_ref, at + here, here, width))
    at = 0
    for part in (slice(0, FF), slice(FF, 2 * FF)):
        update(3, undeal(early_ref, at, here, FF), part)
        at += FF // 128 * here
    down = states[12].shape[0]
    update(4, undeal(early_ref, at, down, width))
    update(2, undeal(early_ref, at + -(-width // 128) * down, here, width))


def table_adam_kernel(factor_ref, grad_ref, w_ref, m_ref, v_ref, new_w_ref, new_m_ref, new_v_ref):
    grad = jnp.transpose(grad_ref[...]) * factor_ref[0]
    new_w_ref[...], new_m_ref[...], new_v_ref[...] = adam_update(
        w_ref[...], m_ref[...], v_ref[...], grad, DECAY
    )


def table_adam(factor, grad, weight, first, second):
    vocab, width = grad.shape
    tile = 512
    spec = pl.BlockSpec((width, tile), lambda i: (0, i))
    outs = pl.pallas_call(
        table_adam_kernel,
        grid=(pl.cdiv(vocab, tile),),
        in_specs=[
            pl.BlockSpec(memory_space=pltpu.SMEM),
            pl.BlockSpec((tile, width), lambda i: (i, 0)),
            spec,
            spec,
            spec,
        ],
        out_specs=[spec] * 3,
        out_shape=[shape((width, vocab), F32)] * 3,
        compiler_params=pltpu.CompilerParams(vmem_limit_bytes=40 * MIB),
        cost_estimate=pl.CostEstimate(flops=20 * vocab * width, bytes_accessed=28 * vocab * width, transcendentals=0),
        name="table_adam",
    )(factor.reshape(1), grad, weight.T, first.T, second.T)
    return tuple(o.T for o in outs)


def body(*arguments):
    token_ids, response_mask = arguments[0], arguments[1]
    masters, firsts, seconds = arguments[4:11], arguments[11:18], arguments[18:25]
    embed_table, w_query, w_kv, w_out, w_gate_up, w_down, gains = masters
    groups = lax.axis_size("seq")
    batch = lax.axis_size("dp")
    me = lax.axis_index("seq")
    local_len = token_ids.shape[1]
    seq_len = groups * local_len
    piece = local_len // 2
    pieces = 2 * groups
    vocab, width = embed_table.shape
    base = me * vocab
    rows = local_len

    here = w_query.shape[0]
    early_pack = jnp.concatenate(
        [
            w_kv.astype(BF),
            w_query.astype(BF),
            gains.T.astype(BF),
            jnp.zeros((here, EARLY - GAIN_AT - 3), BF),
        ],
        1,
    )
    late_pack = jnp.concatenate([w_gate_up.astype(BF), w_out.astype(BF)], 1)
    first_pack = lax.all_gather(early_pack, "seq", axis=0, tiled=True)
    packed_full = lax.all_gather(late_pack, "seq", axis=0, tiled=True)
    down_full = lax.all_gather(w_down.astype(BF), "seq", axis=0, tiled=True)
    gain_rows = first_pack[:, GAIN_AT : GAIN_AT + 3].T.astype(F32)
    padded = (vocab + VTILE - 1) // VTILE * VTILE
    table = low_table(embed_table, padded)

    meta = jnp.concatenate([token_ids, response_mask], 0)
    ordered = lax.all_gather(meta, "seq", axis=1, tiled=True)
    who = jnp.arange(groups) ^ me

    order = jnp.concatenate([who, pieces - 1 - who])
    pick = order[:, None] == jnp.arange(pieces)[None, :]

    def met(values):
        cut = values.reshape(values.shape[0], 1, pieces, piece)
        chosen = jnp.sum(jnp.where(pick[None, :, :, None], cut, jnp.zeros((), values.dtype)), 2)
        return chosen.reshape(values.shape[0], pieces * piece)

    extra = 16
    ids_row = ordered[0]
    follow = jnp.concatenate([ids_row, jnp.zeros((piece,), jnp.int32)]).reshape(pieces + 1, piece)
    ids_wide = jnp.concatenate([ids_row.reshape(pieces, piece), follow[1:, :extra]], 1)
    evens = jnp.arange(0, groups, 2) ^ me
    odds = evens ^ 1
    wanted = jnp.stack(
        [jnp.stack([evens, pieces - 1 - evens], 1), jnp.stack([odds, pieces - 1 - odds], 1)], 0
    ).reshape(-1)
    ids_wide = jnp.sum(
        jnp.where((wanted[:, None] == jnp.arange(pieces)[None, :])[:, :, None], ids_wide[None], 0), 1
    )
    found = lookup((ids_wide - base).reshape(-1), table, 4 * (piece + extra))
    found = found.reshape(2, groups // 2, 2, piece + extra, width)
    terms = scatter_all(found[0], found[1], "seq", BF, BF)
    found = sum(terms[1:], terms[0])
    hidden = jnp.concatenate([found[0, :piece], found[1, :piece]], 0).astype(F32)
    target_rows = jnp.concatenate([found[0, 1 : piece + 1], found[1, 1 : piece + 1]], 0)

    place = lax.axis_index("dp")
    which = jnp.arange(batch) ^ place
    sequence_spots = which[None, :] == jnp.arange(batch)[:, None]

    def by_sequence(values):
        stacked = jnp.stack(values, 0)
        spots = sequence_spots.reshape((batch, batch) + (1,) * (stacked.ndim - 1))
        return jnp.sum(jnp.where(spots, stacked[None], jnp.zeros((), stacked.dtype)), 1)

    def paired(values):
        cut = values.reshape(values.shape[0], pieces, piece)
        return jnp.concatenate([cut[:, :groups], cut[:, groups:][:, ::-1]], 1)

    all_meta = by_sequence(everyone(ordered, "dp"))
    ids_all, mask_all = all_meta[:, 0], all_meta[:, 1]
    last = (jnp.arange(seq_len) < seq_len - 1).astype(F32)[None]
    valid_all = mask_all.astype(F32) * last
    counted = jnp.sum(valid_all)
    targets_all = jnp.concatenate([ids_all[:, 1:], jnp.zeros((batch, 1), jnp.int32)], 1)
    pair_valid = paired(valid_all)
    blocks = seq_len // rows
    half = blocks // 2
    own_valid = met(ordered[1:2].astype(F32) * last).reshape(blocks, 1, rows)
    own_target = jnp.concatenate([ordered[0:1, 1:], jnp.zeros((1, 1), jnp.int32)], 1)
    own_target = met(own_target) - base
    own_target = jnp.where((own_target >= 0) & (own_target < vocab), own_target, -1).reshape(blocks, 1, rows)
    own_scale = own_valid / counted
    own_active = (jnp.max(own_valid.reshape(blocks, rows), -1) > 0).astype(jnp.int32)
    pair_targets = (paired(targets_all) - base).reshape(batch, blocks, 1, rows)
    pair_active = (jnp.max(pair_valid.reshape(batch, blocks, rows), -1) > 0).astype(jnp.int32)

    own_pos = jnp.concatenate(
        [order[0] * piece + jnp.arange(piece), order[groups] * piece + jnp.arange(piece)]
    )
    inverse = 10000.0 ** (-jnp.arange(HALF).astype(F32) * 2.0 / HD)
    phases = own_pos.astype(F32)[:, None] * inverse[None, :]
    cosine, sine_wave = after(jnp.cos(phases), pair_valid, pair_targets, pair_active, own_target, own_scale), jnp.sin(phases)
    me_one = me.reshape(1).astype(jnp.int32)

    layer_flops = 2 * rows * width * (2 * H * HD + 2 * KVH * HD + 3 * FF)
    x0 = hidden
    packed_rows = piece * width // 128
    normed0, q0, kv = call(
        pre_kernel, "pre", [x0, gain_rows, first_pack, cosine, sine_wave], projected_shapes(rows, width),
        flops=layer_flops // 4, managed=(2,),
    )
    o0, lse0, kv0 = attend(me_one, q0, gather_all(kv, "seq"))
    mid0, nf0, gu0, act0, x1, normed1, q1, kv = call(
        mid_kernel, "mid", [x0, o0, gain_rows, first_pack, packed_full, down_full, cosine, sine_wave],
        fed_shapes(rows, width) + projected_shapes(rows, width), flops=layer_flops, managed=(3, 4, 5),
    )
    o1, lse1, kv1 = attend(me_one, q1, gather_all(kv, "seq"))
    mid1, nf1, gu1, act1, x2, final = call(
        post_kernel, "post", [x1, o1, gain_rows, packed_full, down_full],
        fed_shapes(rows, width) + [shape((2, packed_rows, 128), BF)], flops=layer_flops, managed=(3, 4),
    )
    own_rows = gather_all(final, "seq")
    rows_all = lax.all_gather(after(final, *own_rows[1:]), ("dp", "seq"))
    rows_all = rows_all.reshape(batch, groups, 2, packed_rows, 128)

    u, stats = head_forward(own_active, own_target, table, own_rows, vocab)
    norms, keep, send = head_scale(u, own_scale, everyone(stats, "seq"))
    terms = scatter_all(keep, send, "seq", BF)

    def mine(row):
        return jnp.concatenate([row[0, :piece], row[half, :piece]])

    at_target = (jnp.exp(mine(norms[:, 1]) - mine(norms[:, 0])) - 1.0) * mine(own_scale[:, 0])
    at_target = at_target.astype(BF).astype(F32).reshape(1, rows)

    outs = call(
        functools.partial(back_first_kernel, len(terms)), "back_first",
        [x2, target_rows, at_target, gain_rows, packed_full, down_full, mid1, gu1] + terms,
        [shape((1, width), F32)] + fed_back_shapes(rows, width), flops=2 * layer_flops, managed=(4, 5),
    )
    gain_final, db1, dgu1, dmid1, da1, do1, gain_ffn1 = outs
    met_norms = jnp.swapaxes(after(norms, do1), 0, 1).reshape(2, 2, groups, piece)
    spots = (who[None, :] == jnp.arange(groups)[:, None]).astype(F32)
    piece_norms = jnp.sum(spots[None, None, :, :, None] * met_norms[:, :, None], 3).reshape(2, pieces, piece)
    all_norms = by_sequence(everyone(piece_norms, "dp"))
    loss = jnp.sum(jnp.where(pair_valid > 0, all_norms[:, 0] - all_norms[:, 1], 0.0)) / counted
    pair_stats = jnp.stack(
        [all_norms[:, 0].reshape(batch, blocks, rows), (pair_valid / counted).reshape(batch, blocks, rows)], 2
    )
    dq1, keep, send = attend_back(me_one, q1, do1, lse1, kv1, groups)
    place_one = place.reshape(1).astype(jnp.int32)
    terms = scatter_all(keep, send, "seq", BF)
    outs = call(
        functools.partial(back_mid_kernel, len(terms)), "back_mid",
        [dmid1, dq1, x1, cosine, sine_wave, gain_rows, first_pack, packed_full, down_full, mid0, gu0] + terms,
        [shape((rows, H * HD), BF), shape((rows, 2 * KVH * HD), BF), shape((1, width), F32)] + fed_back_shapes(rows, width),
        flops=2 * layer_flops, managed=(6, 7, 8),
    )
    dq_raw1, dkv_raw1, gain_attn1, db0, dgu0, dmid0, da0, do0, gain_ffn0 = outs
    dq0, keep, send = attend_back(me_one, q0, do0, lse0, kv0, groups)
    wide_columns = -(-width // 128) * 128

    def padded_rows(count):
        return -(-count // (16 * batch)) * (16 * batch)

    early_rows = padded_rows((2 * here * FF + w_down.shape[0] * wide_columns + here * wide_columns) // 128)
    early = []

    def start_early_grads():
        early.extend(
            call(
                functools.partial(early_grads_kernel, groups), "early_grads",
                [me_one, nf0, nf1, dgu0, dgu1, act0, act1, after(db0, dq0), db1, o0, o1, da0, da1],
                [shape((groups // 2, early_rows, 128), F32)] * 2,
                [pltpu.VMEM((width, FF), F32), pltpu.VMEM((FF, wide_columns), F32)],
                scalars=1, flops=layer_flops * 2, limit=56,
            )
        )
        return early[1]

    terms = scatter_all(keep, send, "seq", BF, between=start_early_grads)
    outs = call(
        functools.partial(back_last_kernel, len(terms)), "back_last",
        [dmid0, dq0, x0, cosine, sine_wave, gain_rows, first_pack] + terms,
        [shape((rows, H * HD), BF), shape((rows, 2 * KVH * HD), BF), shape((1, width), F32), shape((2, packed_rows, 128), BF)],
        flops=layer_flops // 2, managed=(6,),
    )
    dq_raw0, dkv_raw0, gain_attn0, d_low = outs
    d_all = lax.all_gather(d_low, ("dp", "seq")).reshape(batch, groups, 2, packed_rows, 128)

    late_rows = padded_rows(here * (w_kv.shape[1] + 128 + wide_columns) // 128)
    late = call(
        functools.partial(late_grads_kernel, groups), "late_grads",
        [me_one, normed0, normed1, dkv_raw0, dkv_raw1, dq_raw0, dq_raw1, gain_attn0, gain_attn1, gain_ffn0, gain_ffn1, gain_final],
        [shape((groups // 2, late_rows, 128), F32)] * 2,
        [pltpu.VMEM((width, wide_columns), F32)],
        scalars=1, flops=layer_flops // 2,
    )
    ends = [1, 2, batch]
    done = []

    def head_step(k):
        while len(done) <= k:
            begin = ends[len(done) - 1] if done else 0
            packed = rows_all if done else after(rows_all, late[1])
            done.append(
                head_grad(
                    pair_active, pair_stats, pair_targets, table, packed, vocab,
                    done[-1] if done else None, begin, ends[len(done)],
                )
            )
        return done[k]

    step = [functools.partial(head_step, k) for k in range(3)]
    early_terms = scatter_all(early[0], early[1], "seq", BF, between=lambda: late[1], until=step[0])
    late_terms = scatter_all(late[0], late[1], "seq", F32, between=step[0], until=step[1])
    bits = (seq_len - 1).bit_length()
    met_ids = paired(ids_all).reshape(batch, seq_len) - base
    inside = (met_ids >= 0) & (met_ids < vocab)
    keys = jnp.where(inside, met_ids * (1 << bits) + jnp.arange(seq_len)[None], 2147483647)
    keys = jnp.sort(keys, -1)
    counts = jnp.sum(inside.astype(jnp.int32), -1)
    early_sum = sum_over(early_terms, place_one, "dp", BF, step[1], step[2])
    grad_table, table_squares = add_rows(counts, keys, d_all, head_step(2), bits)
    late_sum = sum_over(late_terms, place_one, "dp", F32, step[2], lambda: table_squares)

    small = [early_sum, late_sum]
    (squares,) = call(squares_kernel, "squares", [table_squares] + small, [shape((1, 1), F32)], limit=24)
    squares = tree([squares] + [swap(squares, "seq", r) for r in range(2, groups, 2)])
    grad_norm = jnp.sqrt((squares + swap(squares, "seq", 1))[0, 0])
    factor = CLIP / jnp.maximum(grad_norm, CLIP)
    states = [v for i in range(1, 7) for v in (masters[i], firsts[i], seconds[i])]
    news = call(
        small_adam_kernel, "small_adam",
        [factor.reshape(1)] + small + states, [shape(v.shape, F32) for v in states], scalars=1, limit=48,
        managed=tuple(range(1, 3 + len(states))),
    )
    table_news = table_adam(factor, grad_table, masters[0], firsts[0], seconds[0])
    results = []
    for k in range(3):
        results += [table_news[k]] + [news[3 * i + k] for i in range(6)]
    return tuple(results) + (loss, grad_norm)


def solution(mesh):
    rows, cols, whole = P("seq", None), P(None, "seq"), P()
    group = (rows,) * 6 + (cols,)
    return jax.shard_map(
        body,
        mesh=mesh,
        in_specs=(P("dp", "seq"), P("dp", "seq"), whole, whole) + group * 3,
        out_specs=group * 3 + (whole, whole),
        check_vma=False,
    )
```

```python
import functools

import jax
import jax.numpy as jnp
from jax import lax
from jax.experimental import pallas as pl
from jax.experimental.pallas import tpu as pltpu
from jax.sharding import PartitionSpec as P

H = 9
KVH = 3
GROUP = H // KVH
HD = 64
HALF = HD // 2
FF = 1536
LAYERS = 2
STEP_NO = 10
EPSILON = 1e-05
CLIP = 0.01
RATE = 0.1
BETA_ONE = 0.9
BETA_TWO = 0.95
ADAM_EPSILON = 1e-08
DECAY = 0.1
MASKED = -1000000000.0
BF = jnp.bfloat16
F32 = jnp.float32
MIB = 1024 * 1024

KV_AT, Q_AT, GAIN_AT, EARLY = 0, 384, 960, 1024
GU_AT, OUT_AT = 0, 3072
CHUNK = 512
VTILE = 1024


def swap(x, axis, bit):
    n = lax.axis_size(axis)
    return lax.ppermute(x, axis, [(i, i ^ bit) for i in range(n)])


def gather_all(x, axis):
    n = lax.axis_size(axis)
    held = {0: x}
    for r in range(2, n, 2):
        held[r] = swap(x, axis, r)
    for r in range(0, n, 2):
        held[r + 1] = swap(held[r], axis, 1)
    return [held[r] for r in range(n)]


def merge_kernel(keep_ref, got_ref, own_ref, *others):
    for k in range(keep_ref.shape[0]):
        ref = others[k - 1] if k else own_ref
        ref[...] = (keep_ref[k].astype(F32) + got_ref[k].astype(F32)).astype(ref.dtype)


def scatter_all(keep, send, axis, wire, own=F32, between=None, until=None):
    got = swap(send, axis, 1)
    if between is not None:
        got = after(got, between())
    block = keep.shape[1:]
    outs = call(
        merge_kernel, "merge", [keep, got],
        [shape(block, own)] + [shape(block, wire)] * (keep.shape[0] - 1), limit=32,
    )
    arrived = [swap(x, axis, 2 * k) for k, x in enumerate(outs) if k]
    if until is not None:
        arrived = all_after(arrived, until())
    return [outs[0]] + arrived


def everyone(x, axis):
    return [x] + [swap(x, axis, r) for r in range(1, lax.axis_size(axis))]


def tree(terms):
    while len(terms) > 1:
        terms = [a + b for a, b in zip(terms[::2], terms[1::2])]
    return terms[0]


def after(x, *needs):
    return lax.optimization_barrier((x,) + needs)[0]


def all_after(xs, *needs):
    return list(lax.optimization_barrier(tuple(xs) + needs)[: len(xs)])


def dot(a, b):
    return jnp.dot(a, b, preferred_element_type=F32)


def dot_t(a, b):
    return lax.dot_general(a, b, (((1,), (1,)), ((), ())), preferred_element_type=F32)


def dot_w(a, b):
    return lax.dot_general(a, b, (((0,), (0,)), ((), ())), preferred_element_type=F32)


def inverse_rms(values):
    return lax.rsqrt(jnp.mean(values * values, -1, keepdims=True) + EPSILON)


def rms_back(values, gain_row, d_out):
    r = inverse_rms(values)
    scaled = gain_row * d_out
    d_values = r * scaled - values * (r * r * r * jnp.mean(values * scaled, -1, keepdims=True))
    return d_values, jnp.sum(d_out * values * r, 0, keepdims=True)


def pack(x):
    p, width = x.shape
    full = width // 128 * 128
    last = x[:, full:]
    return jnp.concatenate(
        [x[:, at : at + 128] for at in range(0, full, 128)] + [jnp.concatenate([last[: p // 2], last[p // 2 :]], 1)], 0
    )


def unpack(x, p):
    full = x.shape[0] // p
    last = x[full * p :]
    side = last.shape[1] // 2
    return jnp.concatenate(
        [x[k * p : (k + 1) * p] for k in range(full)] + [jnp.concatenate([last[:, :side], last[:, side:]], 0)], 1
    )


def column(row):
    return jnp.transpose(jnp.broadcast_to(row, (8, row.shape[1])))[:, 0:1]


def call(kernel, name, inputs, outputs, scratch=(), scalars=0, limit=26, flops=0):
    smem = pl.BlockSpec(memory_space=pltpu.SMEM)

    def whole(v):
        dims = len(v.shape)
        return pl.BlockSpec(v.shape, lambda i: (0,) * dims, pipeline_mode=pl.Buffered(1))

    moved = sum(v.size * v.dtype.itemsize for v in list(inputs) + list(outputs))
    return pl.pallas_call(
        kernel,
        grid=(1,),
        in_specs=[smem if k < scalars else whole(v) for k, v in enumerate(inputs)],
        out_specs=[whole(v) for v in outputs],
        out_shape=list(outputs),
        scratch_shapes=list(scratch),
        compiler_params=pltpu.CompilerParams(vmem_limit_bytes=limit * MIB),
        cost_estimate=pl.CostEstimate(flops=flops, bytes_accessed=moved, transcendentals=0),
        name=name,
    )(*inputs)


def shape(dims, dtype):
    return jax.ShapeDtypeStruct(tuple(dims), dtype)


def table_kernel(vocab, wide_ref, out_ref):
    tile = out_ref.shape[0]
    at = pl.program_id(0) * tile
    x = wide_ref[...]
    cols = lax.broadcasted_iota(jnp.int32, x.shape, 1) + at
    out_ref[...] = jnp.transpose(jnp.where(cols < vocab, x, 0.0)).astype(BF)


def low_table(embed_table, padded):
    vocab, width = embed_table.shape
    tile = 512
    return pl.pallas_call(
        functools.partial(table_kernel, vocab),
        grid=(padded // tile,),
        in_specs=[pl.BlockSpec((width, tile), lambda i: (0, i))],
        out_specs=pl.BlockSpec((tile, width), lambda i: (i, 0)),
        out_shape=shape((padded, width), BF),
        compiler_params=pltpu.CompilerParams(vmem_limit_bytes=24 * MIB),
        cost_estimate=pl.CostEstimate(flops=0, bytes_accessed=6 * padded * width, transcendentals=0),
        name="low_table",
    )(embed_table.T)


def spread_kernel(gathered_ref, packed_ref, down_ref):
    groups, _, columns = packed_ref.shape
    width = down_ref.shape[1]
    third = down_ref.shape[0] // (3 * groups)
    for b in range(groups):
        packed_ref[b] = gathered_ref[b, :, :columns]
        for k in range(3):
            at = columns + 64 + k * width
            down_ref[(3 * b + k) * third : (3 * b + k + 1) * third, :] = gathered_ref[b, :third, at : at + width]


def lookup_kernel(ids_ref, table_ref, out_ref):
    rows = out_ref.shape[0]
    total = jnp.zeros(out_ref.shape, F32)
    for at in range(0, table_ref.shape[0], VTILE):
        cols = lax.broadcasted_iota(jnp.int32, (rows, VTILE), 1) + at
        hot = jnp.where(cols == ids_ref[...], 1.0, 0.0).astype(BF)
        total += dot(hot, table_ref[at : at + VTILE, :])
    out_ref[...] = total.astype(BF)


def lookup(ids, table, block):
    count = ids.shape[0]
    width = table.shape[1]
    return pl.pallas_call(
        lookup_kernel,
        grid=(count // block,),
        in_specs=[
            pl.BlockSpec((block, 1), lambda i: (i, 0)),
            pl.BlockSpec(table.shape, lambda i: (0, 0)),
        ],
        out_specs=pl.BlockSpec((block, width), lambda i: (i, 0)),
        out_shape=shape((count, width), BF),
        compiler_params=pltpu.CompilerParams(vmem_limit_bytes=40 * MIB),
        cost_estimate=pl.CostEstimate(
            flops=2 * count * table.size, bytes_accessed=2 * table.size, transcendentals=0
        ),
        name="lookup",
    )(ids.reshape(count, 1), table)


def project(x, gain, packed_ref, c, s, normed_ref, q_ref, kv_ref):
    piece = x.shape[0] // 2
    normed = (x * inverse_rms(x) * gain).astype(BF)
    normed_ref[...] = normed
    q = dot(normed, packed_ref[:, Q_AT : Q_AT + H * HD])
    kv = dot(normed, packed_ref[:, KV_AT : KV_AT + 2 * KVH * HD])
    nothing = jnp.zeros((x.shape[0], HD), F32)
    for h in range(H):
        g, j = divmod(h, GROUP)
        a = q[:, h * HD : h * HD + HALF]
        b = q[:, h * HD + HALF : (h + 1) * HD]
        turned = jnp.concatenate([(a * c - b * s) * 0.125, (a * s + b * c) * 0.125, nothing], 1).astype(BF)
        for p in range(2):
            q_ref[g, p, j * piece : (j + 1) * piece, :] = turned[p * piece : (p + 1) * piece]
    for g in range(KVH):
        a = kv[:, g * HD : g * HD + HALF]
        b = kv[:, g * HD + HALF : (g + 1) * HD]
        v = kv[:, (KVH + g) * HD : (KVH + g + 1) * HD]
        turned = jnp.concatenate([a * c - b * s, a * s + b * c, v], 1).astype(BF)
        kv_ref[0, g] = turned[:piece]
        kv_ref[1, g] = turned[piece:]


def feed(x, o_ref, gain, packed_ref, down_ref, mid_ref, nf_ref, gu_ref, act_ref):
    x_mid = x + dot(o_ref[...], packed_ref[:, OUT_AT : OUT_AT + x.shape[1]])
    mid_ref[...] = x_mid
    nf = (x_mid * inverse_rms(x_mid) * gain).astype(BF)
    nf_ref[...] = nf
    total = x_mid
    for at in range(0, FF, CHUNK):
        gate = dot(nf, packed_ref[:, GU_AT + at : GU_AT + at + CHUNK])
        up = dot(nf, packed_ref[:, GU_AT + FF + at : GU_AT + FF + at + CHUNK])
        gu_ref[:, at : at + CHUNK] = gate
        gu_ref[:, FF + at : FF + at + CHUNK] = up
        act = (gate * lax.logistic(gate) * up).astype(BF)
        act_ref[:, at : at + CHUNK] = act
        total = total + dot(act, down_ref[at : at + CHUNK, :])
    return total


def pre_kernel(x_ref, gain_ref, first_ref, c_ref, s_ref, normed_ref, q_ref, kv_ref):
    project(x_ref[...], gain_ref[0:1, :], first_ref, c_ref[...], s_ref[...], normed_ref, q_ref, kv_ref)


def mid_kernel(
    x_ref, o_ref, gain_ref, first_ref, packed_ref, down_ref, c_ref, s_ref,
    mid_ref, nf_ref, gu_ref, act_ref, next_ref, normed_ref, q_ref, kv_ref,
):
    x = feed(x_ref[...], o_ref, gain_ref[1:2, :], packed_ref, down_ref, mid_ref, nf_ref, gu_ref, act_ref)
    next_ref[...] = x
    project(x, gain_ref[0:1, :], first_ref, c_ref[...], s_ref[...], normed_ref, q_ref, kv_ref)


def post_kernel(
    x_ref, o_ref, gain_ref, packed_ref, down_ref,
    mid_ref, nf_ref, gu_ref, act_ref, next_ref, both_ref,
):
    x = feed(x_ref[...], o_ref, gain_ref[1:2, :], packed_ref, down_ref, mid_ref, nf_ref, gu_ref, act_ref)
    next_ref[...] = x
    final = x * inverse_rms(x) * gain_ref[2:3, :]
    piece = x.shape[0] // 2
    for p in range(2):
        both_ref[p] = pack(final[p * piece : (p + 1) * piece]).astype(BF)


def projected_shapes(rows, width):
    piece = rows // 2
    return [
        shape((rows, width), BF),
        shape((KVH, 2, GROUP * piece, 2 * HD), BF),
        shape((2, KVH, piece, 2 * HD), BF),
    ]


def fed_shapes(rows, width):
    return [
        shape((rows, width), F32),
        shape((rows, width), BF),
        shape((rows, 2 * FF), F32),
        shape((rows, FF), BF),
        shape((rows, width), F32),
    ]


def causal(scores, piece):
    row = lax.broadcasted_iota(jnp.int32, scores.shape, 0) & (piece - 1)
    col = lax.broadcasted_iota(jnp.int32, scores.shape, 1)
    return jnp.where(row >= col, scores, MASKED)


def attend_kernel(n, me_ref, q_ref, *refs):
    kvs, (o_ref, lse_ref, kv_ref) = refs[:n], refs[n:]
    me = me_ref[0]
    piece = kvs[0].shape[2]
    lows = [None] + [(me ^ r) < me for r in range(1, n)]
    for g in range(KVH):
        for r in range(n):
            kv_ref[g, r * piece : (r + 1) * piece, :] = kvs[r][0, g]
            kv_ref[g, (n + r) * piece : (n + r + 1) * piece, :] = kvs[r][1, g]
        wide_kv = kv_ref[g, 0 : n * piece, :]
        q_a = q_ref[g, 0]
        q_b = q_ref[g, 1]
        wide = dot_t(q_b, wide_kv)
        own_a = causal(dot_t(q_a, kvs[0][0, g]), piece)
        own_b = causal(dot_t(q_b, kvs[0][1, g]), piece)
        m_a = jnp.max(own_a, -1, keepdims=True)
        m_b = jnp.maximum(jnp.max(own_b, -1, keepdims=True), jnp.max(wide, -1, keepdims=True))
        tiles = [None]
        for r in range(1, n):
            low = lows[r]
            tile = dot_t(jnp.where(low, q_a, q_b), jnp.where(low, kvs[r][0, g], kvs[r][1, g]))
            top = jnp.max(tile, -1, keepdims=True)
            m_a = jnp.maximum(m_a, top + jnp.where(low, 0.0, -jnp.inf))
            m_b = jnp.maximum(m_b, top + jnp.where(low, -jnp.inf, 0.0))
            tiles.append(tile)
        e = jnp.exp(wide - m_b)
        l_b = jnp.sum(e, -1, keepdims=True)
        o_b = dot(e.astype(BF), wide_kv)
        e = jnp.exp(own_b - m_b)
        l_b += jnp.sum(e, -1, keepdims=True)
        o_b += dot(e.astype(BF), kvs[0][1, g])
        e = jnp.exp(own_a - m_a)
        l_a = jnp.sum(e, -1, keepdims=True)
        o_a = dot(e.astype(BF), kvs[0][0, g])
        for r in range(1, n):
            low = lows[r]
            in_a = jnp.where(low, 1.0, 0.0)
            in_b = 1.0 - in_a
            e = jnp.exp(tiles[r] - (m_a * in_a + m_b * in_b))
            total = jnp.sum(e, -1, keepdims=True)
            o = dot(e.astype(BF), jnp.where(low, kvs[r][0, g], kvs[r][1, g]))
            l_a += total * in_a
            l_b += total * in_b
            o_a += o * in_a
            o_b += o * in_b
        lse_ref[g, 0] = m_a + jnp.log(l_a)
        lse_ref[g, 1] = m_b + jnp.log(l_b)
        out = [(o_a / l_a).astype(BF), (o_b / l_b).astype(BF)]
        for p in range(2):
            for j in range(GROUP):
                h = g * GROUP + j
                o_ref[p * piece : (p + 1) * piece, h * HD : (h + 1) * HD] = out[p][
                    j * piece : (j + 1) * piece, HD:
                ]


def attend(me, queries, kvs):
    n = len(kvs)
    piece = kvs[0].shape[2]
    stacked = GROUP * piece
    return call(
        functools.partial(attend_kernel, n),
        "attend",
        [me, queries] + kvs,
        [shape((2 * piece, H * HD), BF), shape((KVH, 2, stacked, 1), F32), shape((KVH, 2 * n * piece, 2 * HD), BF)],
        scalars=1,
        limit=28,
        flops=2 * 2 * H * HD * piece * piece * (2 * n + 1) * 2,
    )


def attend_back_kernel(n, me_ref, q_ref, do_ref, lse_ref, kv_ref, *refs):
    (dq_ref, keep_ref, send_ref), (sum_ref,) = refs[:3], refs[3:]
    me = me_ref[0]
    piece = kv_ref.shape[1] // (2 * n)
    lows = [None] + [(me ^ r) < me for r in range(1, n)]
    for g in range(KVH):
        wide_kv = kv_ref[g, 0 : n * piece, :]
        kv_a0 = kv_ref[g, 0:piece, :]
        kv_b0 = kv_ref[g, n * piece : (n + 1) * piece, :]
        q_a, q_b = q_ref[g, 0], q_ref[g, 1]
        do_a, do_b = do_ref[g, 0], do_ref[g, 1]
        lse_a, lse_b = lse_ref[g, 0], lse_ref[g, 1]
        p_wide = jnp.exp(dot_t(q_b, wide_kv) - lse_b)
        w_wide = dot_t(do_b, wide_kv)
        d_b = jnp.sum(p_wide * w_wide, -1, keepdims=True)
        p_own_a = jnp.exp(causal(dot_t(q_a, kv_a0), piece) - lse_a)
        w_own_a = dot_t(do_a, kv_a0)
        d_a = jnp.sum(p_own_a * w_own_a, -1, keepdims=True)
        p_own_b = jnp.exp(causal(dot_t(q_b, kv_b0), piece) - lse_b)
        w_own_b = dot_t(do_b, kv_b0)
        d_b += jnp.sum(p_own_b * w_own_b, -1, keepdims=True)
        tiles = [None]
        for r in range(1, n):
            low = lows[r]
            in_a = jnp.where(low, 1.0, 0.0)
            in_b = 1.0 - in_a
            k = jnp.where(low, kv_ref[g, r * piece : (r + 1) * piece, :], kv_ref[g, (n + r) * piece : (n + r + 1) * piece, :])
            p = jnp.exp(dot_t(jnp.where(low, q_a, q_b), k) - (lse_a * in_a + lse_b * in_b))
            w = dot_t(jnp.where(low, do_a, do_b), k)
            total = jnp.sum(p * w, -1, keepdims=True)
            d_a += total * in_a
            d_b += total * in_b
            tiles.append((p, w))

        def both(p, w, inner, q, do, k):
            ds = (p * (w - inner)).astype(BF)
            dq = dot(ds, k)
            dkv = dot_w(ds, q) + dot_w(p.astype(BF), do)
            return dq, dkv

        dq_b, dkv = both(p_wide, w_wide, d_b, q_b, do_b, wide_kv)
        sum_ref[...] = dkv
        dq, dkv_b0 = both(p_own_b, w_own_b, d_b, q_b, do_b, kv_b0)
        dq_b += dq
        dq_a, dkv_a0 = both(p_own_a, w_own_a, d_a, q_a, do_a, kv_a0)
        sum_ref[0:piece, :] += dkv_a0

        def put(half, r, value):
            ref = send_ref if r & 1 else keep_ref
            ref[r // 2, half, g] = value

        put(1, 0, dkv_b0)
        for r in range(1, n):
            low = lows[r]
            in_a = jnp.where(low, 1.0, 0.0)
            in_b = 1.0 - in_a
            p, w = tiles[r]
            k = jnp.where(low, kv_ref[g, r * piece : (r + 1) * piece, :], kv_ref[g, (n + r) * piece : (n + r + 1) * piece, :])
            dq, dkv = both(p, w, d_a * in_a + d_b * in_b, jnp.where(low, q_a, q_b), jnp.where(low, do_a, do_b), k)
            dq_a += dq * in_a
            dq_b += dq * in_b
            sum_ref[r * piece : (r + 1) * piece, :] += dkv * in_a
            put(1, r, dkv * in_b)
        for r in range(n):
            put(0, r, sum_ref[r * piece : (r + 1) * piece, :])
        out = [(dq_a * 0.125).astype(BF), (dq_b * 0.125).astype(BF)]
        for p in range(2):
            for j in range(GROUP):
                h = g * GROUP + j
                dq_ref[p * piece : (p + 1) * piece, h * HD : (h + 1) * HD] = out[p][
                    j * piece : (j + 1) * piece, :HD
                ]


def attend_back(me, queries, d_out, lse, kv_all, n):
    piece = kv_all.shape[1] // (2 * n)
    block = (n // 2, 2, KVH, piece, 2 * HD)
    return call(
        functools.partial(attend_back_kernel, n),
        "attend_back",
        [me, queries, d_out, lse, kv_all],
        [shape((2 * piece, H * HD), BF), shape(block, F32), shape(block, F32)],
        [pltpu.VMEM((n * piece, 2 * HD), F32)],
        scalars=1,
        limit=32,
        flops=5 * 2 * H * HD * piece * piece * (2 * n + 1) * 2,
    )


def feed_back(d_x, gain, packed_ref, down_ref, mid_ref, gu_ref, outs):
    db_ref, dgu_ref, dmid_ref, da_ref, do_ref, gain_ref = outs
    rows, width = d_x.shape
    piece = rows // 2
    d_branch = d_x.astype(BF)
    db_ref[...] = d_branch
    d_nf = jnp.zeros(d_x.shape, F32)
    for at in range(0, FF, CHUNK):
        d_act = dot_t(d_branch, down_ref[at : at + CHUNK, :])
        gate = gu_ref[:, at : at + CHUNK]
        up = gu_ref[:, FF + at : FF + at + CHUNK]
        sig = lax.logistic(gate)
        d_gate = (d_act * up * (sig * (1.0 + gate * (1.0 - sig)))).astype(BF)
        d_up = (d_act * (gate * sig)).astype(BF)
        dgu_ref[:, at : at + CHUNK] = d_gate
        dgu_ref[:, FF + at : FF + at + CHUNK] = d_up
        d_nf += dot_t(d_gate, packed_ref[:, GU_AT + at : GU_AT + at + CHUNK])
        d_nf += dot_t(d_up, packed_ref[:, GU_AT + FF + at : GU_AT + FF + at + CHUNK])
    d_norm, gain_ref[...] = rms_back(mid_ref[...], gain, d_nf)
    d_mid = d_x + d_norm
    dmid_ref[...] = d_mid
    d_attn = d_mid.astype(BF)
    da_ref[...] = d_attn
    d_att = dot_t(d_attn, packed_ref[:, OUT_AT : OUT_AT + width])
    nothing = jnp.zeros((rows, HD), F32)
    for h in range(H):
        g, j = divmod(h, GROUP)
        part = jnp.concatenate([nothing, d_att[:, h * HD : (h + 1) * HD]], 1).astype(BF)
        for p in range(2):
            do_ref[g, p, j * piece : (j + 1) * piece, :] = part[p * piece : (p + 1) * piece]


def fed_back_shapes(rows, width):
    piece = rows // 2
    return [
        shape((rows, width), BF),
        shape((rows, 2 * FF), BF),
        shape((rows, width), F32),
        shape((rows, width), BF),
        shape((KVH, 2, GROUP * piece, 2 * HD), BF),
        shape((1, width), F32),
    ]


def sum_refs(refs, at):
    total = refs[0][at].astype(F32)
    for ref in refs[1:]:
        total += ref[at].astype(F32)
    return total


def project_back(d_mid, dq_ref, parts, gain, packed_ref, x, c, s, outs):
    dq_raw_ref, dkv_raw_ref, gain_ref = outs
    dq = dq_ref[...].astype(F32)
    for h in range(H):
        a = dq[:, h * HD : h * HD + HALF]
        b = dq[:, h * HD + HALF : (h + 1) * HD]
        dq_raw_ref[:, h * HD : (h + 1) * HD] = jnp.concatenate([a * c + b * s, b * c - a * s], 1).astype(BF)
    for g in range(KVH):
        d = jnp.concatenate(
            [sum_refs(parts, (0, g)), sum_refs(parts, (1, g))], 0
        ).astype(BF).astype(F32)
        a = d[:, :HALF]
        b = d[:, HALF:HD]
        dkv_raw_ref[:, g * HD : (g + 1) * HD] = jnp.concatenate([a * c + b * s, b * c - a * s], 1).astype(BF)
        dkv_raw_ref[:, (KVH + g) * HD : (KVH + g + 1) * HD] = d[:, HD:].astype(BF)
    d_normed = dot_t(dq_raw_ref[...], packed_ref[:, Q_AT : Q_AT + H * HD])
    d_normed += dot_t(dkv_raw_ref[...], packed_ref[:, KV_AT : KV_AT + 2 * KVH * HD])
    d_in, gain_ref[...] = rms_back(x, gain, d_normed)
    return d_mid + d_in


def back_first_kernel(terms, x_ref, target_ref, weight_ref, gain_ref, packed_ref, down_ref, mid_ref, gu_ref, *refs):
    parts, outs = refs[:terms], refs[terms:]
    piece = x_ref.shape[0] // 2
    d_final = jnp.concatenate([unpack(sum_refs(parts, 0), piece), unpack(sum_refs(parts, 1), piece)], 0)
    d_final += column(weight_ref[...]) * target_ref[...].astype(F32)
    d_x, outs[0][...] = rms_back(x_ref[...], gain_ref[2:3, :], d_final)
    feed_back(d_x, gain_ref[1:2, :], packed_ref, down_ref, mid_ref, gu_ref, outs[1:])


def back_mid_kernel(
    terms, dmid_ref, dq_ref, x_ref, c_ref, s_ref, gain_ref, first_ref, packed_ref, down_ref, mid_ref, gu_ref, *refs
):
    parts, outs = refs[:terms], refs[terms:]
    d_x = project_back(
        dmid_ref[...], dq_ref, parts, gain_ref[0:1, :], first_ref, x_ref[...], c_ref[...], s_ref[...], outs[:3]
    )
    feed_back(d_x, gain_ref[1:2, :], packed_ref, down_ref, mid_ref, gu_ref, outs[3:])


def back_last_kernel(terms, dmid_ref, dq_ref, x_ref, c_ref, s_ref, gain_ref, first_ref, *refs):
    parts, outs = refs[:terms], refs[terms:]
    d_x = project_back(
        dmid_ref[...], dq_ref, parts, gain_ref[0:1, :], first_ref, x_ref[...], c_ref[...], s_ref[...], outs[:3]
    )
    piece = d_x.shape[0] // 2
    for p in range(2):
        outs[3][p] = pack(d_x[p * piece : (p + 1) * piece]).astype(BF)


def head_kernel(vocab, active_ref, hit_ref, table_ref, *refs):
    pieces, (u_ref, stat_ref), (rows_ref, s_ref) = refs[:-4], refs[-4:-2], refs[-2:]
    n = len(pieces)
    piece = rows_ref.shape[0] // (2 * n)
    rows = 2 * piece
    for k, ref in enumerate(pieces):
        for p in range(2):
            rows_ref[(p * n + k) * piece : (p * n + k + 1) * piece, :] = unpack(ref[p], piece)
    padded = table_ref.shape[0]

    def block(i, _):
        at_row = pl.multiple_of(i * rows, rows)

        @pl.when(active_ref[i] == 0)
        def _():
            u_ref[pl.ds(at_row, rows), :] = jnp.zeros((rows, u_ref.shape[1]), F32)
            stat_ref[i] = jnp.concatenate([jnp.zeros((1, rows), F32), jnp.ones((1, rows), F32), jnp.zeros((1, rows), F32)], 0)

        @pl.when(active_ref[i] != 0)
        def _():
            mine = rows_ref[pl.ds(at_row, rows), :]
            hits = column(hit_ref[i])
            highest = jnp.full((rows, 1), -jnp.inf, F32)
            for at in range(0, padded, VTILE):
                s = dot_t(mine, table_ref[at : at + VTILE, :])
                if at + VTILE > vocab:
                    cols = lax.broadcasted_iota(jnp.int32, (rows, VTILE), 1) + at
                    s = jnp.where(cols < vocab, s, -jnp.inf)
                s_ref[:, at : at + VTILE] = s
                highest = jnp.maximum(highest, jnp.max(s, -1, keepdims=True))
            total = jnp.zeros((rows, 1), F32)
            picked = jnp.zeros((rows, 1), F32)
            u = jnp.zeros((rows, u_ref.shape[1]), F32)
            for at in range(0, padded, VTILE):
                s = s_ref[:, at : at + VTILE]
                e = jnp.exp(s - highest)
                total += jnp.sum(e, -1, keepdims=True)
                hit = lax.broadcasted_iota(jnp.int32, (rows, VTILE), 1) == hits - at
                picked += jnp.sum(jnp.where(hit, s, 0.0), -1, keepdims=True)
                e = jnp.where(hit, 0.0, e).astype(BF)
                u += dot(e, table_ref[at : at + VTILE, :])
            u_ref[pl.ds(at_row, rows), :] = u
            lane = lax.broadcasted_iota(jnp.int32, (rows, 8), 1)
            found = jnp.where(lane == 0, highest, jnp.where(lane == 1, total, picked))
            stat_ref[i] = jnp.transpose(found)[0:3, :]

        return 0

    lax.fori_loop(0, u_ref.shape[0] // rows, block, 0)


def head_forward(active, hits, table, pieces, vocab):
    width = table.shape[1]
    count = pieces[0].size * len(pieces) // width
    rows = count // len(pieces)
    return call(
        functools.partial(head_kernel, vocab),
        "head_forward",
        [active, hits, table] + pieces,
        [shape((count, width), F32), shape((count // rows, 3, rows), F32)],
        [pltpu.VMEM((count, width), BF), pltpu.VMEM((rows, table.shape[0]), F32)],
        scalars=1,
        flops=4 * count * table.size,
    )


def scale_kernel(n, u_ref, scale_ref, *refs):
    stats, (norm_ref, keep_ref, send_ref) = refs[:n], refs[n:]
    blocks = norm_ref.shape[0]
    rows = norm_ref.shape[2]
    piece = rows // 2
    per_half = blocks // 2
    for j in range(blocks):
        half, jj = divmod(j, per_half)
        found = []
        for b in range(n):
            st = stats[b][half * per_half + (jj ^ (b >> 1))]
            if b & 1:
                st = jnp.concatenate([st[:, piece:], st[:, :piece]], 1)
            found.append(st)
        top = found[0][0:1]
        for st in found[1:]:
            top = jnp.maximum(top, st[0:1])
        total = jnp.zeros_like(top)
        for st in found:
            total += st[1:2] * jnp.exp(st[0:1] - top)
        log_norm = top + jnp.log(total)
        picked = jnp.zeros_like(top)
        for st in found:
            picked += st[2:3]
        norm_ref[j] = jnp.concatenate([log_norm, picked], 0)
        factor = column(jnp.exp(found[0][0:1] - log_norm) * scale_ref[j])
        scaled = u_ref[j * rows : (j + 1) * rows, :] * factor
        for k in range(2):
            ref = send_ref if k else keep_ref
            ref[jj, half] = pack(scaled[k * piece : (k + 1) * piece]).astype(ref.dtype)


def head_scale(u, scale, stats):
    n = len(stats)
    count, width = u.shape
    piece = count // (2 * n)
    block = (n // 2, 2, piece * width // 128, 128)
    return call(
        functools.partial(scale_kernel, n),
        "head_scale",
        [u, scale] + stats,
        [shape((scale.shape[0], 2, scale.shape[2]), F32), shape(block, F32), shape(block, BF)],
        flops=2 * u.size,
        limit=28,
    )


def head_grad_kernel(first, step, begin, active_ref, stat_ref, hit_ref, far_table_ref, far_packed_ref, *refs):
    old_ref = None if first else refs[0]
    out_ref, grad_ref, rows_ref, table_ref, packed_ref, sems = refs[-6:]
    sem = sems.at[0]
    turn = pl.program_id(0)
    n = packed_ref.shape[0]
    blocks = stat_ref.shape[1] // step
    piece = rows_ref.shape[0] // (2 * n)
    rows = 2 * piece * step
    vocab = grad_ref.shape[0]
    tile = vocab // 5

    load = pltpu.make_async_copy(far_packed_ref.at[begin + turn], packed_ref, sems.at[1])
    load.start()

    @pl.when(turn == 0)
    def _():
        table_load = pltpu.make_async_copy(far_table_ref, table_ref, sems.at[2])
        table_load.start()
        if first:
            grad_ref[...] = jnp.zeros_like(grad_ref)
        else:
            copy = pltpu.make_async_copy(old_ref, grad_ref, sem)
            copy.start()
            copy.wait()
        table_load.wait()

    load.wait()

    for b in range(n):
        for p in range(2):
            rows_ref[(p * n + b) * piece : (p * n + b + 1) * piece, :] = unpack(packed_ref[b, p], piece)

    def block(i, _):
        wanted = active_ref[turn, step * i]
        for k in range(1, step):
            wanted = wanted + active_ref[turn, step * i + k]

        @pl.when(wanted != 0)
        def _():
            mine = rows_ref[pl.ds(pl.multiple_of(i * rows, rows), rows), :]
            stat = jnp.concatenate([stat_ref[0, step * i + k] for k in range(step)], 1)
            log_norm, scale = stat[0:1], stat[1:2]
            hits = jnp.concatenate([hit_ref[0, step * i + k] for k in range(step)], 1)
            for at in range(0, vocab, tile):
                s = dot_t(table_ref[at : at + tile, :], mine)
                d = jnp.exp(s - log_norm) * scale
                index = lax.broadcasted_iota(jnp.int32, (tile, rows), 0)
                d = jnp.where(index == hits - at, d - scale, d).astype(BF)
                grad_ref[at : at + tile, :] += dot(d, mine)

        return 0

    lax.fori_loop(0, blocks, block, 0)

    @pl.when(turn == pl.num_programs(0) - 1)
    def _():
        back = pltpu.make_async_copy(grad_ref, out_ref, sem)
        back.start()
        back.wait()


def head_grad(active, stats, hits, table, packed, vocab, so_far, begin, end):
    width = table.shape[1]
    count = packed[0].size // width
    first = so_far is None
    part = slice(begin, end)
    inputs = [active[part], stats, hits, table, packed] + ([] if first else [so_far])
    anywhere = pl.BlockSpec(memory_space=pltpu.HBM)

    def sequence(v):
        dims = len(v.shape)
        return pl.BlockSpec((1,) + v.shape[1:], lambda i: (begin + i,) + (0,) * (dims - 1))

    step = 2 if stats.shape[1] % 4 == 0 else 1
    return pl.pallas_call(
        functools.partial(head_grad_kernel, first, step, begin),
        grid=(end - begin,),
        in_specs=[
            pl.BlockSpec(memory_space=pltpu.SMEM),
            sequence(stats),
            sequence(hits),
            pl.BlockSpec(memory_space=pltpu.HBM),
            pl.BlockSpec(memory_space=pltpu.HBM),
        ] + ([] if first else [anywhere]),
        out_specs=anywhere,
        out_shape=shape((vocab, width), F32),
        scratch_shapes=[
            pltpu.VMEM((vocab, width), F32),
            pltpu.VMEM((count, width), BF),
            pltpu.VMEM(table.shape, BF),
            pltpu.VMEM(packed.shape[1:], BF),
            pltpu.SemaphoreType.DMA((3,)),
        ],
        compiler_params=pltpu.CompilerParams(vmem_limit_bytes=40 * MIB),
        cost_estimate=pl.CostEstimate(
            flops=3 * count * table.size * (end - begin), bytes_accessed=8 * vocab * width, transcendentals=0
        ),
        input_output_aliases={} if first else {5: 0},
        name="head_grad",
    )(*inputs)


def add_rows_kernel(bits, count_ref, key_ref, far_packed_ref, grad_ref, far_out_ref, square_ref, out_ref, wide_ref, packed_ref, sems):
    turn = pl.program_id(0)
    n = packed_ref.shape[1]
    slot = turn & 1
    sem = sems.at[2]
    piece = wide_ref.shape[0] // (2 * n)

    @pl.when(turn == 0)
    def _():
        pltpu.make_async_copy(grad_ref, out_ref, sem).start()
        pltpu.make_async_copy(far_packed_ref.at[0], packed_ref.at[0], sems.at[0]).start()

    @pl.when(turn + 1 < pl.num_programs(0))
    def _():
        pltpu.make_async_copy(far_packed_ref.at[turn + 1], packed_ref.at[1 - slot], sems.at[1 - slot]).start()

    pltpu.make_async_copy(far_packed_ref.at[turn], packed_ref.at[slot], sems.at[slot]).wait()

    for b in range(n):
        for p in range(2):
            wide_ref[(p * n + b) * piece : (p * n + b + 1) * piece, :] = unpack(packed_ref[slot, b, p].astype(F32), piece)

    @pl.when(turn == 0)
    def _():
        pltpu.make_async_copy(grad_ref, out_ref, sem).wait()

    def add(i):
        key = key_ref[turn, i]
        row = key >> bits
        at = key & ((1 << bits) - 1)
        out_ref[pl.ds(row, 1), :] += wide_ref[pl.ds(at, 1), :]

    def add_some(i, _):
        for k in range(8):
            add(8 * i + k)
        return 0

    def add_one(i, _):
        add(i)
        return 0

    count = count_ref[turn]
    lax.fori_loop(0, count >> 3, add_some, 0)
    lax.fori_loop((count >> 3) << 3, count, add_one, 0)

    @pl.when(turn == pl.num_programs(0) - 1)
    def _():
        back = pltpu.make_async_copy(out_ref, far_out_ref, sem)
        back.start()
        tile = 80
        width = out_ref.shape[1]

        def squares(i, total):
            v = out_ref[pl.ds(pl.multiple_of(i * tile, 8), tile), :]
            return total + jnp.sum((v * v).reshape(tile // 8, 8, width), 0)

        square_ref[...] = lax.fori_loop(0, out_ref.shape[0] // tile, squares, jnp.zeros((8, width), F32))
        back.wait()


def add_rows(counts, keys, packed, grad, bits):
    vocab, width = grad.shape
    count = packed[0].size // width
    return pl.pallas_call(
        functools.partial(add_rows_kernel, bits),
        grid=(packed.shape[0],),
        in_specs=[
            pl.BlockSpec(memory_space=pltpu.SMEM),
            pl.BlockSpec(memory_space=pltpu.SMEM),
            pl.BlockSpec(memory_space=pltpu.HBM),
            pl.BlockSpec(memory_space=pltpu.HBM),
        ],
        out_specs=[
            pl.BlockSpec(memory_space=pltpu.HBM),
            pl.BlockSpec((8, width), lambda i: (0, 0)),
        ],
        out_shape=[shape(grad.shape, F32), shape((8, width), F32)],
        scratch_shapes=[
            pltpu.VMEM(grad.shape, F32),
            pltpu.VMEM((count, width), F32),
            pltpu.VMEM((2,) + packed.shape[1:], BF),
            pltpu.SemaphoreType.DMA((3,)),
        ],
        compiler_params=pltpu.CompilerParams(vmem_limit_bytes=60 * MIB),
        cost_estimate=pl.CostEstimate(flops=2 * grad.size, bytes_accessed=8 * grad.size, transcendentals=0),
        name="add_rows",
    )(counts, keys, packed, grad)


def adam_update(weight, first, second, grad, decay):
    next_first = BETA_ONE * first + (1.0 - BETA_ONE) * grad
    next_second = BETA_TWO * second + (1.0 - BETA_TWO) * grad * grad
    corrected = next_first / (1.0 - BETA_ONE**STEP_NO)
    scaled = jnp.sqrt(next_second / (1.0 - BETA_TWO**STEP_NO)) + ADAM_EPSILON
    return (weight - RATE * (corrected / scaled + decay * weight), next_first, next_second)


def deal_blocks(value_ref, rows, columns, at_row, me, keep_ref, send_ref):
    for b in range(value_ref.shape[0] // rows):
        r = me ^ b

        def put(ref):
            for k in range(columns // 128):
                ref[r >> 1, at_row + k * rows : at_row + (k + 1) * rows, :] = value_ref[
                    b * rows : (b + 1) * rows, k * 128 : (k + 1) * 128
                ]

        pl.when((r & 1) == 0)(functools.partial(put, keep_ref))
        pl.when((r & 1) == 1)(functools.partial(put, send_ref))
    return at_row + rows * (columns // 128)


def clear_end(at_row, *refs):
    for ref in refs:
        if ref.shape[1] > at_row:
            ref[:, at_row:, :] = jnp.zeros((ref.shape[0], ref.shape[1] - at_row, ref.shape[2]), F32)


def undeal(ref, at_row, rows, columns):
    count = -(-columns // 128)
    parts = [ref[at_row + k * rows : at_row + (k + 1) * rows, :] for k in range(count)]
    return jnp.concatenate(parts, 1)[:, :columns]


def early_grads_kernel(
    n, me_ref, nf0, nf1, dgu0, dgu1, act0, act1, db0, db1, o0, o1, da0, da1, keep_ref, send_ref, wide, tall
):
    me = me_ref[0]
    width = nf0.shape[1]
    padded = tall.shape[1]

    def product(l0, l1, r0, r1):
        return dot_w(l0[...], r0) + dot_w(l1[...], r1)

    at = 0
    for part in (slice(0, FF), slice(FF, 2 * FF)):
        wide[...] = product(nf0, nf1, dgu0[:, part], dgu1[:, part])
        at = deal_blocks(wide, width // n, FF, at, me, keep_ref, send_ref)
    tall[:, width:] = jnp.zeros((FF, padded - width), F32)
    tall[:, :width] = product(act0, act1, db0[...], db1[...])
    at = deal_blocks(tall, FF // n, padded, at, me, keep_ref, send_ref)
    tall[0:width, :width] = product(o0, o1, da0[...], da1[...])
    at = deal_blocks(tall.at[0:width], width // n, padded, at, me, keep_ref, send_ref)
    clear_end(at, keep_ref, send_ref)


def late_grads_kernel(n, me_ref, n0, n1, kv0, kv1, q0, q1, at0, at1, ff0, ff1, fin, keep_ref, send_ref, wide):
    me = me_ref[0]
    width = n0.shape[1]
    kv_width = kv0.shape[1]
    gains = jnp.concatenate(
        [at0[...] + at1[...], ff0[...] + ff1[...], fin[...], jnp.zeros((5, width), F32)], 0
    )
    wide[:, 0:kv_width] = dot_w(n0[...], kv0[...]) + dot_w(n1[...], kv1[...])
    wide[:, kv_width : kv_width + 128] = jnp.concatenate(
        [jnp.transpose(gains), jnp.zeros((width, 120), F32)], 1
    )
    at = deal_blocks(wide, width // n, kv_width + 128, 0, me, keep_ref, send_ref)
    wide[:, width:] = jnp.zeros((width, wide.shape[1] - width), F32)
    wide[:, :width] = dot_w(n0[...], q0[...]) + dot_w(n1[...], q1[...])
    at = deal_blocks(wide, width // n, wide.shape[1], at, me, keep_ref, send_ref)
    clear_end(at, keep_ref, send_ref)


def split_kernel(terms, place_ref, *refs):
    outs, (total_ref,) = refs[terms:-1], refs[-1:]
    total = refs[0][...].astype(F32)
    for ref in refs[1:terms]:
        total += ref[...].astype(F32)
    total_ref[...] = total
    share = outs[0].shape[0]
    for r, ref in enumerate(outs):
        at = pl.multiple_of((place_ref[0] ^ r) * share, 16)
        ref[...] = total_ref[pl.ds(at, share), :].astype(ref.dtype)


def add_kernel(*refs):
    total = refs[0][...].astype(F32)
    for ref in refs[1:-1]:
        total += ref[...].astype(F32)
    refs[-1][...] = total.astype(refs[-1].dtype)


def join_kernel(place_ref, *refs):
    out_ref = refs[-1]
    share = refs[0].shape[0]
    for r, ref in enumerate(refs[:-1]):
        at = pl.multiple_of((place_ref[0] ^ r) * share, 16)
        out_ref[pl.ds(at, share), :] = ref[...].astype(F32)


def sum_over(terms, place, axis, wire, until, finally_until):
    n = lax.axis_size(axis)
    rows, columns = terms[0].shape
    share = rows // n
    parts = call(
        functools.partial(split_kernel, len(terms)), "split", [place] + terms,
        [shape((share, columns), F32)] + [shape((share, columns), wire)] * (n - 1),
        [pltpu.VMEM((rows, columns), F32)], scalars=1, limit=24,
    )
    got = all_after([swap(v, axis, r) for r, v in enumerate(parts) if r], until())
    got = [parts[0]] + got
    (mine,) = call(add_kernel, "add_up", got, [shape((share, columns), F32)], limit=24)
    everything = [mine] + all_after(everyone(mine, axis)[1:], finally_until())
    return call(
        join_kernel, "join", [place] + everything, [shape((rows, columns), F32)], scalars=1, limit=24,
    )[0]


def squares_kernel(*refs):
    out_ref = refs[-1]
    total = jnp.zeros((1, 1), F32)
    for ref in refs[:-1]:
        v = ref[...]
        v = v if ref is refs[0] else v * v
        total += jnp.sum(jnp.sum(v, 0, keepdims=True), 1, keepdims=True)
    out_ref[...] = total


def small_adam_kernel(factor_ref, early_ref, late_ref, *refs):
    states, results = refs[:18], refs[18:]
    factor = factor_ref[0]

    def update(k, grad, part=slice(None), decay=DECAY):
        olds = [states[3 * k + i][:, part] for i in range(3)]
        for i, value in enumerate(adam_update(*olds, grad * factor, decay)):
            results[3 * k + i][:, part] = value

    here, width = states[0].shape
    kv_width = states[3].shape[1]
    at = kv_width // 128 * here
    update(1, undeal(late_ref, 0, here, kv_width))
    update(5, jnp.transpose(late_ref[at : at + here, :])[0:3], decay=0.0)
    update(0, undeal(late_ref, at + here, here, width))
    at = 0
    for part in (slice(0, FF), slice(FF, 2 * FF)):
        update(3, undeal(early_ref, at, here, FF), part)
        at += FF // 128 * here
    down = states[12].shape[0]
    update(4, undeal(early_ref, at, down, width))
    update(2, undeal(early_ref, at + -(-width // 128) * down, here, width))


def table_adam_kernel(factor_ref, grad_ref, *refs):
    vocab, width = grad_ref.shape
    tile = 512
    factor = factor_ref[0]

    def update(grad_tile, w_tile, m_tile, v_tile, new_w, new_m, new_v):
        grad = jnp.transpose(grad_tile[...]) * factor
        new_w[...], new_m[...], new_v[...] = adam_update(w_tile[...], m_tile[...], v_tile[...], grad, DECAY)

    spec = pl.BlockSpec((width, tile), lambda i: (0, i))
    pltpu.emit_pipeline(
        update,
        grid=(pl.cdiv(vocab, tile),),
        in_specs=[pl.BlockSpec((tile, width), lambda i: (i, 0)), spec, spec, spec],
        out_specs=[spec] * 3,
    )(grad_ref, *refs)


def table_adam(factor, grad, weight, first, second):
    vocab, width = grad.shape
    far = pl.BlockSpec(memory_space=pltpu.HBM)
    outs = pl.pallas_call(
        table_adam_kernel,
        in_specs=[pl.BlockSpec(memory_space=pltpu.SMEM)] + [far] * 4,
        out_specs=[far] * 3,
        out_shape=[shape((width, vocab), F32)] * 3,
        compiler_params=pltpu.CompilerParams(vmem_limit_bytes=60 * MIB),
        cost_estimate=pl.CostEstimate(flops=20 * vocab * width, bytes_accessed=28 * vocab * width, transcendentals=0),
        name="table_adam",
    )(factor.reshape(1), grad, weight.T, first.T, second.T)
    return tuple(o.T for o in outs)


def body(*arguments):
    token_ids, response_mask = arguments[0], arguments[1]
    masters, firsts, seconds = arguments[4:11], arguments[11:18], arguments[18:25]
    embed_table, w_query, w_kv, w_out, w_gate_up, w_down, gains = masters
    groups = lax.axis_size("seq")
    batch = lax.axis_size("dp")
    me = lax.axis_index("seq")
    local_len = token_ids.shape[1]
    seq_len = groups * local_len
    piece = local_len // 2
    pieces = 2 * groups
    vocab, width = embed_table.shape
    base = me * vocab
    rows = local_len

    here = w_query.shape[0]
    early_pack = jnp.concatenate(
        [
            w_kv.astype(BF),
            w_query.astype(BF),
            gains.T.astype(BF),
            jnp.zeros((here, EARLY - GAIN_AT - 3), BF),
        ],
        1,
    )
    third = w_down.shape[0] // 3
    down_low = w_down.astype(BF)
    down_side = jnp.concatenate([down_low[k * third : (k + 1) * third] for k in range(3)], 1)
    late_pack = jnp.concatenate(
        [
            w_gate_up.astype(BF),
            w_out.astype(BF),
            jnp.zeros((here, 64), BF),
            jnp.pad(down_side, ((0, here - third), (0, 0))),
        ],
        1,
    )
    first_pack = lax.all_gather(early_pack, "seq", axis=0, tiled=True)
    gathered = lax.all_gather(late_pack, "seq")
    packed_full, down_full = call(
        spread_kernel, "spread", [gathered],
        [shape((groups, here, OUT_AT + width), BF), shape((groups * w_down.shape[0], width), BF)],
    )
    packed_full = packed_full.reshape(groups * here, OUT_AT + width)
    gain_rows = first_pack[:, GAIN_AT : GAIN_AT + 3].T.astype(F32)
    padded = (vocab + VTILE - 1) // VTILE * VTILE
    table = low_table(embed_table, padded)

    meta = jnp.concatenate([token_ids, response_mask], 0)
    ordered = lax.all_gather(meta, "seq", axis=1, tiled=True)
    who = jnp.arange(groups) ^ me

    order = jnp.concatenate([who, pieces - 1 - who])
    pick = order[:, None] == jnp.arange(pieces)[None, :]

    def met(values):
        cut = values.reshape(values.shape[0], 1, pieces, piece)
        chosen = jnp.sum(jnp.where(pick[None, :, :, None], cut, jnp.zeros((), values.dtype)), 2)
        return chosen.reshape(values.shape[0], pieces * piece)

    extra = 16
    ids_row = ordered[0]
    follow = jnp.concatenate([ids_row, jnp.zeros((piece,), jnp.int32)]).reshape(pieces + 1, piece)
    ids_wide = jnp.concatenate([ids_row.reshape(pieces, piece), follow[1:, :extra]], 1)
    evens = jnp.arange(0, groups, 2) ^ me
    odds = evens ^ 1
    wanted = jnp.stack(
        [jnp.stack([evens, pieces - 1 - evens], 1), jnp.stack([odds, pieces - 1 - odds], 1)], 0
    ).reshape(-1)
    ids_wide = jnp.sum(
        jnp.where((wanted[:, None] == jnp.arange(pieces)[None, :])[:, :, None], ids_wide[None], 0), 1
    )
    found = lookup((ids_wide - base).reshape(-1), table, 4 * (piece + extra))
    found_flag = found[:16, :128]
    found = found.reshape(2, groups // 2, 2, piece + extra, width)
    terms = scatter_all(found[0], found[1], "seq", BF, BF)
    found = sum(terms[1:], terms[0])
    hidden = jnp.concatenate([found[0, :piece], found[1, :piece]], 0).astype(F32)
    target_rows = jnp.concatenate([found[0, 1 : piece + 1], found[1, 1 : piece + 1]], 0)

    place = lax.axis_index("dp")
    which = jnp.arange(batch) ^ place
    sequence_spots = which[None, :] == jnp.arange(batch)[:, None]

    def by_sequence(values):
        stacked = jnp.stack(values, 0)
        spots = sequence_spots.reshape((batch, batch) + (1,) * (stacked.ndim - 1))
        return jnp.sum(jnp.where(spots, stacked[None], jnp.zeros((), stacked.dtype)), 1)

    def paired(values):
        cut = values.reshape(values.shape[0], pieces, piece)
        return jnp.concatenate([cut[:, :groups], cut[:, groups:][:, ::-1]], 1)

    all_meta = by_sequence(everyone(after(ordered, found_flag), "dp"))
    ids_all, mask_all = all_meta[:, 0], all_meta[:, 1]
    last = (jnp.arange(seq_len) < seq_len - 1).astype(F32)[None]
    valid_all = mask_all.astype(F32) * last
    counted = jnp.sum(valid_all)
    targets_all = jnp.concatenate([ids_all[:, 1:], jnp.zeros((batch, 1), jnp.int32)], 1)
    pair_valid = paired(valid_all)
    blocks = seq_len // rows
    half = blocks // 2
    own_valid = met(ordered[1:2].astype(F32) * last).reshape(blocks, 1, rows)
    own_target = jnp.concatenate([ordered[0:1, 1:], jnp.zeros((1, 1), jnp.int32)], 1)
    own_target = met(own_target) - base
    own_target = jnp.where((own_target >= 0) & (own_target < vocab), own_target, -1).reshape(blocks, 1, rows)
    own_scale = own_valid / counted
    own_active = (jnp.max(own_valid.reshape(blocks, rows), -1) > 0).astype(jnp.int32)
    pair_targets = (paired(targets_all) - base).reshape(batch, blocks, 1, rows)
    pair_active = (jnp.max(pair_valid.reshape(batch, blocks, rows), -1) > 0).astype(jnp.int32)

    own_pos = jnp.concatenate(
        [order[0] * piece + jnp.arange(piece), order[groups] * piece + jnp.arange(piece)]
    )
    inverse = 10000.0 ** (-jnp.arange(HALF).astype(F32) * 2.0 / HD)
    phases = own_pos.astype(F32)[:, None] * inverse[None, :]
    cosine, sine_wave = after(jnp.cos(phases), pair_valid, pair_targets, pair_active, own_target, own_scale), jnp.sin(phases)
    me_one = me.reshape(1).astype(jnp.int32)

    layer_flops = 2 * rows * width * (2 * H * HD + 2 * KVH * HD + 3 * FF)
    x0 = hidden
    packed_rows = piece * width // 128
    normed0, q0, kv = call(
        pre_kernel, "pre", [x0, gain_rows, first_pack, cosine, sine_wave], projected_shapes(rows, width),
        flops=layer_flops // 4, limit=24,
    )
    o0, lse0, kv0 = attend(me_one, q0, gather_all(kv, "seq"))
    mid0, nf0, gu0, act0, x1, normed1, q1, kv = call(
        mid_kernel, "mid", [x0, o0, gain_rows, first_pack, packed_full, down_full, cosine, sine_wave],
        fed_shapes(rows, width) + projected_shapes(rows, width), flops=layer_flops, limit=32,
    )
    o1, lse1, kv1 = attend(me_one, q1, gather_all(kv, "seq"))
    mid1, nf1, gu1, act1, x2, final = call(
        post_kernel, "post", [x1, o1, gain_rows, packed_full, down_full],
        fed_shapes(rows, width) + [shape((2, packed_rows, 128), BF)], flops=layer_flops, limit=32,
    )
    own_rows = gather_all(final, "seq")
    arrived = own_rows[groups - 1][0, :16]
    rows_all = lax.all_gather(after(final, arrived), ("dp", "seq"))
    rows_all = rows_all.reshape(batch, groups, 2, packed_rows, 128)

    u, stats = head_forward(own_active, own_target, table, own_rows, vocab)
    norms, keep, send = head_scale(u, own_scale, everyone(stats, "seq"))
    terms = scatter_all(keep, send, "seq", BF)

    def mine(row):
        return jnp.concatenate([row[0, :piece], row[half, :piece]])

    at_target = (jnp.exp(mine(norms[:, 1]) - mine(norms[:, 0])) - 1.0) * mine(own_scale[:, 0])
    at_target = at_target.astype(BF).astype(F32).reshape(1, rows)

    outs = call(
        functools.partial(back_first_kernel, len(terms)), "back_first",
        [x2, target_rows, at_target, gain_rows, packed_full, down_full, mid1, gu1] + terms,
        [shape((1, width), F32)] + fed_back_shapes(rows, width), flops=2 * layer_flops, limit=32,
    )
    gain_final, db1, dgu1, dmid1, da1, do1, gain_ffn1 = outs
    met_norms = jnp.swapaxes(after(norms, do1), 0, 1).reshape(2, 2, groups, piece)
    spots = (who[None, :] == jnp.arange(groups)[:, None]).astype(F32)
    piece_norms = jnp.sum(spots[None, None, :, :, None] * met_norms[:, :, None], 3).reshape(2, pieces, piece)
    all_norms = by_sequence(everyone(piece_norms, "dp"))
    loss = jnp.sum(jnp.where(pair_valid > 0, all_norms[:, 0] - all_norms[:, 1], 0.0)) / counted
    pair_stats = jnp.stack(
        [all_norms[:, 0].reshape(batch, blocks, rows), (pair_valid / counted).reshape(batch, blocks, rows)], 2
    )
    dq1, keep, send = attend_back(me_one, q1, do1, lse1, kv1, groups)
    place_one = place.reshape(1).astype(jnp.int32)
    terms = scatter_all(keep, send, "seq", BF)
    outs = call(
        functools.partial(back_mid_kernel, len(terms)), "back_mid",
        [dmid1, dq1, x1, cosine, sine_wave, gain_rows, first_pack, packed_full, down_full, mid0, gu0] + terms,
        [shape((rows, H * HD), BF), shape((rows, 2 * KVH * HD), BF), shape((1, width), F32)] + fed_back_shapes(rows, width),
        flops=2 * layer_flops, limit=32,
    )
    dq_raw1, dkv_raw1, gain_attn1, db0, dgu0, dmid0, da0, do0, gain_ffn0 = outs
    dq0, keep, send = attend_back(me_one, q0, do0, lse0, kv0, groups)
    wide_columns = -(-width // 128) * 128

    def padded_rows(count):
        return -(-count // (16 * batch)) * (16 * batch)

    early_rows = padded_rows((2 * here * FF + w_down.shape[0] * wide_columns + here * wide_columns) // 128)
    early = []

    def start_early_grads():
        early.extend(
            call(
                functools.partial(early_grads_kernel, groups), "early_grads",
                [me_one, nf0, nf1, dgu0, dgu1, act0, act1, after(db0, dq0), db1, o0, o1, da0, da1],
                [shape((groups // 2, early_rows, 128), F32)] * 2,
                [pltpu.VMEM((width, FF), F32), pltpu.VMEM((FF, wide_columns), F32)],
                scalars=1, flops=layer_flops * 2, limit=56,
            )
        )
        return early[1]

    terms = scatter_all(keep, send, "seq", BF, between=start_early_grads)
    outs = call(
        functools.partial(back_last_kernel, len(terms)), "back_last",
        [dmid0, dq0, x0, cosine, sine_wave, gain_rows, first_pack] + terms,
        [shape((rows, H * HD), BF), shape((rows, 2 * KVH * HD), BF), shape((1, width), F32), shape((2, packed_rows, 128), BF)],
        flops=layer_flops // 2, limit=24,
    )
    dq_raw0, dkv_raw0, gain_attn0, d_low = outs
    d_all = lax.all_gather(d_low, ("dp", "seq")).reshape(batch, groups, 2, packed_rows, 128)

    late_rows = padded_rows(here * (w_kv.shape[1] + 128 + wide_columns) // 128)
    late = call(
        functools.partial(late_grads_kernel, groups), "late_grads",
        [me_one, normed0, normed1, dkv_raw0, dkv_raw1, dq_raw0, dq_raw1, gain_attn0, gain_attn1, gain_ffn0, gain_ffn1, gain_final],
        [shape((groups // 2, late_rows, 128), F32)] * 2,
        [pltpu.VMEM((width, wide_columns), F32)],
        scalars=1, flops=layer_flops // 2,
    )
    ends = [1, 2, 3, batch]
    done = []

    def head_step(k):
        while len(done) <= k:
            begin = ends[len(done) - 1] if done else 0
            packed = rows_all if done else after(rows_all, late[1])
            done.append(
                head_grad(
                    pair_active, pair_stats, pair_targets, table, packed, vocab,
                    done[-1] if done else None, begin, ends[len(done)],
                )
            )
        return done[k]

    step = [functools.partial(head_step, k) for k in range(4)]
    early_terms = scatter_all(early[0], early[1], "seq", BF, between=lambda: late[1], until=step[1])
    late_terms = scatter_all(late[0], late[1], "seq", F32, between=step[0], until=step[1])
    bits = (seq_len - 1).bit_length()
    met_ids = paired(ids_all).reshape(batch, seq_len) - base
    inside = (met_ids >= 0) & (met_ids < vocab)
    keys = jnp.where(inside, met_ids * (1 << bits) + jnp.arange(seq_len)[None], 2147483647)
    keys = jnp.sort(keys, -1)
    counts = jnp.sum(inside.astype(jnp.int32), -1)
    early_sum = sum_over(early_terms, place_one, "dp", BF, step[2], step[3])
    grad_table, table_squares = add_rows(counts, keys, d_all, head_step(3), bits)
    late_sum = sum_over(late_terms, place_one, "dp", F32, step[2], lambda: table_squares)

    small = [early_sum, late_sum]
    (squares,) = call(squares_kernel, "squares", [table_squares] + small, [shape((1, 1), F32)], limit=24)
    squares = tree([squares] + [swap(squares, "seq", r) for r in range(2, groups, 2)])
    grad_norm = jnp.sqrt((squares + swap(squares, "seq", 1))[0, 0])
    factor = CLIP / jnp.maximum(grad_norm, CLIP)
    states = [v for i in range(1, 7) for v in (masters[i], firsts[i], seconds[i])]
    news = call(
        small_adam_kernel, "small_adam",
        [factor.reshape(1)] + small + states, [shape(v.shape, F32) for v in states], scalars=1, limit=48,
    )
    table_news = table_adam(factor, grad_table, masters[0], firsts[0], seconds[0])
    results = []
    for k in range(3):
        results += [table_news[k]] + [news[3 * i + k] for i in range(6)]
    return tuple(results) + (loss, grad_norm)


def solution(mesh):
    rows, cols, whole = P("seq", None), P(None, "seq"), P()
    group = (rows,) * 6 + (cols,)
    return jax.shard_map(
        body,
        mesh=mesh,
        in_specs=(P("dp", "seq"), P("dp", "seq"), whole, whole) + group * 3,
        out_specs=group * 3 + (whole, whole),
        check_vma=False,
    )
```

```python
import functools

import jax
import jax.numpy as jnp
from jax import lax
from jax.experimental import pallas as pl
from jax.experimental.pallas import tpu as pltpu
from jax.sharding import PartitionSpec as P

H = 9
KVH = 3
GROUP = H // KVH
HD = 64
HALF = HD // 2
FF = 1536
LAYERS = 2
STEP_NO = 10
EPSILON = 1e-05
CLIP = 0.01
RATE = 0.1
BETA_ONE = 0.9
BETA_TWO = 0.95
ADAM_EPSILON = 1e-08
DECAY = 0.1
MASKED = -1000000000.0
BF = jnp.bfloat16
F32 = jnp.float32
MIB = 1024 * 1024

KV_AT, Q_AT, GAIN_AT, EARLY = 0, 384, 960, 1024
GU_AT, OUT_AT = 0, 3072
CHUNK = 512
VTILE = 1024


def swap(x, axis, bit):
    n = lax.axis_size(axis)
    return lax.ppermute(x, axis, [(i, i ^ bit) for i in range(n)])


def gather_all(x, axis):
    n = lax.axis_size(axis)
    held = {0: x}
    for r in range(2, n, 2):
        held[r] = swap(x, axis, r)
    for r in range(0, n, 2):
        held[r + 1] = swap(held[r], axis, 1)
    return [held[r] for r in range(n)]


def merge_kernel(keep_ref, got_ref, own_ref, *others):
    for k in range(keep_ref.shape[0]):
        ref = others[k - 1] if k else own_ref
        ref[...] = (keep_ref[k].astype(F32) + got_ref[k].astype(F32)).astype(ref.dtype)


def scatter_all(keep, send, axis, wire, own=F32, between=None, until=None):
    got = swap(send, axis, 1)
    if between is not None:
        got = after(got, between())
    block = keep.shape[1:]
    outs = call(
        merge_kernel, "merge", [keep, got],
        [shape(block, own)] + [shape(block, wire)] * (keep.shape[0] - 1), limit=32,
    )
    arrived = [swap(x, axis, 2 * k) for k, x in enumerate(outs) if k]
    if until is not None:
        arrived = all_after(arrived, until())
    return [outs[0]] + arrived


def everyone(x, axis):
    return [x] + [swap(x, axis, r) for r in range(1, lax.axis_size(axis))]


def tree(terms):
    while len(terms) > 1:
        terms = [a + b for a, b in zip(terms[::2], terms[1::2])]
    return terms[0]


def after(x, *needs):
    return lax.optimization_barrier((x,) + needs)[0]


def all_after(xs, *needs):
    return list(lax.optimization_barrier(tuple(xs) + needs)[: len(xs)])


def dot(a, b):
    return jnp.dot(a, b, preferred_element_type=F32)


def dot_t(a, b):
    return lax.dot_general(a, b, (((1,), (1,)), ((), ())), preferred_element_type=F32)


def dot_w(a, b):
    return lax.dot_general(a, b, (((0,), (0,)), ((), ())), preferred_element_type=F32)


def inverse_rms(values):
    return lax.rsqrt(jnp.mean(values * values, -1, keepdims=True) + EPSILON)


def rms_back(values, gain_row, d_out):
    r = inverse_rms(values)
    scaled = gain_row * d_out
    d_values = r * scaled - values * (r * r * r * jnp.mean(values * scaled, -1, keepdims=True))
    return d_values, jnp.sum(d_out * values * r, 0, keepdims=True)


def pack(x):
    p, width = x.shape
    full = width // 128 * 128
    last = x[:, full:]
    return jnp.concatenate(
        [x[:, at : at + 128] for at in range(0, full, 128)] + [jnp.concatenate([last[: p // 2], last[p // 2 :]], 1)], 0
    )


def unpack(x, p):
    full = x.shape[0] // p
    last = x[full * p :]
    side = last.shape[1] // 2
    return jnp.concatenate(
        [x[k * p : (k + 1) * p] for k in range(full)] + [jnp.concatenate([last[:, :side], last[:, side:]], 0)], 1
    )


def column(row):
    return jnp.transpose(jnp.broadcast_to(row, (8, row.shape[1])))[:, 0:1]


def call(kernel, name, inputs, outputs, scratch=(), scalars=0, limit=26, flops=0):
    smem = pl.BlockSpec(memory_space=pltpu.SMEM)

    def whole(v):
        dims = len(v.shape)
        return pl.BlockSpec(v.shape, lambda i: (0,) * dims, pipeline_mode=pl.Buffered(1))

    moved = sum(v.size * v.dtype.itemsize for v in list(inputs) + list(outputs))
    return pl.pallas_call(
        kernel,
        grid=(1,),
        in_specs=[smem if k < scalars else whole(v) for k, v in enumerate(inputs)],
        out_specs=[whole(v) for v in outputs],
        out_shape=list(outputs),
        scratch_shapes=list(scratch),
        compiler_params=pltpu.CompilerParams(vmem_limit_bytes=limit * MIB),
        cost_estimate=pl.CostEstimate(flops=flops, bytes_accessed=moved, transcendentals=0),
        name=name,
    )(*inputs)


def shape(dims, dtype):
    return jax.ShapeDtypeStruct(tuple(dims), dtype)


def table_kernel(vocab, wide_ref, out_ref):
    tile = out_ref.shape[0]
    at = pl.program_id(0) * tile
    x = wide_ref[...]
    cols = lax.broadcasted_iota(jnp.int32, x.shape, 1) + at
    out_ref[...] = jnp.transpose(jnp.where(cols < vocab, x, 0.0)).astype(BF)


def low_table(embed_table, padded):
    vocab, width = embed_table.shape
    tile = 512
    return pl.pallas_call(
        functools.partial(table_kernel, vocab),
        grid=(padded // tile,),
        in_specs=[pl.BlockSpec((width, tile), lambda i: (0, i))],
        out_specs=pl.BlockSpec((tile, width), lambda i: (i, 0)),
        out_shape=shape((padded, width), BF),
        compiler_params=pltpu.CompilerParams(vmem_limit_bytes=24 * MIB),
        cost_estimate=pl.CostEstimate(flops=0, bytes_accessed=6 * padded * width, transcendentals=0),
        name="low_table",
    )(embed_table.T)


def spread_kernel(gathered_ref, packed_ref, down_ref):
    groups, _, columns = packed_ref.shape
    width = down_ref.shape[1]
    third = down_ref.shape[0] // (3 * groups)
    for b in range(groups):
        packed_ref[b] = gathered_ref[b, :, :columns]
        for k in range(3):
            at = columns + 64 + k * width
            down_ref[(3 * b + k) * third : (3 * b + k + 1) * third, :] = gathered_ref[b, :third, at : at + width]


def lookup_kernel(ids_ref, table_ref, out_ref):
    rows = out_ref.shape[0]
    total = jnp.zeros(out_ref.shape, F32)
    for at in range(0, table_ref.shape[0], VTILE):
        cols = lax.broadcasted_iota(jnp.int32, (rows, VTILE), 1) + at
        hot = jnp.where(cols == ids_ref[...], 1.0, 0.0).astype(BF)
        total += dot(hot, table_ref[at : at + VTILE, :])
    out_ref[...] = total.astype(BF)


def lookup(ids, table, block):
    count = ids.shape[0]
    width = table.shape[1]
    return pl.pallas_call(
        lookup_kernel,
        grid=(count // block,),
        in_specs=[
            pl.BlockSpec((block, 1), lambda i: (i, 0)),
            pl.BlockSpec(table.shape, lambda i: (0, 0)),
        ],
        out_specs=pl.BlockSpec((block, width), lambda i: (i, 0)),
        out_shape=shape((count, width), BF),
        compiler_params=pltpu.CompilerParams(vmem_limit_bytes=40 * MIB),
        cost_estimate=pl.CostEstimate(
            flops=2 * count * table.size, bytes_accessed=2 * table.size, transcendentals=0
        ),
        name="lookup",
    )(ids.reshape(count, 1), table)


def project(x, gain, packed_ref, c, s, normed_ref, q_ref, kv_ref):
    piece = x.shape[0] // 2
    normed = (x * inverse_rms(x) * gain).astype(BF)
    normed_ref[...] = normed
    q = dot(normed, packed_ref[:, Q_AT : Q_AT + H * HD])
    kv = dot(normed, packed_ref[:, KV_AT : KV_AT + 2 * KVH * HD])
    nothing = jnp.zeros((x.shape[0], HD), F32)
    for h in range(H):
        g, j = divmod(h, GROUP)
        a = q[:, h * HD : h * HD + HALF]
        b = q[:, h * HD + HALF : (h + 1) * HD]
        turned = jnp.concatenate([(a * c - b * s) * 0.125, (a * s + b * c) * 0.125, nothing], 1).astype(BF)
        for p in range(2):
            q_ref[g, p, j * piece : (j + 1) * piece, :] = turned[p * piece : (p + 1) * piece]
    for g in range(KVH):
        a = kv[:, g * HD : g * HD + HALF]
        b = kv[:, g * HD + HALF : (g + 1) * HD]
        v = kv[:, (KVH + g) * HD : (KVH + g + 1) * HD]
        turned = jnp.concatenate([a * c - b * s, a * s + b * c, v], 1).astype(BF)
        kv_ref[0, g] = turned[:piece]
        kv_ref[1, g] = turned[piece:]


def feed(x, o_ref, gain, packed_ref, down_ref, mid_ref, nf_ref, gu_ref, act_ref):
    x_mid = x + dot(o_ref[...], packed_ref[:, OUT_AT : OUT_AT + x.shape[1]])
    mid_ref[...] = x_mid
    nf = (x_mid * inverse_rms(x_mid) * gain).astype(BF)
    nf_ref[...] = nf
    total = x_mid
    for at in range(0, FF, CHUNK):
        gate = dot(nf, packed_ref[:, GU_AT + at : GU_AT + at + CHUNK])
        up = dot(nf, packed_ref[:, GU_AT + FF + at : GU_AT + FF + at + CHUNK])
        gu_ref[:, at : at + CHUNK] = gate
        gu_ref[:, FF + at : FF + at + CHUNK] = up
        act = (gate * lax.logistic(gate) * up).astype(BF)
        act_ref[:, at : at + CHUNK] = act
        total = total + dot(act, down_ref[at : at + CHUNK, :])
    return total


def pre_kernel(x_ref, gain_ref, first_ref, c_ref, s_ref, normed_ref, q_ref, kv_ref):
    project(x_ref[...], gain_ref[0:1, :], first_ref, c_ref[...], s_ref[...], normed_ref, q_ref, kv_ref)


def mid_kernel(
    x_ref, o_ref, gain_ref, first_ref, packed_ref, down_ref, c_ref, s_ref,
    mid_ref, nf_ref, gu_ref, act_ref, next_ref, normed_ref, q_ref, kv_ref,
):
    x = feed(x_ref[...], o_ref, gain_ref[1:2, :], packed_ref, down_ref, mid_ref, nf_ref, gu_ref, act_ref)
    next_ref[...] = x
    project(x, gain_ref[0:1, :], first_ref, c_ref[...], s_ref[...], normed_ref, q_ref, kv_ref)


def post_kernel(
    x_ref, o_ref, gain_ref, packed_ref, down_ref,
    mid_ref, nf_ref, gu_ref, act_ref, next_ref, both_ref,
):
    x = feed(x_ref[...], o_ref, gain_ref[1:2, :], packed_ref, down_ref, mid_ref, nf_ref, gu_ref, act_ref)
    next_ref[...] = x
    final = x * inverse_rms(x) * gain_ref[2:3, :]
    piece = x.shape[0] // 2
    for p in range(2):
        both_ref[p] = pack(final[p * piece : (p + 1) * piece]).astype(BF)


def projected_shapes(rows, width):
    piece = rows // 2
    return [
        shape((rows, width), BF),
        shape((KVH, 2, GROUP * piece, 2 * HD), BF),
        shape((2, KVH, piece, 2 * HD), BF),
    ]


def fed_shapes(rows, width):
    return [
        shape((rows, width), F32),
        shape((rows, width), BF),
        shape((rows, 2 * FF), F32),
        shape((rows, FF), BF),
        shape((rows, width), F32),
    ]


def causal(scores, piece):
    row = lax.broadcasted_iota(jnp.int32, scores.shape, 0) & (piece - 1)
    col = lax.broadcasted_iota(jnp.int32, scores.shape, 1)
    return jnp.where(row >= col, scores, MASKED)


def attend_kernel(n, me_ref, q_ref, *refs):
    kvs, (o_ref, lse_ref, kv_ref) = refs[:n], refs[n:]
    me = me_ref[0]
    piece = kvs[0].shape[2]
    lows = [None] + [(me ^ r) < me for r in range(1, n)]
    for g in range(KVH):
        for r in range(n):
            kv_ref[g, r * piece : (r + 1) * piece, :] = kvs[r][0, g]
            kv_ref[g, (n + r) * piece : (n + r + 1) * piece, :] = kvs[r][1, g]
        wide_kv = kv_ref[g, 0 : n * piece, :]
        q_a = q_ref[g, 0]
        q_b = q_ref[g, 1]
        wide = dot_t(q_b, wide_kv)
        own_a = causal(dot_t(q_a, kvs[0][0, g]), piece)
        own_b = causal(dot_t(q_b, kvs[0][1, g]), piece)
        m_a = jnp.max(own_a, -1, keepdims=True)
        m_b = jnp.maximum(jnp.max(own_b, -1, keepdims=True), jnp.max(wide, -1, keepdims=True))
        tiles = [None]
        for r in range(1, n):
            low = lows[r]
            tile = dot_t(jnp.where(low, q_a, q_b), jnp.where(low, kvs[r][0, g], kvs[r][1, g]))
            top = jnp.max(tile, -1, keepdims=True)
            m_a = jnp.maximum(m_a, top + jnp.where(low, 0.0, -jnp.inf))
            m_b = jnp.maximum(m_b, top + jnp.where(low, -jnp.inf, 0.0))
            tiles.append(tile)
        e = jnp.exp(wide - m_b)
        l_b = jnp.sum(e, -1, keepdims=True)
        o_b = dot(e.astype(BF), wide_kv)
        e = jnp.exp(own_b - m_b)
        l_b += jnp.sum(e, -1, keepdims=True)
        o_b += dot(e.astype(BF), kvs[0][1, g])
        e = jnp.exp(own_a - m_a)
        l_a = jnp.sum(e, -1, keepdims=True)
        o_a = dot(e.astype(BF), kvs[0][0, g])
        for r in range(1, n):
            low = lows[r]
            in_a = jnp.where(low, 1.0, 0.0)
            in_b = 1.0 - in_a
            e = jnp.exp(tiles[r] - (m_a * in_a + m_b * in_b))
            total = jnp.sum(e, -1, keepdims=True)
            o = dot(e.astype(BF), jnp.where(low, kvs[r][0, g], kvs[r][1, g]))
            l_a += total * in_a
            l_b += total * in_b
            o_a += o * in_a
            o_b += o * in_b
        lse_ref[g, 0] = m_a + jnp.log(l_a)
        lse_ref[g, 1] = m_b + jnp.log(l_b)
        out = [(o_a / l_a).astype(BF), (o_b / l_b).astype(BF)]
        for p in range(2):
            for j in range(GROUP):
                h = g * GROUP + j
                o_ref[p * piece : (p + 1) * piece, h * HD : (h + 1) * HD] = out[p][
                    j * piece : (j + 1) * piece, HD:
                ]


def attend(me, queries, kvs):
    n = len(kvs)
    piece = kvs[0].shape[2]
    stacked = GROUP * piece
    return call(
        functools.partial(attend_kernel, n),
        "attend",
        [me, queries] + kvs,
        [shape((2 * piece, H * HD), BF), shape((KVH, 2, stacked, 1), F32), shape((KVH, 2 * n * piece, 2 * HD), BF)],
        scalars=1,
        limit=28,
        flops=2 * 2 * H * HD * piece * piece * (2 * n + 1) * 2,
    )


def attend_back_kernel(n, me_ref, q_ref, do_ref, lse_ref, kv_ref, *refs):
    (dq_ref, keep_ref, send_ref), (sum_ref,) = refs[:3], refs[3:]
    me = me_ref[0]
    piece = kv_ref.shape[1] // (2 * n)
    lows = [None] + [(me ^ r) < me for r in range(1, n)]
    for g in range(KVH):
        wide_kv = kv_ref[g, 0 : n * piece, :]
        kv_a0 = kv_ref[g, 0:piece, :]
        kv_b0 = kv_ref[g, n * piece : (n + 1) * piece, :]
        q_a, q_b = q_ref[g, 0], q_ref[g, 1]
        do_a, do_b = do_ref[g, 0], do_ref[g, 1]
        lse_a, lse_b = lse_ref[g, 0], lse_ref[g, 1]
        p_wide = jnp.exp(dot_t(q_b, wide_kv) - lse_b)
        w_wide = dot_t(do_b, wide_kv)
        d_b = jnp.sum(p_wide * w_wide, -1, keepdims=True)
        p_own_a = jnp.exp(causal(dot_t(q_a, kv_a0), piece) - lse_a)
        w_own_a = dot_t(do_a, kv_a0)
        d_a = jnp.sum(p_own_a * w_own_a, -1, keepdims=True)
        p_own_b = jnp.exp(causal(dot_t(q_b, kv_b0), piece) - lse_b)
        w_own_b = dot_t(do_b, kv_b0)
        d_b += jnp.sum(p_own_b * w_own_b, -1, keepdims=True)
        tiles = [None]
        for r in range(1, n):
            low = lows[r]
            in_a = jnp.where(low, 1.0, 0.0)
            in_b = 1.0 - in_a
            k = jnp.where(low, kv_ref[g, r * piece : (r + 1) * piece, :], kv_ref[g, (n + r) * piece : (n + r + 1) * piece, :])
            p = jnp.exp(dot_t(jnp.where(low, q_a, q_b), k) - (lse_a * in_a + lse_b * in_b))
            w = dot_t(jnp.where(low, do_a, do_b), k)
            total = jnp.sum(p * w, -1, keepdims=True)
            d_a += total * in_a
            d_b += total * in_b
            tiles.append((p, w))

        def both(p, w, inner, q, do, k):
            ds = (p * (w - inner)).astype(BF)
            dq = dot(ds, k)
            dkv = dot_w(ds, q) + dot_w(p.astype(BF), do)
            return dq, dkv

        dq_b, dkv = both(p_wide, w_wide, d_b, q_b, do_b, wide_kv)
        sum_ref[...] = dkv
        dq, dkv_b0 = both(p_own_b, w_own_b, d_b, q_b, do_b, kv_b0)
        dq_b += dq
        dq_a, dkv_a0 = both(p_own_a, w_own_a, d_a, q_a, do_a, kv_a0)
        sum_ref[0:piece, :] += dkv_a0

        def put(half, r, value):
            ref = send_ref if r & 1 else keep_ref
            ref[r // 2, half, g] = value

        put(1, 0, dkv_b0)
        for r in range(1, n):
            low = lows[r]
            in_a = jnp.where(low, 1.0, 0.0)
            in_b = 1.0 - in_a
            p, w = tiles[r]
            k = jnp.where(low, kv_ref[g, r * piece : (r + 1) * piece, :], kv_ref[g, (n + r) * piece : (n + r + 1) * piece, :])
            dq, dkv = both(p, w, d_a * in_a + d_b * in_b, jnp.where(low, q_a, q_b), jnp.where(low, do_a, do_b), k)
            dq_a += dq * in_a
            dq_b += dq * in_b
            sum_ref[r * piece : (r + 1) * piece, :] += dkv * in_a
            put(1, r, dkv * in_b)
        for r in range(n):
            put(0, r, sum_ref[r * piece : (r + 1) * piece, :])
        out = [(dq_a * 0.125).astype(BF), (dq_b * 0.125).astype(BF)]
        for p in range(2):
            for j in range(GROUP):
                h = g * GROUP + j
                dq_ref[p * piece : (p + 1) * piece, h * HD : (h + 1) * HD] = out[p][
                    j * piece : (j + 1) * piece, :HD
                ]


def attend_back(me, queries, d_out, lse, kv_all, n):
    piece = kv_all.shape[1] // (2 * n)
    block = (n // 2, 2, KVH, piece, 2 * HD)
    return call(
        functools.partial(attend_back_kernel, n),
        "attend_back",
        [me, queries, d_out, lse, kv_all],
        [shape((2 * piece, H * HD), BF), shape(block, F32), shape(block, F32)],
        [pltpu.VMEM((n * piece, 2 * HD), F32)],
        scalars=1,
        limit=32,
        flops=5 * 2 * H * HD * piece * piece * (2 * n + 1) * 2,
    )


def feed_back(d_x, gain, packed_ref, down_ref, mid_ref, gu_ref, outs):
    db_ref, dgu_ref, dmid_ref, da_ref, do_ref, gain_ref = outs
    rows, width = d_x.shape
    piece = rows // 2
    d_branch = d_x.astype(BF)
    db_ref[...] = d_branch
    d_nf = jnp.zeros(d_x.shape, F32)
    for at in range(0, FF, CHUNK):
        d_act = dot_t(d_branch, down_ref[at : at + CHUNK, :])
        gate = gu_ref[:, at : at + CHUNK]
        up = gu_ref[:, FF + at : FF + at + CHUNK]
        sig = lax.logistic(gate)
        d_gate = (d_act * up * (sig * (1.0 + gate * (1.0 - sig)))).astype(BF)
        d_up = (d_act * (gate * sig)).astype(BF)
        dgu_ref[:, at : at + CHUNK] = d_gate
        dgu_ref[:, FF + at : FF + at + CHUNK] = d_up
        d_nf += dot_t(d_gate, packed_ref[:, GU_AT + at : GU_AT + at + CHUNK])
        d_nf += dot_t(d_up, packed_ref[:, GU_AT + FF + at : GU_AT + FF + at + CHUNK])
    d_norm, gain_ref[...] = rms_back(mid_ref[...], gain, d_nf)
    d_mid = d_x + d_norm
    dmid_ref[...] = d_mid
    d_attn = d_mid.astype(BF)
    da_ref[...] = d_attn
    d_att = dot_t(d_attn, packed_ref[:, OUT_AT : OUT_AT + width])
    nothing = jnp.zeros((rows, HD), F32)
    for h in range(H):
        g, j = divmod(h, GROUP)
        part = jnp.concatenate([nothing, d_att[:, h * HD : (h + 1) * HD]], 1).astype(BF)
        for p in range(2):
            do_ref[g, p, j * piece : (j + 1) * piece, :] = part[p * piece : (p + 1) * piece]


def fed_back_shapes(rows, width):
    piece = rows // 2
    return [
        shape((rows, width), BF),
        shape((rows, 2 * FF), BF),
        shape((rows, width), F32),
        shape((rows, width), BF),
        shape((KVH, 2, GROUP * piece, 2 * HD), BF),
        shape((1, width), F32),
    ]


def sum_refs(refs, at):
    total = refs[0][at].astype(F32)
    for ref in refs[1:]:
        total += ref[at].astype(F32)
    return total


def project_back(d_mid, dq_ref, parts, gain, packed_ref, x, c, s, outs):
    dq_raw_ref, dkv_raw_ref, gain_ref = outs
    dq = dq_ref[...].astype(F32)
    for h in range(H):
        a = dq[:, h * HD : h * HD + HALF]
        b = dq[:, h * HD + HALF : (h + 1) * HD]
        dq_raw_ref[:, h * HD : (h + 1) * HD] = jnp.concatenate([a * c + b * s, b * c - a * s], 1).astype(BF)
    for g in range(KVH):
        d = jnp.concatenate(
            [sum_refs(parts, (0, g)), sum_refs(parts, (1, g))], 0
        ).astype(BF).astype(F32)
        a = d[:, :HALF]
        b = d[:, HALF:HD]
        dkv_raw_ref[:, g * HD : (g + 1) * HD] = jnp.concatenate([a * c + b * s, b * c - a * s], 1).astype(BF)
        dkv_raw_ref[:, (KVH + g) * HD : (KVH + g + 1) * HD] = d[:, HD:].astype(BF)
    d_normed = dot_t(dq_raw_ref[...], packed_ref[:, Q_AT : Q_AT + H * HD])
    d_normed += dot_t(dkv_raw_ref[...], packed_ref[:, KV_AT : KV_AT + 2 * KVH * HD])
    d_in, gain_ref[...] = rms_back(x, gain, d_normed)
    return d_mid + d_in


def back_first_kernel(terms, x_ref, target_ref, weight_ref, gain_ref, packed_ref, down_ref, mid_ref, gu_ref, *refs):
    parts, outs = refs[:terms], refs[terms:]
    piece = x_ref.shape[0] // 2
    d_final = jnp.concatenate([unpack(sum_refs(parts, 0), piece), unpack(sum_refs(parts, 1), piece)], 0)
    d_final += column(weight_ref[...]) * target_ref[...].astype(F32)
    d_x, outs[0][...] = rms_back(x_ref[...], gain_ref[2:3, :], d_final)
    feed_back(d_x, gain_ref[1:2, :], packed_ref, down_ref, mid_ref, gu_ref, outs[1:])


def back_mid_kernel(
    terms, dmid_ref, dq_ref, x_ref, c_ref, s_ref, gain_ref, first_ref, packed_ref, down_ref, mid_ref, gu_ref, *refs
):
    parts, outs = refs[:terms], refs[terms:]
    d_x = project_back(
        dmid_ref[...], dq_ref, parts, gain_ref[0:1, :], first_ref, x_ref[...], c_ref[...], s_ref[...], outs[:3]
    )
    feed_back(d_x, gain_ref[1:2, :], packed_ref, down_ref, mid_ref, gu_ref, outs[3:])


def back_last_kernel(terms, dmid_ref, dq_ref, x_ref, c_ref, s_ref, gain_ref, first_ref, *refs):
    parts, outs = refs[:terms], refs[terms:]
    d_x = project_back(
        dmid_ref[...], dq_ref, parts, gain_ref[0:1, :], first_ref, x_ref[...], c_ref[...], s_ref[...], outs[:3]
    )
    piece = d_x.shape[0] // 2
    for p in range(2):
        outs[3][p] = pack(d_x[p * piece : (p + 1) * piece]).astype(BF)


def head_kernel(vocab, active_ref, hit_ref, table_ref, *refs):
    pieces, (u_ref, stat_ref), (rows_ref, s_ref) = refs[:-4], refs[-4:-2], refs[-2:]
    n = len(pieces)
    piece = rows_ref.shape[0] // (2 * n)
    rows = 2 * piece
    for k, ref in enumerate(pieces):
        for p in range(2):
            rows_ref[(p * n + k) * piece : (p * n + k + 1) * piece, :] = unpack(ref[p], piece)
    padded = table_ref.shape[0]

    def block(i, _):
        at_row = pl.multiple_of(i * rows, rows)

        @pl.when(active_ref[i] == 0)
        def _():
            u_ref[pl.ds(at_row, rows), :] = jnp.zeros((rows, u_ref.shape[1]), F32)
            stat_ref[i] = jnp.concatenate([jnp.zeros((1, rows), F32), jnp.ones((1, rows), F32), jnp.zeros((1, rows), F32)], 0)

        @pl.when(active_ref[i] != 0)
        def _():
            mine = rows_ref[pl.ds(at_row, rows), :]
            hits = column(hit_ref[i])
            highest = jnp.full((rows, 1), -jnp.inf, F32)
            for at in range(0, padded, VTILE):
                s = dot_t(mine, table_ref[at : at + VTILE, :])
                if at + VTILE > vocab:
                    cols = lax.broadcasted_iota(jnp.int32, (rows, VTILE), 1) + at
                    s = jnp.where(cols < vocab, s, -jnp.inf)
                s_ref[:, at : at + VTILE] = s
                highest = jnp.maximum(highest, jnp.max(s, -1, keepdims=True))
            total = jnp.zeros((rows, 1), F32)
            picked = jnp.zeros((rows, 1), F32)
            u = jnp.zeros((rows, u_ref.shape[1]), F32)
            for at in range(0, padded, VTILE):
                s = s_ref[:, at : at + VTILE]
                e = jnp.exp(s - highest)
                total += jnp.sum(e, -1, keepdims=True)
                hit = lax.broadcasted_iota(jnp.int32, (rows, VTILE), 1) == hits - at
                picked += jnp.sum(jnp.where(hit, s, 0.0), -1, keepdims=True)
                e = jnp.where(hit, 0.0, e).astype(BF)
                u += dot(e, table_ref[at : at + VTILE, :])
            u_ref[pl.ds(at_row, rows), :] = u
            lane = lax.broadcasted_iota(jnp.int32, (rows, 8), 1)
            found = jnp.where(lane == 0, highest, jnp.where(lane == 1, total, picked))
            stat_ref[i] = jnp.transpose(found)[0:3, :]

        return 0

    lax.fori_loop(0, u_ref.shape[0] // rows, block, 0)


def head_forward(active, hits, table, pieces, vocab):
    width = table.shape[1]
    count = pieces[0].size * len(pieces) // width
    rows = count // len(pieces)
    return call(
        functools.partial(head_kernel, vocab),
        "head_forward",
        [active, hits, table] + pieces,
        [shape((count, width), F32), shape((count // rows, 3, rows), F32)],
        [pltpu.VMEM((count, width), BF), pltpu.VMEM((rows, table.shape[0]), F32)],
        scalars=1,
        flops=4 * count * table.size,
    )


def scale_kernel(n, u_ref, scale_ref, *refs):
    stats, (norm_ref, keep_ref, send_ref) = refs[:n], refs[n:]
    blocks = norm_ref.shape[0]
    rows = norm_ref.shape[2]
    piece = rows // 2
    per_half = blocks // 2
    for j in range(blocks):
        half, jj = divmod(j, per_half)
        found = []
        for b in range(n):
            st = stats[b][half * per_half + (jj ^ (b >> 1))]
            if b & 1:
                st = jnp.concatenate([st[:, piece:], st[:, :piece]], 1)
            found.append(st)
        top = found[0][0:1]
        for st in found[1:]:
            top = jnp.maximum(top, st[0:1])
        total = jnp.zeros_like(top)
        for st in found:
            total += st[1:2] * jnp.exp(st[0:1] - top)
        log_norm = top + jnp.log(total)
        picked = jnp.zeros_like(top)
        for st in found:
            picked += st[2:3]
        norm_ref[j] = jnp.concatenate([log_norm, picked], 0)
        factor = column(jnp.exp(found[0][0:1] - log_norm) * scale_ref[j])
        scaled = u_ref[j * rows : (j + 1) * rows, :] * factor
        for k in range(2):
            ref = send_ref if k else keep_ref
            ref[jj, half] = pack(scaled[k * piece : (k + 1) * piece]).astype(ref.dtype)


def head_scale(u, scale, stats):
    n = len(stats)
    count, width = u.shape
    piece = count // (2 * n)
    block = (n // 2, 2, piece * width // 128, 128)
    return call(
        functools.partial(scale_kernel, n),
        "head_scale",
        [u, scale] + stats,
        [shape((scale.shape[0], 2, scale.shape[2]), F32), shape(block, F32), shape(block, BF)],
        flops=2 * u.size,
        limit=28,
    )


def head_grad_kernel(first, step, begin, active_ref, stat_ref, hit_ref, far_table_ref, far_packed_ref, *refs):
    old_ref = None if first else refs[0]
    out_ref, grad_ref, rows_ref, table_ref, packed_ref, sems = refs[-6:]
    sem = sems.at[0]
    turn = pl.program_id(0)
    n = packed_ref.shape[0]
    blocks = stat_ref.shape[1] // step
    piece = rows_ref.shape[0] // (2 * n)
    rows = 2 * piece * step
    vocab = grad_ref.shape[0]
    tile = vocab // 5

    load = pltpu.make_async_copy(far_packed_ref.at[begin + turn], packed_ref, sems.at[1])
    load.start()

    @pl.when(turn == 0)
    def _():
        table_load = pltpu.make_async_copy(far_table_ref, table_ref, sems.at[2])
        table_load.start()
        if first:
            grad_ref[...] = jnp.zeros_like(grad_ref)
        else:
            copy = pltpu.make_async_copy(old_ref, grad_ref, sem)
            copy.start()
            copy.wait()
        table_load.wait()

    load.wait()

    for b in range(n):
        for p in range(2):
            rows_ref[(p * n + b) * piece : (p * n + b + 1) * piece, :] = unpack(packed_ref[b, p], piece)

    def block(i, _):
        wanted = active_ref[turn, step * i]
        for k in range(1, step):
            wanted = wanted + active_ref[turn, step * i + k]

        @pl.when(wanted != 0)
        def _():
            mine = rows_ref[pl.ds(pl.multiple_of(i * rows, rows), rows), :]
            stat = jnp.concatenate([stat_ref[0, step * i + k] for k in range(step)], 1)
            log_norm, scale = stat[0:1], stat[1:2]
            hits = jnp.concatenate([hit_ref[0, step * i + k] for k in range(step)], 1)
            for at in range(0, vocab, tile):
                s = dot_t(table_ref[at : at + tile, :], mine)
                d = jnp.exp(s - log_norm) * scale
                index = lax.broadcasted_iota(jnp.int32, (tile, rows), 0)
                d = jnp.where(index == hits - at, d - scale, d).astype(BF)
                grad_ref[at : at + tile, :] += dot(d, mine)

        return 0

    lax.fori_loop(0, blocks, block, 0)

    @pl.when(turn == pl.num_programs(0) - 1)
    def _():
        back = pltpu.make_async_copy(grad_ref, out_ref, sem)
        back.start()
        back.wait()


def head_grad(active, stats, hits, table, packed, vocab, so_far, begin, end):
    width = table.shape[1]
    count = packed[0].size // width
    first = so_far is None
    part = slice(begin, end)
    inputs = [active[part], stats, hits, table, packed] + ([] if first else [so_far])
    anywhere = pl.BlockSpec(memory_space=pltpu.HBM)

    def sequence(v):
        dims = len(v.shape)
        return pl.BlockSpec((1,) + v.shape[1:], lambda i: (begin + i,) + (0,) * (dims - 1))

    step = 2 if stats.shape[1] % 4 == 0 else 1
    return pl.pallas_call(
        functools.partial(head_grad_kernel, first, step, begin),
        grid=(end - begin,),
        in_specs=[
            pl.BlockSpec(memory_space=pltpu.SMEM),
            sequence(stats),
            sequence(hits),
            pl.BlockSpec(memory_space=pltpu.HBM),
            pl.BlockSpec(memory_space=pltpu.HBM),
        ] + ([] if first else [anywhere]),
        out_specs=anywhere,
        out_shape=shape((vocab, width), F32),
        scratch_shapes=[
            pltpu.VMEM((vocab, width), F32),
            pltpu.VMEM((count, width), BF),
            pltpu.VMEM(table.shape, BF),
            pltpu.VMEM(packed.shape[1:], BF),
            pltpu.SemaphoreType.DMA((3,)),
        ],
        compiler_params=pltpu.CompilerParams(vmem_limit_bytes=40 * MIB),
        cost_estimate=pl.CostEstimate(
            flops=3 * count * table.size * (end - begin), bytes_accessed=8 * vocab * width, transcendentals=0
        ),
        input_output_aliases={} if first else {5: 0},
        name="head_grad",
    )(*inputs)


def add_rows_kernel(bits, count_ref, key_ref, far_packed_ref, grad_ref, far_out_ref, square_ref, out_ref, wide_ref, packed_ref, sems):
    turn = pl.program_id(0)
    n = packed_ref.shape[1]
    slot = turn & 1
    sem = sems.at[2]
    piece = wide_ref.shape[0] // (2 * n)

    @pl.when(turn == 0)
    def _():
        pltpu.make_async_copy(grad_ref, out_ref, sem).start()
        pltpu.make_async_copy(far_packed_ref.at[0], packed_ref.at[0], sems.at[0]).start()

    @pl.when(turn + 1 < pl.num_programs(0))
    def _():
        pltpu.make_async_copy(far_packed_ref.at[turn + 1], packed_ref.at[1 - slot], sems.at[1 - slot]).start()

    pltpu.make_async_copy(far_packed_ref.at[turn], packed_ref.at[slot], sems.at[slot]).wait()

    for b in range(n):
        for p in range(2):
            wide_ref[(p * n + b) * piece : (p * n + b + 1) * piece, :] = unpack(packed_ref[slot, b, p].astype(F32), piece)

    @pl.when(turn == 0)
    def _():
        pltpu.make_async_copy(grad_ref, out_ref, sem).wait()

    def add(i):
        key = key_ref[turn, i]
        row = key >> bits
        at = key & ((1 << bits) - 1)
        out_ref[pl.ds(row, 1), :] += wide_ref[pl.ds(at, 1), :]

    def add_some(i, _):
        for k in range(8):
            add(8 * i + k)
        return 0

    def add_one(i, _):
        add(i)
        return 0

    count = count_ref[turn]
    lax.fori_loop(0, count >> 3, add_some, 0)
    lax.fori_loop((count >> 3) << 3, count, add_one, 0)

    @pl.when(turn == pl.num_programs(0) - 1)
    def _():
        back = pltpu.make_async_copy(out_ref, far_out_ref, sem)
        back.start()
        tile = 80
        width = out_ref.shape[1]

        def squares(i, total):
            v = out_ref[pl.ds(pl.multiple_of(i * tile, 8), tile), :]
            return total + jnp.sum((v * v).reshape(tile // 8, 8, width), 0)

        square_ref[...] = lax.fori_loop(0, out_ref.shape[0] // tile, squares, jnp.zeros((8, width), F32))
        back.wait()


def add_rows(counts, keys, packed, grad, bits):
    vocab, width = grad.shape
    count = packed[0].size // width
    return pl.pallas_call(
        functools.partial(add_rows_kernel, bits),
        grid=(packed.shape[0],),
        in_specs=[
            pl.BlockSpec(memory_space=pltpu.SMEM),
            pl.BlockSpec(memory_space=pltpu.SMEM),
            pl.BlockSpec(memory_space=pltpu.HBM),
            pl.BlockSpec(memory_space=pltpu.HBM),
        ],
        out_specs=[
            pl.BlockSpec(memory_space=pltpu.HBM),
            pl.BlockSpec((8, width), lambda i: (0, 0)),
        ],
        out_shape=[shape(grad.shape, F32), shape((8, width), F32)],
        scratch_shapes=[
            pltpu.VMEM(grad.shape, F32),
            pltpu.VMEM((count, width), F32),
            pltpu.VMEM((2,) + packed.shape[1:], BF),
            pltpu.SemaphoreType.DMA((3,)),
        ],
        compiler_params=pltpu.CompilerParams(vmem_limit_bytes=60 * MIB),
        cost_estimate=pl.CostEstimate(flops=2 * grad.size, bytes_accessed=8 * grad.size, transcendentals=0),
        name="add_rows",
    )(counts, keys, packed, grad)


def adam_update(weight, first, second, grad, decay):
    next_first = BETA_ONE * first + (1.0 - BETA_ONE) * grad
    next_second = BETA_TWO * second + (1.0 - BETA_TWO) * grad * grad
    corrected = next_first / (1.0 - BETA_ONE**STEP_NO)
    scaled = jnp.sqrt(next_second / (1.0 - BETA_TWO**STEP_NO)) + ADAM_EPSILON
    return (weight - RATE * (corrected / scaled + decay * weight), next_first, next_second)


def deal_blocks(value_ref, rows, columns, at_row, me, keep_ref, send_ref):
    for b in range(value_ref.shape[0] // rows):
        r = me ^ b

        def put(ref):
            for k in range(columns // 128):
                ref[r >> 1, at_row + k * rows : at_row + (k + 1) * rows, :] = value_ref[
                    b * rows : (b + 1) * rows, k * 128 : (k + 1) * 128
                ]

        pl.when((r & 1) == 0)(functools.partial(put, keep_ref))
        pl.when((r & 1) == 1)(functools.partial(put, send_ref))
    return at_row + rows * (columns // 128)


def clear_end(at_row, *refs):
    for ref in refs:
        if ref.shape[1] > at_row:
            ref[:, at_row:, :] = jnp.zeros((ref.shape[0], ref.shape[1] - at_row, ref.shape[2]), F32)


def undeal(ref, at_row, rows, columns):
    count = -(-columns // 128)
    parts = [ref[at_row + k * rows : at_row + (k + 1) * rows, :] for k in range(count)]
    return jnp.concatenate(parts, 1)[:, :columns]


def early_grads_kernel(
    n, me_ref, nf0, nf1, dgu0, dgu1, act0, act1, db0, db1, o0, o1, da0, da1, keep_ref, send_ref, wide, tall
):
    me = me_ref[0]
    width = nf0.shape[1]
    padded = tall.shape[1]

    def product(l0, l1, r0, r1):
        return dot_w(l0[...], r0) + dot_w(l1[...], r1)

    at = 0
    for part in (slice(0, FF), slice(FF, 2 * FF)):
        wide[...] = product(nf0, nf1, dgu0[:, part], dgu1[:, part])
        at = deal_blocks(wide, width // n, FF, at, me, keep_ref, send_ref)
    tall[:, width:] = jnp.zeros((FF, padded - width), F32)
    tall[:, :width] = product(act0, act1, db0[...], db1[...])
    at = deal_blocks(tall, FF // n, padded, at, me, keep_ref, send_ref)
    tall[0:width, :width] = product(o0, o1, da0[...], da1[...])
    at = deal_blocks(tall.at[0:width], width // n, padded, at, me, keep_ref, send_ref)
    clear_end(at, keep_ref, send_ref)


def late_grads_kernel(n, me_ref, n0, n1, kv0, kv1, q0, q1, at0, at1, ff0, ff1, fin, keep_ref, send_ref, wide):
    me = me_ref[0]
    width = n0.shape[1]
    kv_width = kv0.shape[1]
    gains = jnp.concatenate(
        [at0[...] + at1[...], ff0[...] + ff1[...], fin[...], jnp.zeros((5, width), F32)], 0
    )
    wide[:, 0:kv_width] = dot_w(n0[...], kv0[...]) + dot_w(n1[...], kv1[...])
    wide[:, kv_width : kv_width + 128] = jnp.concatenate(
        [jnp.transpose(gains), jnp.zeros((width, 120), F32)], 1
    )
    at = deal_blocks(wide, width // n, kv_width + 128, 0, me, keep_ref, send_ref)
    wide[:, width:] = jnp.zeros((width, wide.shape[1] - width), F32)
    wide[:, :width] = dot_w(n0[...], q0[...]) + dot_w(n1[...], q1[...])
    at = deal_blocks(wide, width // n, wide.shape[1], at, me, keep_ref, send_ref)
    clear_end(at, keep_ref, send_ref)


def split_kernel(terms, place_ref, *refs):
    outs, (total_ref,) = refs[terms:-1], refs[-1:]
    total = refs[0][...].astype(F32)
    for ref in refs[1:terms]:
        total += ref[...].astype(F32)
    total_ref[...] = total
    share = outs[0].shape[0]
    for r, ref in enumerate(outs):
        at = pl.multiple_of((place_ref[0] ^ r) * share, 16)
        ref[...] = total_ref[pl.ds(at, share), :].astype(ref.dtype)


def add_kernel(*refs):
    total = refs[0][...].astype(F32)
    for ref in refs[1:-1]:
        total += ref[...].astype(F32)
    refs[-1][...] = total.astype(refs[-1].dtype)


def join_kernel(place_ref, *refs):
    out_ref = refs[-1]
    share = refs[0].shape[0]
    for r, ref in enumerate(refs[:-1]):
        at = pl.multiple_of((place_ref[0] ^ r) * share, 16)
        out_ref[pl.ds(at, share), :] = ref[...].astype(F32)


def sum_over(terms, place, axis, wire, until, finally_until):
    n = lax.axis_size(axis)
    rows, columns = terms[0].shape
    share = rows // n
    parts = call(
        functools.partial(split_kernel, len(terms)), "split", [place] + terms,
        [shape((share, columns), F32)] + [shape((share, columns), wire)] * (n - 1),
        [pltpu.VMEM((rows, columns), F32)], scalars=1, limit=24,
    )
    got = all_after([swap(v, axis, r) for r, v in enumerate(parts) if r], until())
    got = [parts[0]] + got
    (mine,) = call(add_kernel, "add_up", got, [shape((share, columns), F32)], limit=24)
    everything = [mine] + all_after(everyone(mine, axis)[1:], finally_until())
    return call(
        join_kernel, "join", [place] + everything, [shape((rows, columns), F32)], scalars=1, limit=24,
    )[0]


def squares_kernel(*refs):
    out_ref = refs[-1]
    total = jnp.zeros((1, 1), F32)
    for ref in refs[:-1]:
        v = ref[...]
        v = v if ref is refs[0] else v * v
        total += jnp.sum(jnp.sum(v, 0, keepdims=True), 1, keepdims=True)
    out_ref[...] = total


def small_adam_kernel(factor_ref, early_ref, late_ref, *refs):
    states, results = refs[:18], refs[18:]
    factor = factor_ref[0]

    def update(k, grad, part=slice(None), decay=DECAY):
        olds = [states[3 * k + i][:, part] for i in range(3)]
        for i, value in enumerate(adam_update(*olds, grad * factor, decay)):
            results[3 * k + i][:, part] = value

    here, width = states[0].shape
    kv_width = states[3].shape[1]
    at = kv_width // 128 * here
    update(1, undeal(late_ref, 0, here, kv_width))
    update(5, jnp.transpose(late_ref[at : at + here, :])[0:3], decay=0.0)
    update(0, undeal(late_ref, at + here, here, width))
    at = 0
    for part in (slice(0, FF), slice(FF, 2 * FF)):
        update(3, undeal(early_ref, at, here, FF), part)
        at += FF // 128 * here
    down = states[12].shape[0]
    update(4, undeal(early_ref, at, down, width))
    update(2, undeal(early_ref, at + -(-width // 128) * down, here, width))


def table_adam_kernel(factor_ref, grad_ref, *refs):
    vocab, width = grad_ref.shape
    tile = 512
    factor = factor_ref[0]

    def update(grad_tile, w_tile, m_tile, v_tile, new_w, new_m, new_v):
        grad = jnp.transpose(grad_tile[...]) * factor
        new_w[...], new_m[...], new_v[...] = adam_update(w_tile[...], m_tile[...], v_tile[...], grad, DECAY)

    spec = pl.BlockSpec((width, tile), lambda i: (0, i))
    pltpu.emit_pipeline(
        update,
        grid=(pl.cdiv(vocab, tile),),
        in_specs=[pl.BlockSpec((tile, width), lambda i: (i, 0)), spec, spec, spec],
        out_specs=[spec] * 3,
    )(grad_ref, *refs)


def table_adam(factor, grad, weight, first, second):
    vocab, width = grad.shape
    far = pl.BlockSpec(memory_space=pltpu.HBM)
    outs = pl.pallas_call(
        table_adam_kernel,
        in_specs=[pl.BlockSpec(memory_space=pltpu.SMEM)] + [far] * 4,
        out_specs=[far] * 3,
        out_shape=[shape((width, vocab), F32)] * 3,
        compiler_params=pltpu.CompilerParams(vmem_limit_bytes=60 * MIB),
        cost_estimate=pl.CostEstimate(flops=20 * vocab * width, bytes_accessed=28 * vocab * width, transcendentals=0),
        name="table_adam",
    )(factor.reshape(1), grad, weight.T, first.T, second.T)
    return tuple(o.T for o in outs)


def body(*arguments):
    token_ids, response_mask = arguments[0], arguments[1]
    masters, firsts, seconds = arguments[4:11], arguments[11:18], arguments[18:25]
    embed_table, w_query, w_kv, w_out, w_gate_up, w_down, gains = masters
    groups = lax.axis_size("seq")
    batch = lax.axis_size("dp")
    me = lax.axis_index("seq")
    local_len = token_ids.shape[1]
    seq_len = groups * local_len
    piece = local_len // 2
    pieces = 2 * groups
    vocab, width = embed_table.shape
    base = me * vocab
    rows = local_len

    here = w_query.shape[0]
    early_pack = jnp.concatenate(
        [
            w_kv.astype(BF),
            w_query.astype(BF),
            gains.T.astype(BF),
            jnp.zeros((here, EARLY - GAIN_AT - 3), BF),
        ],
        1,
    )
    third = w_down.shape[0] // 3
    down_low = w_down.astype(BF)
    down_side = jnp.concatenate([down_low[k * third : (k + 1) * third] for k in range(3)], 1)
    late_pack = jnp.concatenate(
        [
            w_gate_up.astype(BF),
            w_out.astype(BF),
            jnp.zeros((here, 64), BF),
            jnp.pad(down_side, ((0, here - third), (0, 0))),
        ],
        1,
    )
    first_pack = lax.all_gather(early_pack, "seq", axis=0, tiled=True)
    gathered = lax.all_gather(late_pack, "seq")
    packed_full, down_full = call(
        spread_kernel, "spread", [gathered],
        [shape((groups, here, OUT_AT + width), BF), shape((groups * w_down.shape[0], width), BF)],
    )
    packed_full = packed_full.reshape(groups * here, OUT_AT + width)
    gain_rows = first_pack[:, GAIN_AT : GAIN_AT + 3].T.astype(F32)
    padded = (vocab + VTILE - 1) // VTILE * VTILE
    table = low_table(embed_table, padded)

    meta = jnp.concatenate([token_ids, response_mask], 0)
    ordered = lax.all_gather(meta, "seq", axis=1, tiled=True)
    who = jnp.arange(groups) ^ me

    order = jnp.concatenate([who, pieces - 1 - who])
    pick = order[:, None] == jnp.arange(pieces)[None, :]

    def met(values):
        cut = values.reshape(values.shape[0], 1, pieces, piece)
        chosen = jnp.sum(jnp.where(pick[None, :, :, None], cut, jnp.zeros((), values.dtype)), 2)
        return chosen.reshape(values.shape[0], pieces * piece)

    extra = 16
    ids_row = ordered[0]
    follow = jnp.concatenate([ids_row, jnp.zeros((piece,), jnp.int32)]).reshape(pieces + 1, piece)
    ids_wide = jnp.concatenate([ids_row.reshape(pieces, piece), follow[1:, :extra]], 1)
    evens = jnp.arange(0, groups, 2) ^ me
    odds = evens ^ 1
    wanted = jnp.stack(
        [jnp.stack([evens, pieces - 1 - evens], 1), jnp.stack([odds, pieces - 1 - odds], 1)], 0
    ).reshape(-1)
    ids_wide = jnp.sum(
        jnp.where((wanted[:, None] == jnp.arange(pieces)[None, :])[:, :, None], ids_wide[None], 0), 1
    )
    found = lookup((ids_wide - base).reshape(-1), table, 4 * (piece + extra))
    found_flag = found[:16, :128]
    found = found.reshape(2, groups // 2, 2, piece + extra, width)
    terms = scatter_all(found[0], found[1], "seq", BF, BF)
    found = sum(terms[1:], terms[0])
    hidden = jnp.concatenate([found[0, :piece], found[1, :piece]], 0).astype(F32)
    target_rows = jnp.concatenate([found[0, 1 : piece + 1], found[1, 1 : piece + 1]], 0)

    place = lax.axis_index("dp")
    which = jnp.arange(batch) ^ place
    sequence_spots = which[None, :] == jnp.arange(batch)[:, None]

    def by_sequence(values):
        stacked = jnp.stack(values, 0)
        spots = sequence_spots.reshape((batch, batch) + (1,) * (stacked.ndim - 1))
        return jnp.sum(jnp.where(spots, stacked[None], jnp.zeros((), stacked.dtype)), 1)

    def paired(values):
        cut = values.reshape(values.shape[0], pieces, piece)
        return jnp.concatenate([cut[:, :groups], cut[:, groups:][:, ::-1]], 1)

    all_meta = by_sequence(everyone(after(ordered, found_flag), "dp"))
    ids_all, mask_all = all_meta[:, 0], all_meta[:, 1]
    last = (jnp.arange(seq_len) < seq_len - 1).astype(F32)[None]
    valid_all = mask_all.astype(F32) * last
    counted = jnp.sum(valid_all)
    targets_all = jnp.concatenate([ids_all[:, 1:], jnp.zeros((batch, 1), jnp.int32)], 1)
    pair_valid = paired(valid_all)
    blocks = seq_len // rows
    half = blocks // 2
    own_valid = met(ordered[1:2].astype(F32) * last).reshape(blocks, 1, rows)
    own_target = jnp.concatenate([ordered[0:1, 1:], jnp.zeros((1, 1), jnp.int32)], 1)
    own_target = met(own_target) - base
    own_target = jnp.where((own_target >= 0) & (own_target < vocab), own_target, -1).reshape(blocks, 1, rows)
    own_scale = own_valid / counted
    own_active = (jnp.max(own_valid.reshape(blocks, rows), -1) > 0).astype(jnp.int32)
    pair_targets = (paired(targets_all) - base).reshape(batch, blocks, 1, rows)
    pair_active = (jnp.max(pair_valid.reshape(batch, blocks, rows), -1) > 0).astype(jnp.int32)

    own_pos = jnp.concatenate(
        [order[0] * piece + jnp.arange(piece), order[groups] * piece + jnp.arange(piece)]
    )
    inverse = 10000.0 ** (-jnp.arange(HALF).astype(F32) * 2.0 / HD)
    phases = own_pos.astype(F32)[:, None] * inverse[None, :]
    cosine, sine_wave = after(jnp.cos(phases), pair_valid, pair_targets, pair_active, own_target, own_scale), jnp.sin(phases)
    me_one = me.reshape(1).astype(jnp.int32)

    layer_flops = 2 * rows * width * (2 * H * HD + 2 * KVH * HD + 3 * FF)
    x0 = hidden
    packed_rows = piece * width // 128
    normed0, q0, kv = call(
        pre_kernel, "pre", [x0, gain_rows, first_pack, cosine, sine_wave], projected_shapes(rows, width),
        flops=layer_flops // 4, limit=24,
    )
    o0, lse0, kv0 = attend(me_one, q0, gather_all(kv, "seq"))
    mid0, nf0, gu0, act0, x1, normed1, q1, kv = call(
        mid_kernel, "mid", [x0, o0, gain_rows, first_pack, packed_full, down_full, cosine, sine_wave],
        fed_shapes(rows, width) + projected_shapes(rows, width), flops=layer_flops, limit=32,
    )
    o1, lse1, kv1 = attend(me_one, q1, gather_all(kv, "seq"))
    mid1, nf1, gu1, act1, x2, final = call(
        post_kernel, "post", [x1, o1, gain_rows, packed_full, down_full],
        fed_shapes(rows, width) + [shape((2, packed_rows, 128), BF)], flops=layer_flops, limit=32,
    )
    own_rows = gather_all(final, "seq")
    arrived = own_rows[groups - 1][0, :16]
    rows_all = lax.all_gather(after(final, arrived), ("dp", "seq"))
    rows_all = rows_all.reshape(batch, groups, 2, packed_rows, 128)

    u, stats = head_forward(own_active, own_target, table, own_rows, vocab)
    norms, keep, send = head_scale(u, own_scale, everyone(stats, "seq"))
    terms = scatter_all(keep, send, "seq", BF)

    def mine(row):
        return jnp.concatenate([row[0, :piece], row[half, :piece]])

    at_target = (jnp.exp(mine(norms[:, 1]) - mine(norms[:, 0])) - 1.0) * mine(own_scale[:, 0])
    at_target = at_target.astype(BF).astype(F32).reshape(1, rows)

    outs = call(
        functools.partial(back_first_kernel, len(terms)), "back_first",
        [x2, target_rows, at_target, gain_rows, packed_full, down_full, mid1, gu1] + terms,
        [shape((1, width), F32)] + fed_back_shapes(rows, width), flops=2 * layer_flops, limit=32,
    )
    gain_final, db1, dgu1, dmid1, da1, do1, gain_ffn1 = outs
    met_norms = jnp.swapaxes(after(norms, do1), 0, 1).reshape(2, 2, groups, piece)
    spots = (who[None, :] == jnp.arange(groups)[:, None]).astype(F32)
    piece_norms = jnp.sum(spots[None, None, :, :, None] * met_norms[:, :, None], 3).reshape(2, pieces, piece)
    all_norms = by_sequence(everyone(piece_norms, "dp"))
    loss = jnp.sum(jnp.where(pair_valid > 0, all_norms[:, 0] - all_norms[:, 1], 0.0)) / counted
    pair_stats = jnp.stack(
        [all_norms[:, 0].reshape(batch, blocks, rows), (pair_valid / counted).reshape(batch, blocks, rows)], 2
    )
    dq1, keep, send = attend_back(me_one, q1, do1, lse1, kv1, groups)
    place_one = place.reshape(1).astype(jnp.int32)
    terms = scatter_all(keep, send, "seq", BF, until=lambda: pair_stats)
    outs = call(
        functools.partial(back_mid_kernel, len(terms)), "back_mid",
        [dmid1, dq1, x1, cosine, sine_wave, gain_rows, first_pack, packed_full, down_full, mid0, gu0] + terms,
        [shape((rows, H * HD), BF), shape((rows, 2 * KVH * HD), BF), shape((1, width), F32)] + fed_back_shapes(rows, width),
        flops=2 * layer_flops, limit=32,
    )
    dq_raw1, dkv_raw1, gain_attn1, db0, dgu0, dmid0, da0, do0, gain_ffn0 = outs
    dq0, keep, send = attend_back(me_one, q0, do0, lse0, kv0, groups)
    wide_columns = -(-width // 128) * 128

    def padded_rows(count):
        return -(-count // (16 * batch)) * (16 * batch)

    early_rows = padded_rows((2 * here * FF + w_down.shape[0] * wide_columns + here * wide_columns) // 128)
    early = []

    def start_early_grads():
        early.extend(
            call(
                functools.partial(early_grads_kernel, groups), "early_grads",
                [me_one, nf0, nf1, dgu0, dgu1, act0, act1, after(db0, dq0), db1, o0, o1, da0, da1],
                [shape((groups // 2, early_rows, 128), F32)] * 2,
                [pltpu.VMEM((width, FF), F32), pltpu.VMEM((FF, wide_columns), F32)],
                scalars=1, flops=layer_flops * 2, limit=56,
            )
        )
        return early[1]

    terms = scatter_all(keep, send, "seq", BF, between=start_early_grads)
    outs = call(
        functools.partial(back_last_kernel, len(terms)), "back_last",
        [dmid0, dq0, x0, cosine, sine_wave, gain_rows, first_pack] + terms,
        [shape((rows, H * HD), BF), shape((rows, 2 * KVH * HD), BF), shape((1, width), F32), shape((2, packed_rows, 128), BF)],
        flops=layer_flops // 2, limit=24,
    )
    dq_raw0, dkv_raw0, gain_attn0, d_low = outs
    d_all = lax.all_gather(d_low, ("dp", "seq")).reshape(batch, groups, 2, packed_rows, 128)

    late_rows = padded_rows(here * (w_kv.shape[1] + 128 + wide_columns) // 128)
    late = call(
        functools.partial(late_grads_kernel, groups), "late_grads",
        [me_one, normed0, normed1, dkv_raw0, dkv_raw1, dq_raw0, dq_raw1, gain_attn0, gain_attn1, gain_ffn0, gain_ffn1, gain_final],
        [shape((groups // 2, late_rows, 128), F32)] * 2,
        [pltpu.VMEM((width, wide_columns), F32)],
        scalars=1, flops=layer_flops // 2,
    )
    ends = [1, 2, 3, batch]
    done = []

    def head_step(k):
        while len(done) <= k:
            begin = ends[len(done) - 1] if done else 0
            packed = rows_all if done else after(rows_all, late[1])
            done.append(
                head_grad(
                    pair_active, pair_stats, pair_targets, table, packed, vocab,
                    done[-1] if done else None, begin, ends[len(done)],
                )
            )
        return done[k]

    step = [functools.partial(head_step, k) for k in range(4)]
    early_terms = scatter_all(early[0], early[1], "seq", BF, between=lambda: late[1], until=step[1])
    late_terms = scatter_all(late[0], late[1], "seq", F32, between=step[0], until=step[1])
    bits = (seq_len - 1).bit_length()
    met_ids = paired(ids_all).reshape(batch, seq_len) - base
    inside = (met_ids >= 0) & (met_ids < vocab)
    keys = jnp.where(inside, met_ids * (1 << bits) + jnp.arange(seq_len)[None], 2147483647)
    keys = jnp.sort(keys, -1)
    counts = jnp.sum(inside.astype(jnp.int32), -1)
    early_sum = sum_over(early_terms, place_one, "dp", BF, step[2], step[3])
    grad_table, table_squares = add_rows(counts, keys, d_all, head_step(3), bits)
    late_sum = sum_over(late_terms, place_one, "dp", F32, step[2], lambda: table_squares)

    small = [early_sum, late_sum]
    (squares,) = call(squares_kernel, "squares", [table_squares] + small, [shape((1, 1), F32)], limit=24)
    squares = tree([squares] + [swap(squares, "seq", r) for r in range(2, groups, 2)])
    grad_norm = jnp.sqrt((squares + swap(squares, "seq", 1))[0, 0])
    factor = CLIP / jnp.maximum(grad_norm, CLIP)
    states = [v for i in range(1, 7) for v in (masters[i], firsts[i], seconds[i])]
    news = call(
        small_adam_kernel, "small_adam",
        [factor.reshape(1)] + small + states, [shape(v.shape, F32) for v in states], scalars=1, limit=48,
    )
    table_news = table_adam(factor, grad_table, masters[0], firsts[0], seconds[0])
    results = []
    for k in range(3):
        results += [table_news[k]] + [news[3 * i + k] for i in range(6)]
    return tuple(results) + (loss, grad_norm)


def solution(mesh):
    rows, cols, whole = P("seq", None), P(None, "seq"), P()
    group = (rows,) * 6 + (cols,)
    return jax.shard_map(
        body,
        mesh=mesh,
        in_specs=(P("dp", "seq"), P("dp", "seq"), whole, whole) + group * 3,
        out_specs=group * 3 + (whole, whole),
        check_vma=False,
    )
```
